32 devices in a mesh: dp: 8 (over z, x), heads: 4 (over y, core).
Axes of the slice: x: 2, y: 2, z: 4, core: 2. Of those that a mesh axis runs over, the one named last changes fastest.
Arguments:
- noisy_mel: bfloat16 [16384, 100], P(('dp', 'heads')), may hold values from -6 to 6
- cond_mel: bfloat16 [16384, 100], P(('dp', 'heads')), may hold values from -6 to 6
- text_embed: bfloat16 [16384, 512], P(('dp', 'heads')), may hold values from -6 to 6
- time_embed: bfloat16 [32, 1024], P('dp'), may hold values from -6 to 6
- lengths: int32 [32], P('dp'), may hold values from 256 to 512, as said below
- spans: int32 [32, 2], P(('dp', 'heads')), may hold values from 0 to 512, as said below
- dw_kernel: float32 [7, 512], replicated, may hold values from -2 to 2
- text_bias: float32 [3, 512], replicated, may hold values from -1.8 to 1.8
- text_gain: float32 [512], replicated, may hold values from 0.1 to 1.9
- text_hidden: float32 [3, 1024], replicated, may hold values from -3 to 3
- pw_in: bfloat16 [512, 1024], replicated, may hold values from -0.25 to 0.25
- pw_out: bfloat16 [1024, 512], replicated, may hold values from -0.1875 to 0.1875
- in_proj: bfloat16 [712, 1024], replicated, may hold values from -0.21875 to 0.21875
- frame_bias: float32 [3, 1024], replicated, may hold values from -1.8 to 1.8
- mod_weight: bfloat16 [1024, 6144], P(None, 'heads'), may hold values from -0.1875 to 0.1875
- mod_bias: float32 [6144], P('heads'), may hold values from -4 to 4
- qkv_weight: bfloat16 [3, 1024, 1024], P(None, None, 'heads'), may hold values from -0.1875 to 0.1875
- qkv_bias: bfloat16 [3, 1024], P(None, 'heads'), may hold values from -1.796875 to 1.796875
- out_weight: bfloat16 [1024, 1024], P('heads'), may hold values from -0.75 to 0.75
- ff_in: bfloat16 [1024, 2048], P(None, 'heads'), may hold values from -0.1875 to 0.1875
- ff_in_bias: bfloat16 [2048], P('heads'), may hold values from -1.796875 to 1.796875
- ff_out: bfloat16 [2048, 1024], P('heads'), may hold values from -0.125 to 0.125
- cotangent: bfloat16 [16384, 1024], P(('dp', 'heads')), may hold values from -6 to 6
Outputs:
- output_frames: bfloat16 [16384, 1024], P(('dp', 'heads'))
- text_grad: float32 [16384, 512], P(('dp', 'heads'))
- time_grad: float32 [32, 1024], P('dp')
- dw_kernel_grad: float32 [7, 512], replicated
- text_bias_grad: float32 [3, 512], replicated
- text_gain_grad: float32 [512], replicated
- text_hidden_grad: float32 [3, 1024], replicated
- pw_in_grad: float32 [512, 1024], replicated
- pw_out_grad: float32 [1024, 512], replicated
- in_proj_grad: float32 [712, 1024], replicated
- frame_bias_grad: float32 [3, 1024], replicated
- mod_weight_grad: float32 [1024, 6144], P(None, 'heads')
- mod_bias_grad: float32 [6144], P('heads')
- qkv_weight_grad: float32 [3, 1024, 1024], P(None, None, 'heads')
- qkv_bias_grad: float32 [3, 1024], P(None, 'heads')
- out_weight_grad: float32 [1024, 1024], P('heads')
- ff_in_grad: float32 [1024, 2048], P(None, 'heads')
- ff_in_bias_grad: float32 [2048], P('heads')
- ff_out_grad: float32 [2048, 1024], P('heads')
The draws below stay inside these ranges and needn't reach their ends.
Inputs may be any that keep to these rules, and one draw needn't show every extreme that they name: `lengths`: each utterance has 256 to 512 frames, and among the 4 utterances of every index of dp one has exactly 512. `spans`: start below end, end at most the utterance's length, the span covering 69 to 100 percent of that length.
All inputs are finite; a program needn't handle non-finite values.
Results may differ from the reference program's by a relative error of at most 0.029.
Values may be sent and summed in bfloat16 or wider, within the bound.
No kernel may reach another device: no remote copies, remote signals or barrier semaphores. Data moves between devices by JAX's collectives and lax.ppermute only.
A program may use at most 320 MiB of HBM per device.

```python
import jax
import jax.numpy as jnp
from jax import lax

D = 1024
HEADS = 16
HD = 64
FF = 2048
TD = 512
TFF = 1024
MEL = 100
KS = 7
ROWS = 512
UTTS = 32
FRAMES = 16384
N_HEADS = 4


def utterance_lengths(key):
    base = jax.random.randint(jax.random.fold_in(key, 101), (UTTS,), ROWS // 2, ROWS + 1)
    chosen = jax.random.randint(jax.random.fold_in(key, 102), (UTTS // N_HEADS,), 0, N_HEADS)
    place = jnp.arange(UTTS, dtype=jnp.int32) % N_HEADS
    full = place == jnp.repeat(chosen, N_HEADS, total_repeat_length=UTTS)
    return jnp.where(full, ROWS, base).astype(jnp.int32)


def draw_lengths(key, part):
    counts = utterance_lengths(key)
    return counts


def draw_spans(key, part):
    counts = utterance_lengths(key)
    key = jax.random.fold_in(key, 7)
    share = jax.random.randint(jax.random.fold_in(key, 1), (UTTS,), 70, 101)
    width = counts * share // 100
    start = jax.random.randint(jax.random.fold_in(key, 2), (UTTS,), 0, counts - width + 1)
    return jnp.stack([start, start + width], axis=1).astype(jnp.int32)


def shard_levels(own_key, extent, cuts, least, largest):
    loudness, own = 1.0, jax.random.fold_in(own_key, 6)
    for axis_at, blocks in cuts:
        draws = jnp.exp(jax.random.uniform(jax.random.fold_in(own, axis_at), (blocks,), jnp.float32, least / len(cuts), largest / len(cuts)))
        loudness = loudness * jnp.repeat(draws, extent[axis_at] // blocks).reshape([-1 if axis == axis_at else 1 for axis in range(len(extent))])
    return loudness


def bell_draw(key, shape, scale, reach, split=(), held_as=jnp.bfloat16):
    drawn = scale * jax.random.normal(key, shape, jnp.float32)
    if split:
        drawn = drawn * shard_levels(key, shape, split, -0.22, 0.18)
    return jnp.clip(drawn, -reach, reach).astype(held_as)


def setup_inputs(seed: int = 0) -> dict:
    keys = jax.random.split(jax.random.key(seed), 24)
    return {
        "noisy_mel": bell_draw(keys[0], (FRAMES, MEL), 1.0, 6.0, ((0, 32),)),
        "cond_mel": bell_draw(keys[1], (FRAMES, MEL), 1.0, 6.0, ((0, 32),)),
        "text_embed": bell_draw(keys[2], (FRAMES, TD), 1.0, 6.0, ((0, 32),)),
        "time_embed": bell_draw(keys[3], (UTTS, D), 1.0, 6.0, ((0, 8),)),
        "lengths": draw_lengths(jax.random.fold_in(keys[23], 71), 0),
        "spans": draw_spans(jax.random.fold_in(keys[23], 71), 0),
        "dw_kernel": bell_draw(keys[6], (KS, TD), KS ** -0.5, 2.0, (), jnp.float32),
        "text_bias": bell_draw(keys[7], (3, TD), 0.3, 1.8, (), jnp.float32),
        "text_gain": jnp.clip(1.0 + 0.18 * jax.random.normal(keys[8], (TD,), jnp.float32), 0.1, 1.9),
        "text_hidden": bell_draw(keys[9], (3, TFF), 0.5, 3.0, (), jnp.float32),
        "pw_in": bell_draw(keys[10], (TD, TFF), TD ** -0.5, 0.25),
        "pw_out": bell_draw(keys[11], (TFF, TD), TFF ** -0.5, 0.1875),
        "in_proj": bell_draw(keys[12], (2 * MEL + TD, D), (2 * MEL + TD) ** -0.5, 0.21875),
        "frame_bias": bell_draw(keys[13], (3, D), 0.3, 1.8, (), jnp.float32),
        "mod_weight": bell_draw(keys[14], (D, 6 * D), D ** -0.5, 0.1875, ((1, 4),)),
        "mod_bias": bell_draw(keys[15], (6 * D,), 1.0, 4.0, ((0, 4),), jnp.float32),
        "qkv_weight": bell_draw(keys[16], (3, D, D), D ** -0.5, 0.1875, ((2, 4),)),
        "qkv_bias": bell_draw(keys[17], (3, D), 0.3, 1.796875, ((1, 4),)),
        "out_weight": bell_draw(keys[18], (D, D), HD ** -0.5, 0.75, ((0, 4),)),
        "ff_in": bell_draw(keys[19], (D, FF), D ** -0.5, 0.1875, ((1, 4),)),
        "ff_in_bias": bell_draw(keys[20], (FF,), 0.3, 1.796875, ((0, 4),)),
        "ff_out": bell_draw(keys[21], (FF, D), FF ** -0.5, 0.125, ((0, 4),)),
        "cotangent": bell_draw(keys[22], (FRAMES, D), 1.0, 6.0, ((0, 32),)),
    }


@jax.custom_vjp
def low(v):
    return lax.optimization_barrier(v.astype(jnp.bfloat16)).astype(jnp.float32)

@jax.custom_vjp
def low_back(v):
    return v

def low_keep(v):
    return (low(v), None)

def low_pass(kept, grad):
    return (grad,)

def back_keep(v):
    return (v, None)

def back_low(kept, grad):
    return (low(grad),)
low.defvjp(low_keep, low_pass)
low_back.defvjp(back_keep, back_low)

def matmul(left, right):
    return jnp.dot(left, right, precision=lax.Precision.HIGHEST)

def layer_norm(values, epsilon):
    mean = lax.optimization_barrier(jnp.mean(values, axis=-1, keepdims=True))
    centred = values - mean
    spread = lax.optimization_barrier(jnp.mean(centred * centred, axis=-1, keepdims=True))
    return centred * lax.rsqrt(spread + epsilon)

def norm_mod(values, scale, shift):
    return layer_norm(values, 1e-06) * (1.0 + scale) + shift

def depthwise(rows_in, kernel):
    width = kernel.shape[0]
    margin = width // 2
    count = rows_in.shape[-2]
    widths = [(0, 0)] * (rows_in.ndim - 2) + [(margin, margin), (0, 0)]
    padded = jnp.pad(rows_in, widths)
    result = padded[..., 0:count, :] * kernel[0]
    for offset in range(1, width):
        result = result + padded[..., offset:offset + count, :] * kernel[offset]
    return result

def text_front(text_rows, kernel, conv_bias, gain, norm_bias):
    return layer_norm(depthwise(text_rows, kernel) + conv_bias, 1e-06) * gain + norm_bias

def grn_part(pre_act, gamma, beta):
    hidden = jax.nn.gelu(pre_act, approximate=False)
    energy = jnp.sqrt(lax.optimization_barrier(jnp.sum(hidden * hidden, axis=-2, keepdims=True)))
    ratio = energy / (lax.optimization_barrier(jnp.mean(energy, axis=-1, keepdims=True)) + 1e-06)
    return gamma * (hidden * ratio) + beta + hidden

def rope_tables(rows, width):
    half = width // 2
    inverse = 10000.0 ** (-2.0 * jnp.arange(half, dtype=jnp.float32) / width)
    angle = jnp.arange(rows, dtype=jnp.float32)[:, None] * inverse[None, :]
    return (jnp.cos(angle), jnp.sin(angle))

def rotate(values, cosine, sine):
    pairs = values.reshape(values.shape[:-1] + (values.shape[-1] // 2, 2))
    first = pairs[..., 0]
    second = pairs[..., 1]
    turned = jnp.stack([first * cosine - second * sine, second * cosine + first * sine], axis=-1)
    return turned.reshape(values.shape)

def reference(noisy_mel, cond_mel, text_embed, time_embed, lengths, spans, dw_kernel, text_bias, text_gain, text_hidden, pw_in, pw_out, in_proj, frame_bias, mod_weight, mod_bias, qkv_weight, qkv_bias, out_weight, ff_in, ff_in_bias, ff_out, cotangent):
    position = jnp.arange(ROWS, dtype=jnp.int32)
    inside = (position[None, :] >= spans[:, 0:1]) & (position[None, :] < spans[:, 1:2])
    keep = jnp.where(inside, 0.0, 1.0).astype(jnp.float32)[:, :, None]
    valid = (position[None, :] < lengths[:, None]).astype(jnp.float32)[:, :, None]
    noisy = noisy_mel.astype(jnp.float32).reshape(UTTS, ROWS, MEL)
    cond = cond_mel.astype(jnp.float32).reshape(UTTS, ROWS, MEL) * keep
    cosine, sine = rope_tables(ROWS, HD)
    cosine = cosine[:, None, :]
    sine = sine[:, None, :]
    scale = HD ** (-0.5)

    def attend_one(args):
        queries, key_rows, value_rows, count = args
        scores = low_back(jnp.einsum('qhe,khe->hqk', queries, key_rows, precision=lax.Precision.HIGHEST) * scale)
        live = jnp.arange(ROWS, dtype=jnp.int32) < count
        scores = jnp.where(live[None, None, :], scores, -1e+30)
        top = lax.optimization_barrier(jnp.max(scores, axis=-1, keepdims=True))
        expo = jnp.exp(scores - top)
        probs = expo / lax.optimization_barrier(jnp.sum(expo, axis=-1, keepdims=True))
        return jnp.einsum('hqk,khe->qhe', low(probs), value_rows, precision=lax.Precision.HIGHEST)

    def forward(params):
        text_rows, time_rows, kernel, bias_text, gain_text, hidden_text, weight_pin, weight_pout, weight_in, bias_frames, weight_mod, bias_mod, weight_qkv, bias_qkv, weight_out, weight_up, bias_up, weight_down = params
        normed_text = text_front(text_rows, kernel, bias_text[0], gain_text, bias_text[1])
        pre_act = low_back(matmul(low(normed_text), weight_pin)) + hidden_text[0]
        mixed = grn_part(pre_act, hidden_text[1], hidden_text[2])
        refined = text_rows + low_back(matmul(low(mixed), weight_pout)) + bias_text[2]
        frames_in = jnp.concatenate([noisy, cond, low(refined)], axis=-1)
        state_zero = low_back(matmul(frames_in, weight_in)) + bias_frames[0]
        modulation = low_back(low(matmul(low(jax.nn.silu(time_rows)), weight_mod) + bias_mod))[:, None, :]
        blocks = [modulation[..., part * D:(part + 1) * D] for part in range(6)]
        attn_in = low(norm_mod(state_zero, blocks[1], blocks[0]))
        linear = [low_back(matmul(attn_in, weight_qkv[which])) + bias_qkv[which] for which in range(3)]
        shape_heads = (UTTS, ROWS, HEADS, HD)
        queries = low(rotate(linear[0].reshape(shape_heads), cosine, sine))
        key_rows = low(rotate(linear[1].reshape(shape_heads), cosine, sine))
        value_rows = low(linear[2].reshape(shape_heads))
        attended = lax.map(jax.checkpoint(attend_one), (queries, key_rows, value_rows, lengths))
        attended = low_back(low(attended.reshape(UTTS, ROWS, D) * valid))
        state_one = state_zero + blocks[2] * (low_back(matmul(attended, weight_out)) + bias_frames[1])
        ffn_in = low(norm_mod(state_one, blocks[4], blocks[3]))
        hidden_ffn = low(jax.nn.gelu(low_back(matmul(ffn_in, weight_up)) + bias_up, approximate=True))
        return state_one + blocks[5] * (low_back(matmul(hidden_ffn, weight_down)) + bias_frames[2])
    params = (text_embed.astype(jnp.float32).reshape(UTTS, ROWS, TD), time_embed.astype(jnp.float32), dw_kernel.astype(jnp.float32), text_bias.astype(jnp.float32), text_gain.astype(jnp.float32), text_hidden.astype(jnp.float32), pw_in.astype(jnp.float32), pw_out.astype(jnp.float32), in_proj.astype(jnp.float32), frame_bias.astype(jnp.float32), mod_weight.astype(jnp.float32), mod_bias.astype(jnp.float32), qkv_weight.astype(jnp.float32), qkv_bias.astype(jnp.float32), out_weight.astype(jnp.float32), ff_in.astype(jnp.float32), ff_in_bias.astype(jnp.float32), ff_out.astype(jnp.float32))
    output, pull = jax.vjp(forward, params)
    grads, = pull(cotangent.astype(jnp.float32).reshape(UTTS, ROWS, D))
    return (output.reshape(FRAMES, D).astype(jnp.bfloat16), grads[0].reshape(FRAMES, TD), grads[1], grads[2], grads[3], grads[4], grads[5], grads[6], grads[7], grads[8], grads[9], grads[10], grads[11], grads[12], grads[13], grads[14], grads[15], grads[16], grads[17])
```

```python
from functools import partial

import jax
import jax.numpy as jnp
from jax import lax
from jax.experimental import pallas as pl
from jax.experimental.pallas import tpu as pltpu
from jax.sharding import PartitionSpec as P

HD = 64


def inner_rows(left, right):
    return lax.dot_general(
        left, right, (((0,), (0,)), ((), ())), preferred_element_type=jnp.float32
    )


def inner_cols(left, right):
    return lax.dot_general(
        left, right, (((1,), (1,)), ((), ())), preferred_element_type=jnp.float32
    )


F32 = jnp.float32
BF16 = jnp.bfloat16
CHUNK = 64
SPAN = 256
VMEM = 60 * 1024 * 1024


def mm(left, right):
    return jnp.dot(left, right, preferred_element_type=F32)


def fold(values):
    return jnp.sum(values.reshape(values.shape[0] // 8, 8, values.shape[1]), axis=0)


def norm_parts(values):
    mean = jnp.mean(values, axis=-1, keepdims=True)
    centred = values - mean
    root = lax.rsqrt(jnp.mean(centred * centred, axis=-1, keepdims=True) + 1e-06)
    return centred * root, root


def norm_pull(grad, scale, xhat, root):
    entry = grad * (1.0 + scale)
    mean = jnp.mean(entry, axis=-1, keepdims=True)
    along = jnp.mean(entry * xhat, axis=-1, keepdims=True)
    return root * (entry - mean - xhat * along)


def swap_pairs(block):
    width = block.shape[1]
    lane = lax.broadcasted_iota(jnp.int32, block.shape, 1)
    if width % 128 == 0:
        after = pltpu.roll(block, width - 1, 1)
        before = pltpu.roll(block, 1, 1)
    else:
        after = jnp.concatenate([block[:, 1:], block[:, :1]], axis=1)
        before = jnp.concatenate([block[:, width - 1 :], block[:, : width - 1]], axis=1)
    return jnp.where(lane % 2 == 0, after, before)


def head_lanes(block, head):
    if block.shape[1] == HD:
        return block
    lane = lax.broadcasted_iota(jnp.int32, block.shape, 1)
    return jnp.where((lane >= head * HD) & (lane < (head + 1) * HD), block, jnp.zeros_like(block))


def slot_copies(pieces, target, sems, at, axis, half):
    if len(pieces) == 1:
        return [pltpu.make_async_copy(pieces[0], target.at[at], sems.at[at, 0])]
    copies = []
    for which, piece in enumerate(pieces):
        size = piece.shape[axis]
        start = pl.multiple_of((half if which == 0 else 1 - half) * size, size)
        index = (at,) + (slice(None),) * axis + (pl.ds(start, size),)
        copies.append(pltpu.make_async_copy(piece, target.at[index], sems.at[at, which]))
    return copies


def start_all(step, copies):
    @pl.when(step == 0)
    def _():
        for members in copies:
            for copy in members:
                copy.start()


def wait_own(step, copies):
    for at, members in enumerate(copies):

        @pl.when(step == at)
        def _(members=members):
            for copy in members:
                copy.wait()


def send_own(step, results):
    for at, members in enumerate(results):

        @pl.when(step == at)
        def _(members=members):
            for copy in members:
                copy.start()


def wait_all(step, results):
    @pl.when(step == len(results) - 1)
    def _():
        for members in results:
            for copy in members:
                copy.wait()


def attention_forward(pieces, first, last, *refs):
    parts = len(pieces)
    refs = list(refs)

    def take(count=1):
        taken = [refs.pop(0) for _ in range(count)]
        return taken[0] if count == 1 else taken

    count_ref, half_ref, state_ref, mod_ref, bias_ref, frame_ref, cosine_ref, sine_ref = take(8)
    weights = [[take() for _ in range(number)] for number in pieces]
    outs = [[take() for _ in range(number)] for number in pieces]
    if not first:
        normed_ref, before_ref = take(2)
    query_ref, key_ref, value_ref, attended_ref, log_ref = take(5)
    if first:
        normed_ref = take()
    if last:
        branch_ref, one_ref, ffn_ref = take(3)
    else:
        total_ref = take()
    weight_ref, out_ref, weight_sem, out_sem = take(4)
    if last:
        total_ref = take()
    step = pl.program_id(0)
    rows = state_ref.shape[0]
    width = weight_ref.shape[3]
    block = cosine_ref.shape[1]
    count = count_ref[0]
    half = half_ref[0]
    copies = [
        slot_copies(weights[at], weight_ref, weight_sem, at, 1, half)
        + slot_copies(outs[at], out_ref, out_sem, at, 0, half)
        for at in range(parts)
    ]
    start_all(step, copies)

    @pl.when(step == 0)
    def _():
        if first:

            def chunk(at, carry):
                here = pl.ds(at * CHUNK, CHUNK)
                xhat, _ = norm_parts(state_ref[here, :])
                normed_ref[here, :] = (xhat * (1.0 + mod_ref[1:2, :]) + mod_ref[0:1, :]).astype(
                    BF16
                )
                return carry

            lax.fori_loop(0, rows // CHUNK, chunk, 0)
            total_ref[...] = jnp.zeros_like(total_ref)
        else:
            total_ref[...] = before_ref[...]

    wait_own(step, copies)
    normed = normed_ref[...]
    cosine = cosine_ref[...]
    sine = sine_ref[...]
    logs = jnp.zeros((rows, 128), F32)
    lane = lax.broadcasted_iota(jnp.int32, (rows, 128), 1)
    query_lin = mm(normed, weight_ref[step, 0]) + bias_ref[0, 0:1, :]
    key_lin = mm(normed, weight_ref[step, 1]) + bias_ref[0, 1:2, :]
    value_ref[0] = (mm(normed, weight_ref[step, 2]) + bias_ref[0, 2:3, :]).astype(BF16)
    for at in range(width // block):
        cut = slice(at * block, (at + 1) * block)
        piece = query_lin[:, cut]
        turned = piece * cosine + swap_pairs(piece) * sine
        query_ref[0, :, cut] = (turned * HD**-0.5).astype(BF16)
        piece = key_lin[:, cut]
        key_ref[0, :, cut] = (piece * cosine + swap_pairs(piece) * sine).astype(BF16)
    live = lax.broadcasted_iota(jnp.int32, (1, rows), 1) < count
    for at in range(width // block):
        cut = slice(at * block, (at + 1) * block)
        keys = key_ref[0, :, cut]
        values = value_ref[0, :, cut]
        results = [None] * (rows // SPAN)
        pieces = [[] for _ in range(rows // SPAN)]
        for head in range(block // HD):
            own_values = head_lanes(values, head)
            for part in range(rows // SPAN):
                queries = head_lanes(query_ref[0, part * SPAN : (part + 1) * SPAN, cut], head)
                scores = jnp.where(live, inner_cols(queries, keys), -1e30)
                top = jnp.max(scores, axis=1, keepdims=True)
                expo = jnp.exp(scores - top)
                total = jnp.sum(expo, axis=1, keepdims=True)
                weights = (expo * (1.0 / total)).astype(BF16)
                result = mm(weights, own_values)
                results[part] = result if head == 0 else results[part] + result
                pieces[part].append(top + jnp.log(total))
        for head in range(block // HD):
            column = jnp.concatenate([pieces[part][head] for part in range(rows // SPAN)], axis=0)
            logs = jnp.where(lane == at * (block // HD) + head, column, logs)
        for part in range(rows // SPAN):
            place = part * SPAN + lax.broadcasted_iota(jnp.int32, (SPAN, block), 0)
            attended_ref[0, part * SPAN : (part + 1) * SPAN, cut] = jnp.where(
                place < count, results[part], 0.0
            ).astype(BF16)
    log_ref[0] = jnp.transpose(logs)[0:8, :]
    total_ref[...] += mm(attended_ref[0], out_ref[step])

    if last:

        @pl.when(step == parts - 1)
        def _():
            def chunk(at, carry):
                here = pl.ds(at * CHUNK, CHUNK)
                branch = total_ref[here, :] + frame_ref[1:2, :]
                branch_ref[here, :] = branch
                state_one = state_ref[here, :] + mod_ref[2:3, :] * branch
                one_ref[here, :] = state_one
                xhat, _ = norm_parts(state_one)
                ffn_ref[here, :] = (xhat * (1.0 + mod_ref[4:5, :]) + mod_ref[3:4, :]).astype(BF16)
                return carry

            lax.fori_loop(0, rows // CHUNK, chunk, 0)


def lay(target_ref, at, start, value):
    model, width = value.shape
    for block in range(model // width):
        target_ref[at, start : start + width, block * width : (block + 1) * width] = value[
            block * width : (block + 1) * width, :
        ]


def feed_forward(pieces, first, last, *refs):
    parts = len(pieces)
    refs = list(refs)

    def take(count=1):
        taken = [refs.pop(0) for _ in range(count)]
        return taken[0] if count == 1 else taken

    half_ref, cotangent_ref, one_ref, branch_ref, source_ref, mod_ref, bias_ref, frame_ref = take(8)
    ups = [[take() for _ in range(number)] for number in pieces]
    downs = [[take() for _ in range(number)] for number in pieces]
    if not first:
        grad_ref, total_in_ref, back_in_ref = take(3)
    grad_bias_ref, sums_ref = take(2)
    grads = [take() for _ in range(parts)]
    if first:
        grad_ref = take()
    if last:
        output_ref, grad_one_ref, grad_attn_ref = take(3)
    else:
        total_ref, back_ref = take(2)
    up_ref, down_ref, up_sem, down_sem = take(4)
    grads_ref, grads_sem = take(2)
    turned_ref, hidden_ref, pre_ref = take(3)
    if last:
        total_ref, back_ref = take(2)
    step = pl.program_id(0)
    rows, wide = one_ref.shape
    inner = 0.7978845608028654
    cubic = 0.044715
    half = half_ref[0]
    copies = [
        slot_copies(ups[at], up_ref, up_sem, at, 0, half)
        + slot_copies(downs[at], down_ref, down_sem, at, 0, half)
        for at in range(parts)
    ]
    results = [
        (pltpu.make_async_copy(grads_ref.at[at], grads[at], grads_sem.at[at]),)
        for at in range(parts)
    ]
    start_all(step, copies)

    @pl.when(step == 0)
    def _():
        if first:

            def chunk(at, carry):
                here = pl.ds(at * CHUNK, CHUNK)
                grad = cotangent_ref[here, :].astype(F32) * mod_ref[5:6, :]
                grad_ref[here, :] = grad.astype(BF16)
                return carry + fold(grad)

            lanes = lax.fori_loop(0, rows // CHUNK, chunk, jnp.zeros((8, wide), F32))
            sums_ref[0:1, :] = jnp.sum(lanes, axis=0, keepdims=True)
            total_ref[...] = jnp.zeros_like(total_ref)
            back_ref[...] = jnp.zeros_like(back_ref)
        else:
            total_ref[...] = total_in_ref[...]
            back_ref[...] = back_in_ref[...]
        turned_ref[...] = jnp.transpose(source_ref[...])

    wait_own(step, copies)
    up = up_ref[step]
    down = down_ref[step]
    lanes = jnp.zeros((8, up.shape[1]), F32)
    for part in range(rows // SPAN):
        here = slice(part * SPAN, (part + 1) * SPAN)
        pre = mm(source_ref[here, :], up) + bias_ref[0]
        grad_hidden = inner_cols(grad_ref[here, :], down)
        square = pre * pre
        bend = jnp.tanh(pre * (inner + inner * cubic * square))
        half = 0.5 * (1.0 + bend)
        hidden = (pre * half).astype(BF16)
        slope = half + 0.5 * pre * (1.0 - bend * bend) * (inner + 3.0 * inner * cubic * square)
        grad_pre = grad_hidden * slope
        lanes = lanes + fold(grad_pre)
        grad_pre = grad_pre.astype(BF16)
        hidden_ref[here, :] = hidden
        pre_ref[here, :] = grad_pre
        total_ref[here, :] += mm(hidden, down)
        back_ref[here, :] += inner_cols(grad_pre, up)
    grad_bias_ref[0] = jnp.sum(lanes, axis=0, keepdims=True)
    width = up_ref.shape[2]
    grads_ref[step, width:, :] = inner_rows(hidden_ref[...], grad_ref[...]).astype(BF16)
    lay(grads_ref, step, 0, mm(turned_ref[...], pre_ref[...]).astype(BF16))
    send_own(step, results)

    if last:

        @pl.when(step == parts - 1)
        def _():
            def chunk(at, carry):
                gate_ffn, scale_ffn, shift_ffn, bias_attn, gate_attn = carry
                here = pl.ds(at * CHUNK, CHUNK)
                branch = total_ref[here, :] + frame_ref[2:3, :]
                state_one = one_ref[here, :]
                output_ref[here, :] = (state_one + mod_ref[5:6, :] * branch).astype(BF16)
                cotangent = cotangent_ref[here, :].astype(F32)
                xhat, root = norm_parts(state_one)
                back = back_ref[here, :]
                grad_one = cotangent + norm_pull(back, mod_ref[4:5, :], xhat, root)
                grad_one_ref[here, :] = grad_one
                grad_attn = grad_one * mod_ref[2:3, :]
                grad_attn_ref[here, :] = grad_attn.astype(BF16)
                return (
                    gate_ffn + fold(cotangent * branch),
                    scale_ffn + fold(back * xhat),
                    shift_ffn + fold(back),
                    bias_attn + fold(grad_attn),
                    gate_attn + fold(grad_one * branch_ref[here, :]),
                )

            start = tuple(jnp.zeros((8, wide), F32) for _ in range(5))
            lanes = lax.fori_loop(0, rows // CHUNK, chunk, start)
            for at, member in enumerate(lanes):
                sums_ref[at + 1 : at + 2, :] = jnp.sum(member, axis=0, keepdims=True)

    wait_all(step, results)


def attention_backward(pieces, first, last, *refs):
    parts = len(pieces)
    refs = list(refs)

    def take(count=1):
        taken = [refs.pop(0) for _ in range(count)]
        return taken[0] if count == 1 else taken

    count_ref, half_ref, grad_attn_ref, normed_ref, mod_ref, cosine_ref, sine_ref = take(7)
    query_ref, key_ref, value_ref, attended_ref, log_ref = take(5)
    weights = [[take() for _ in range(number)] for number in pieces]
    outs = [[take() for _ in range(number)] for number in pieces]
    if not first:
        before_ref = take()
    if last:
        state_ref, grad_one_ref = take(2)
    grad_bias_ref = take()
    grads = [take() for _ in range(parts)]
    if last:
        grad_zero_ref, sums_ref = take(2)
    else:
        back_ref = take()
    weight_ref, out_ref, weight_sem, out_sem = take(4)
    grads_ref, grads_sem = take(2)
    turned_ref, item_ref = take(2)
    if last:
        back_ref = take()
    step = pl.program_id(0)
    rows, wide = normed_ref.shape
    width = weight_ref.shape[3]
    block = cosine_ref.shape[1]
    count = count_ref[0]
    half = half_ref[0]
    copies = [
        slot_copies(weights[at], weight_ref, weight_sem, at, 1, half)
        + slot_copies(outs[at], out_ref, out_sem, at, 0, half)
        for at in range(parts)
    ]
    results = [
        (pltpu.make_async_copy(grads_ref.at[at], grads[at], grads_sem.at[at]),)
        for at in range(parts)
    ]
    start_all(step, copies)

    @pl.when(step == 0)
    def _():
        turned_ref[...] = jnp.transpose(normed_ref[...])
        back_ref[...] = jnp.zeros_like(back_ref) if first else before_ref[...]

    wait_own(step, copies)
    grad_attn = grad_attn_ref[...]
    place = lax.broadcasted_iota(jnp.int32, (rows, width), 0)
    item_ref[...] = jnp.where(place < count, inner_cols(grad_attn, out_ref[step]), 0.0).astype(BF16)
    grads_ref[step, 3 * width :, :] = inner_rows(attended_ref[0], grad_attn).astype(BF16)
    cosine = cosine_ref[...]
    sine = sine_ref[...]
    live = lax.broadcasted_iota(jnp.int32, (rows, 1), 0) < count
    linear = [[], [], []]
    for at in range(width // block):
        cut = slice(at * block, (at + 1) * block)
        keys = key_ref[0, :, cut]
        values = value_ref[0, :, cut]
        keys_turned = jnp.transpose(keys)
        grad_keys = jnp.zeros((rows, block), F32)
        grad_values = jnp.zeros((rows, block), F32)
        grad_queries = [[] for _ in range(rows // SPAN)]
        for head in range(block // HD):
            index = at * (block // HD) + head
            for part in range(rows // SPAN):
                here = slice(part * SPAN, (part + 1) * SPAN)
                queries = head_lanes(query_ref[0, here, cut], head)
                items = head_lanes(item_ref[here, cut], head)
                scores = jnp.where(live, inner_cols(keys, queries), -1e30)
                weights = jnp.exp(scores - log_ref[0, index : index + 1, here])
                grad_weights = inner_cols(values, items)
                along = jnp.sum(grad_weights * weights, axis=0, keepdims=True)
                grad_scores = (weights * (grad_weights - along)).astype(BF16)
                grad_values = grad_values + mm(weights.astype(BF16), items)
                grad_keys = grad_keys + mm(grad_scores, queries)
                grad_queries[part].append(
                    mm(keys_turned[head * HD : (head + 1) * HD, :], grad_scores)
                )
        grad_query = jnp.concatenate(
            [jnp.concatenate(grad_queries[part], axis=0) for part in range(rows // SPAN)], axis=1
        )
        grad_query = jnp.transpose(grad_query) * HD**-0.5
        for which, member in enumerate((grad_query, grad_keys)):
            linear[which].append(member * cosine - swap_pairs(member) * sine)
        linear[2].append(grad_values)
    for which in range(3):
        member = jnp.concatenate(linear[which], axis=1) if width > block else linear[which][0]
        grad_bias_ref[0, which : which + 1, :] = jnp.sum(member, axis=0, keepdims=True)
        member = member.astype(BF16)
        lay(grads_ref, step, which * width, mm(turned_ref[...], member).astype(BF16))
        back_ref[...] += inner_cols(member, weight_ref[step, which])

    send_own(step, results)

    if last:

        @pl.when(step == parts - 1)
        def _():
            def chunk(at, carry):
                scale_attn, shift_attn, bias_in = carry
                here = pl.ds(at * CHUNK, CHUNK)
                xhat, root = norm_parts(state_ref[here, :])
                back = back_ref[here, :]
                grad_zero = grad_one_ref[here, :] + norm_pull(back, mod_ref[1:2, :], xhat, root)
                grad_zero_ref[here, :] = grad_zero.astype(BF16)
                return (
                    scale_attn + fold(back * xhat),
                    shift_attn + fold(back),
                    bias_in + fold(grad_zero),
                )

            start = tuple(jnp.zeros((8, wide), F32) for _ in range(3))
            lanes = lax.fori_loop(0, rows // CHUNK, chunk, start)
            for at, member in enumerate(lanes):
                sums_ref[at : at + 1, :] = jnp.sum(member, axis=0, keepdims=True)

    wait_all(step, results)


def total_of(refs):
    total = refs[0][...].astype(F32)
    for ref in refs[1:]:
        total = total + ref[...].astype(F32)
    return total.astype(BF16)


def sum_kernel(count, *refs):
    refs[count][...] = total_of(refs[:count])


def split_kernel(count, *refs):
    upper_kept = refs[0][0] == 1
    lower = total_of(refs[1 : 1 + count])
    upper = total_of(refs[1 + count : 1 + 2 * count])
    keep_ref, send_ref = refs[1 + 2 * count :]
    keep_ref[...] = jnp.where(upper_kept, upper, lower)
    send_ref[...] = jnp.where(upper_kept, lower, upper)


def bring(starts_ref, pieces, stack_ref, sems):
    size = pieces[0].shape[0]
    copies = []
    for at, piece in enumerate(pieces):
        start = pl.multiple_of(starts_ref[at], 16)
        copies.append(
            pltpu.make_async_copy(piece, stack_ref.at[pl.ds(start, size), :], sems.at[at])
        )
    for copy in copies:
        copy.start()
    for copy in copies:
        copy.wait()


def unlay(target, stack_ref, start, width):
    for block in range(target.shape[0] // width):
        target[block * width : (block + 1) * width, :] = stack_ref[
            start : start + width, block * width : (block + 1) * width
        ].astype(F32)


def ffn_unpack(count, starts_ref, *refs):
    pieces = refs[:count]
    up_ref, down_ref, stack_ref, sems = refs[count:]
    bring(starts_ref, pieces, stack_ref, sems)
    width = up_ref.shape[1]
    unlay(up_ref, stack_ref, 0, width)
    down_ref[...] = stack_ref[width:, :].astype(F32)


def attn_unpack(count, starts_ref, *refs):
    pieces = refs[:count]
    weight_ref, out_ref, stack_ref, sems = refs[count:]
    bring(starts_ref, pieces, stack_ref, sems)
    width = weight_ref.shape[2]
    for which in range(3):
        unlay(weight_ref.at[which], stack_ref, which * width, width)
    out_ref[...] = stack_ref[3 * width :, :].astype(F32)


def gelu_parts(pre):
    share = 0.5 * (1.0 + lax.erf(pre * 0.7071067811865476))
    slope = share + pre * (0.3989422804014327 * jnp.exp(-0.5 * pre * pre))
    return pre * share, slope


def fill_padded(padded_ref, text_ref):
    rows, wide = text_ref.shape
    edge = jnp.zeros((8, wide), F32)
    padded_ref[0:8, :] = edge
    padded_ref[rows + 8 : rows + 16, :] = edge
    for at in range(rows // CHUNK):
        here = slice(at * CHUNK, (at + 1) * CHUNK)
        padded_ref[at * CHUNK + 8 : (at + 1) * CHUNK + 8, :] = text_ref[here, :].astype(F32)


def text_forward(
    text_ref,
    mel_ref,
    kernel_ref,
    bias_ref,
    gain_ref,
    hidden_bias_ref,
    in_ref,
    out_ref,
    project_ref,
    frame_ref,
    normed_ref,
    pre_ref,
    energy_ref,
    mixed_ref,
    refined_ref,
    state_ref,
    padded_ref,
    hidden_ref,
):
    rows, wide = text_ref.shape
    taps = kernel_ref.shape[0]
    fill_padded(padded_ref, text_ref)

    def front(at, carry):
        start = pl.multiple_of(at * CHUNK, CHUNK)
        near = padded_ref[pl.ds(start, CHUNK + 16), :]
        conv = bias_ref[0:1, :]
        for tap in range(taps):
            shift = 8 + tap - taps // 2
            conv = conv + near[shift : shift + CHUNK, :] * kernel_ref[tap : tap + 1, :]
        xhat, _ = norm_parts(conv)
        normed_ref[pl.ds(start, CHUNK), :] = (xhat * gain_ref[...] + bias_ref[1:2, :]).astype(BF16)
        return carry

    lax.fori_loop(0, rows // CHUNK, front, 0)
    pre_ref[...] = mm(normed_ref[...], in_ref[...]) + hidden_bias_ref[0:1, :]

    def gelu(at, carry):
        here = pl.ds(at * CHUNK, CHUNK)
        hidden, _ = gelu_parts(pre_ref[here, :])
        hidden_ref[here, :] = hidden
        return carry + fold(hidden * hidden)

    squares = lax.fori_loop(0, rows // CHUNK, gelu, jnp.zeros((8, pre_ref.shape[1]), F32))
    energy = jnp.sqrt(jnp.sum(squares, axis=0, keepdims=True))
    energy_ref[0:1, :] = energy
    ratio = energy / (jnp.mean(energy, axis=1, keepdims=True) + 1e-06)

    def mix(at, carry):
        here = pl.ds(at * CHUNK, CHUNK)
        hidden = hidden_ref[here, :]
        mixed = hidden_bias_ref[1:2, :] * (hidden * ratio) + hidden_bias_ref[2:3, :] + hidden
        mixed_ref[here, :] = mixed.astype(BF16)
        return carry

    lax.fori_loop(0, rows // CHUNK, mix, 0)
    refined_ref[...] = (
        text_ref[...].astype(F32) + mm(mixed_ref[...], out_ref[...]) + bias_ref[2:3, :]
    ).astype(BF16)
    state_ref[...] = (
        mm(mel_ref[...], project_ref[0 : mel_ref.shape[1], :])
        + mm(refined_ref[...], project_ref[mel_ref.shape[1] :, :])
        + frame_ref[0:1, :]
    )


def full_line(members, wide):
    have = sum(member.shape[1] for member in members)
    return jnp.concatenate(list(members) + [jnp.zeros((1, wide - have), F32)], axis=1)


def small_rows(group):
    count = 12 + 2 * group
    return count + -count % 16


def text_backward(group, *refs):
    refs = list(refs)

    def take(count=1):
        taken = [refs.pop(0) for _ in range(count)]
        return taken[0] if count == 1 else taken

    own_ref, grad_zero_ref, text_ref, mel_ref, refined_ref, mixed_ref, normed_ref = take(7)
    pre_ref, energy_ref, kernel_ref, bias_ref, gain_ref, hidden_bias_ref = take(6)
    in_ref, out_ref, project_ref, attn_sums_ref, ffn_sums_ref = take(5)
    high_bias_ref, low_bias_ref, up_bias_ref = take(3)
    grad_text_ref, mods_ref = take(2)
    slots = [take() for _ in range(group)]
    stack_ref, sems, padded_ref, outer_ref, refined_grad_ref, low_ref, mixed_grad_ref = take(7)
    pre_low_ref, normed_grad_ref, lines_ref = take(3)
    small = small_rows(group)
    own = own_ref[0]
    rows, wide = text_ref.shape
    model = grad_zero_ref.shape[1]
    taps = kernel_ref.shape[0]
    mel_at = 3 * wide
    small_at = mel_at + mel_ref.shape[1] + (-(mel_at + mel_ref.shape[1])) % 16

    for at, (source, row) in enumerate(
        (
            (attn_sums_ref, 1),
            (attn_sums_ref, 0),
            (ffn_sums_ref, 5),
            (ffn_sums_ref, 3),
            (ffn_sums_ref, 2),
            (ffn_sums_ref, 1),
        )
    ):
        mods_ref[at : at + 1, :] = source[row : row + 1, :]

    grad_zero = grad_zero_ref[...]
    grad_refined = inner_cols(grad_zero, project_ref[mel_ref.shape[1] :, :])
    refined_grad_ref[...] = grad_refined
    low_ref[...] = grad_refined.astype(BF16)
    sum_out = jnp.sum(fold(grad_refined), axis=0, keepdims=True)
    mixed_grad_ref[...] = inner_cols(low_ref[...], out_ref[...])
    stack_ref[0:wide, :] = inner_rows(refined_ref[...], grad_zero).astype(BF16)
    spare = jnp.zeros((small_at - mel_at - mel_ref.shape[1], model), F32)
    grad_mel = inner_rows(mel_ref[...], grad_zero)
    stack_ref[mel_at:small_at, :] = jnp.concatenate([grad_mel, spare], axis=0).astype(BF16)
    rest = stack_ref.shape[0] - small_at - small
    if rest:
        stack_ref[small_at + small :, :] = jnp.zeros((rest, model), BF16)
    grad_out = inner_rows(mixed_ref[...], low_ref[...]).astype(BF16)
    stack_ref[2 * wide : 3 * wide, 0:wide] = grad_out[0:wide, :]
    stack_ref[2 * wide : 3 * wide, wide:] = grad_out[wide:, :]

    energy = energy_ref[0:1, :]
    mean = jnp.mean(energy, axis=1, keepdims=True) + 1e-06
    ratio = energy / mean

    def first_pass(at, carry):
        along, plain = carry
        here = pl.ds(at * CHUNK, CHUNK)
        hidden, _ = gelu_parts(pre_ref[here, :])
        grad = mixed_grad_ref[here, :]
        return along + fold(grad * hidden), plain + fold(grad)

    zero = jnp.zeros((8, model), F32)
    along, plain = lax.fori_loop(0, rows // CHUNK, first_pass, (zero, zero))
    along = jnp.sum(along, axis=0, keepdims=True)
    sum_beta = jnp.sum(plain, axis=0, keepdims=True)
    gamma = hidden_bias_ref[1:2, :]
    grad_ratio = gamma * along
    grad_mean = jnp.sum(grad_ratio * energy, axis=1, keepdims=True) / (mean * mean)
    grad_energy = grad_ratio / mean - grad_mean / model
    spread = grad_energy / energy
    factor = 1.0 + gamma * ratio

    def second_pass(at, carry):
        here = pl.ds(at * CHUNK, CHUNK)
        hidden, slope = gelu_parts(pre_ref[here, :])
        grad = (mixed_grad_ref[here, :] * factor + hidden * spread) * slope
        pre_low_ref[here, :] = grad.astype(BF16)
        return carry + fold(grad)

    sum_in = jnp.sum(lax.fori_loop(0, rows // CHUNK, second_pass, zero), axis=0, keepdims=True)
    normed_grad_ref[...] = inner_cols(pre_low_ref[...], in_ref[...])
    stack_ref[wide : 2 * wide, :] = inner_rows(normed_ref[...], pre_low_ref[...]).astype(BF16)

    fill_padded(padded_ref, text_ref)
    edge = jnp.zeros((8, wide), F32)
    outer_ref[0:8, :] = edge
    outer_ref[rows + 8 : rows + 16, :] = edge
    narrow = jnp.zeros((8, wide), F32)
    step = CHUNK // 2

    def conv_back(at, carry):
        sum_gain, sum_norm, sum_conv, sum_taps = carry
        start = pl.multiple_of(at * step, step)
        near = padded_ref[pl.ds(start, step + 16), :]
        conv = bias_ref[0:1, :]
        for tap in range(taps):
            shift = 8 + tap - taps // 2
            conv = conv + near[shift : shift + step, :] * kernel_ref[tap : tap + 1, :]
        xhat, root = norm_parts(conv)
        grad = normed_grad_ref[pl.ds(start, step), :]
        entry = grad * gain_ref[...]
        entry_mean = jnp.mean(entry, axis=-1, keepdims=True)
        entry_along = jnp.mean(entry * xhat, axis=-1, keepdims=True)
        grad_conv = root * (entry - entry_mean - xhat * entry_along)
        outer_ref[pl.ds(start + 8, step), :] = grad_conv
        sum_taps = tuple(
            member
            + fold(grad_conv * near[8 + tap - taps // 2 : 8 + tap - taps // 2 + step, :])
            for tap, member in enumerate(sum_taps)
        )
        return (
            sum_gain + fold(grad * xhat),
            sum_norm + fold(grad),
            sum_conv + fold(grad_conv),
            sum_taps,
        )

    sum_gain, sum_norm, sum_conv, sum_taps = lax.fori_loop(
        0, rows // step, conv_back, (narrow, narrow, narrow, (narrow,) * taps)
    )

    def text_grad(at, carry):
        start = pl.multiple_of(at * CHUNK, CHUNK)
        near = outer_ref[pl.ds(start, CHUNK + 16), :]
        total = refined_grad_ref[pl.ds(start, CHUNK), :]
        for tap in range(taps):
            shift = 8 + taps // 2 - tap
            total = total + near[shift : shift + CHUNK, :] * kernel_ref[tap : tap + 1, :]
        grad_text_ref[pl.ds(start, CHUNK), :] = total
        return carry

    lax.fori_loop(0, rows // CHUNK, text_grad, 0)

    def line(member):
        return jnp.sum(member, axis=0, keepdims=True)

    halves = [line(member) for member in sum_taps] + [line(sum_gain)]
    halves += [line(sum_conv), line(sum_norm), sum_out, jnp.zeros((1, wide), F32)]
    lines = [
        jnp.concatenate(halves[at : at + 2], axis=1) for at in range(0, len(halves), 2)
    ]
    lines += [sum_in, ratio * along, sum_beta]
    lines += [attn_sums_ref[2:3, :], ffn_sums_ref[4:5, :], ffn_sums_ref[0:1, :]]
    lines_ref[...] = jnp.zeros_like(lines_ref)
    for at, member in enumerate(lines):
        lines_ref[at : at + 1, :] = member
    parts = group // 2
    row = lax.broadcasted_iota(jnp.int32, lines_ref.shape, 0)
    total = lines_ref[...]
    for slot in range(group):
        source_ref = low_bias_ref if slot < parts else high_bias_ref
        owner = jnp.bitwise_xor(own, slot)
        members = [source_ref[slot % parts, which : which + 1, :] for which in range(3)]
        total = jnp.where(row == 12 + owner, full_line(members, model), total)
        total = jnp.where(row == 12 + group + owner, full_line([up_bias_ref[slot]], model), total)
    lines_ref[...] = total
    stack_ref[small_at : small_at + small, :] = lines_ref[...].astype(BF16)

    size = stack_ref.shape[0] // group
    copies = []
    for slot in range(group):
        start = pl.multiple_of(jnp.bitwise_xor(own, slot) * size, size)
        copies.append(
            pltpu.make_async_copy(stack_ref.at[pl.ds(start, size), :], slots[slot], sems.at[slot])
        )
    for copy in copies:
        copy.start()
    for copy in copies:
        copy.wait()


def text_unpack(count, group, starts_ref, own_ref, *refs):
    pieces = refs[:count]
    project_ref, in_ref, out_ref, taps_ref, bias_ref, gain_ref = refs[count : count + 6]
    hidden_ref, frame_ref, qkv_bias_ref, up_bias_ref, stack_ref, sems, lines_ref = refs[count + 6 :]
    bring(starts_ref, pieces, stack_ref, sems)
    own = own_ref[0]
    wide = in_ref.shape[0]
    taps = taps_ref.shape[0]
    mels = project_ref.shape[0] - wide
    mel_at = 3 * wide
    small_at = mel_at + mels + (-(mel_at + mels)) % 16
    project_ref[0:mels, :] = stack_ref[mel_at : mel_at + mels, :].astype(F32)
    project_ref[mels:, :] = stack_ref[0:wide, :].astype(F32)
    in_ref[...] = stack_ref[wide : 2 * wide, :].astype(F32)
    out_ref[0:wide, :] = stack_ref[2 * wide : 3 * wide, 0:wide].astype(F32)
    out_ref[wide:, :] = stack_ref[2 * wide : 3 * wide, wide:].astype(F32)
    lines_ref[...] = stack_ref[small_at : small_at + small_rows(group), :].astype(F32)

    def half(at):
        return lines_ref[at // 2 : at // 2 + 1, (at % 2) * wide : (at % 2 + 1) * wide]

    for tap in range(taps):
        taps_ref[tap : tap + 1, :] = half(tap)
    gain_ref[...] = half(taps)
    for at in range(3):
        bias_ref[at : at + 1, :] = half(taps + 1 + at)
    first = (taps + 5) // 2
    hidden_ref[...] = lines_ref[first : first + 3, :]
    frame_ref[...] = lines_ref[first + 3 : first + 6, :]
    row = lax.broadcasted_iota(jnp.int32, lines_ref.shape, 0)

    def pick(at):
        return jnp.sum(jnp.where(row == at, lines_ref[...], 0.0), axis=0, keepdims=True)

    line = pick(12 + own)
    width = qkv_bias_ref.shape[1]
    for which in range(3):
        qkv_bias_ref[which : which + 1, :] = line[:, which * width : (which + 1) * width]
    up_bias_ref[...] = pick(12 + group + own)[:, 0 : up_bias_ref.shape[1]]


ANY = pl.BlockSpec(memory_space=pl.ANY)
SMEM = pl.BlockSpec(memory_space=pltpu.SMEM)


def whole(shape):
    return pl.BlockSpec(shape, lambda g: (0,) * len(shape))


def held(shape, parts=None):
    if parts is None:
        return pl.BlockSpec((1,) + shape, lambda g: (g,) + (0,) * len(shape))
    return pl.BlockSpec((1,) + shape, lambda g: (parts - 1 - g,) + (0,) * len(shape))


def run_kernel(kernel, parts, inputs, outputs, scratch):
    return pl.pallas_call(
        kernel,
        grid=(parts,),
        in_specs=[spec for spec, _ in inputs],
        out_specs=[spec for spec, _, _ in outputs],
        out_shape=[jax.ShapeDtypeStruct(shape, kind) for _, shape, kind in outputs],
        scratch_shapes=scratch,
        compiler_params=pltpu.CompilerParams(vmem_limit_bytes=VMEM),
        cost_estimate=pl.CostEstimate(flops=1024, bytes_accessed=1024, transcendentals=0),
    )(*[array for _, array in inputs])


def after(arrays, *others):
    arrays = tuple(arrays)
    return lax.optimization_barrier(arrays + others)[: len(arrays)]


def swap(array, axis, bit):
    return lax.ppermute(array, axis, [(at, at ^ bit) for at in range(lax.axis_size(axis))])


def low_bit(slot):
    return slot & -slot


def tile_rows(rows):
    return next(size for size in (256, 224, 128, 112, 96, 80, 64, 48, 32, 16) if rows % size == 0)


def add_arrays(arrays):
    rows, wide = arrays[0].shape
    tile = tile_rows(rows)
    spec = pl.BlockSpec((tile, wide), lambda g: (g, 0))
    return run_kernel(
        partial(sum_kernel, len(arrays)),
        rows // tile,
        [(spec, array) for array in arrays],
        [(spec, (rows, wide), BF16)],
        [],
    )[0]


def add_and_split(arrays, upper):
    rows, wide = arrays[0].shape
    half = rows // 2
    tile = tile_rows(half)
    steps = half // tile
    spec = pl.BlockSpec((tile, wide), lambda g: (g, 0))
    high = pl.BlockSpec((tile, wide), lambda g: (g + steps, 0))
    return run_kernel(
        partial(split_kernel, len(arrays)),
        steps,
        [(SMEM, upper)]
        + [(spec, array) for array in arrays]
        + [(high, array) for array in arrays],
        [(spec, (half, wide), BF16)] * 2,
        [],
    )


class Fetch:
    def __init__(self, array, axis):
        size = array.shape[axis] // 2
        start = lax.axis_index("dp") % 2 * size
        self.half = lax.dynamic_slice_in_dim(array, start, size, axis=axis)
        self.group = lax.axis_size("heads")
        self.slots = {0: [array]}
        self.sent = {}

    def core(self, slot, *others):
        pieces = after(self.slots[slot], *others)
        self.slots[slot + 1] = [swap(piece, "heads", 1) for piece in pieces]

    def send(self, *others):
        (self.half,) = after([self.half], *others)
        for slot in range(2, self.group, 2):
            bit = low_bit(slot)
            if slot == bit:
                self.sent[slot] = swap(self.half, "heads", bit)

    def share(self, *others):
        for slot in range(2, self.group, 2):
            bit = low_bit(slot)
            if slot == bit:
                (came,) = after([self.sent[slot]], *others)
            else:
                came = swap(self.slots[slot - bit][0], "heads", bit)
            self.slots[slot] = [came, swap(came, "dp", 1)]

    def cores(self, first, last, *others):
        for slot in range(first, last, 2):
            self.core(slot, *others)

    def listed(self):
        return [self.slots[slot] for slot in range(self.group)]


def flat(slots):
    return [piece for pieces in slots for piece in pieces]


class GroupSum:
    def __init__(self):
        self.arrived = {}

    def put(self, slot, array, *others):
        arrays = [array] + self.arrived.pop(slot, [])
        if slot == 0:
            return arrays
        total = add_arrays(after(arrays, *others)) if len(arrays) > 1 else array
        bit = low_bit(slot)
        self.arrived.setdefault(slot - bit, []).append(swap(total, "heads", bit))
        return total


class DataSum:
    def __init__(self, arrays, bits):
        self.arrays = list(arrays)
        self.bits = list(bits)
        self.halved = []
        self.rows = arrays[0].shape[0]
        self.pieces = None

    def step(self, *others):
        arrays = after(self.arrays, *others)
        if not self.bits:
            total = add_arrays(arrays)
            self.gather(total)
            return total
        bit = self.bits.pop(0)
        if arrays[0].shape[0] % 32 == 0:
            upper = (lax.axis_index("dp") // bit % 2).astype(jnp.int32).reshape(1)
            keep, send = add_and_split(arrays, upper)
            self.halved.append(bit)
        else:
            keep = send = add_arrays(arrays)
        self.arrays = [keep, swap(send, "dp", bit)]
        return keep

    def gather(self, total):
        self.pieces = {0: total}
        for bit in self.halved[::-1]:
            for mask, piece in list(self.pieces.items()):
                self.pieces[mask | bit] = swap(piece, "dp", bit)

    def starts(self):
        own = lax.axis_index("dp")
        return [
            sum(
                (own ^ mask) // bit % 2 * (self.rows >> (at + 1))
                for at, bit in enumerate(self.halved)
            )
            for mask in self.pieces
        ]


def axis_bits(axis):
    size = lax.axis_size(axis)
    return [1 << at for at in range(size.bit_length() - 1)]


def on_device(
    noisy_mel,
    cond_mel,
    text_embed,
    time_embed,
    lengths,
    spans,
    dw_kernel,
    text_bias,
    text_gain,
    text_hidden,
    pw_in,
    pw_out,
    in_proj,
    frame_bias,
    mod_weight,
    mod_bias,
    qkv_weight,
    qkv_bias,
    out_weight,
    ff_in,
    ff_in_bias,
    ff_out,
    cotangent,
):
    group = lax.axis_size("heads")
    own = lax.axis_index("heads")
    own_data = lax.axis_index("dp")
    rows = text_embed.shape[0]
    model_width = in_proj.shape[1]
    width = qkv_weight.shape[2]
    units = ff_in.shape[1]
    block = min(128, width)
    parts = group // 2
    full = (rows, model_width)

    fetches = [Fetch(qkv_weight, 1), Fetch(out_weight, 0), Fetch(ff_in, 0), Fetch(ff_out, 0)]
    for fetch in fetches[:2]:
        fetch.send()
        fetch.core(0)

    time_rows = time_embed.astype(F32)
    activated, silu_back = jax.vjp(jax.nn.silu, time_rows)
    activated_low = activated.astype(BF16)
    modulation = (mm(activated_low, mod_weight) + mod_bias).astype(BF16)
    biases = jnp.concatenate([qkv_bias.reshape(-1), ff_in_bias])
    riders = jnp.broadcast_to(biases[None, :], (group, biases.size))
    sent = jnp.concatenate([modulation, riders], axis=1)
    came = lax.all_to_all(sent, "heads", split_axis=0, concat_axis=1, tiled=True)
    came = came.reshape(group, sent.shape[1]).astype(F32)
    mod_rows = came[:, : modulation.shape[1]].reshape(6, model_width)
    slot_owner = jnp.bitwise_xor(jnp.arange(group, dtype=jnp.int32), own)
    biases_all = jnp.take(came[:, modulation.shape[1] :], slot_owner, axis=0)
    qkv_bias_all = biases_all[:, : 3 * width].reshape(group, 3, width)
    up_bias_all = biases_all[:, 3 * width :].reshape(group, 1, units)

    position = jnp.arange(rows, dtype=jnp.int32)
    inside = (position >= spans[0, 0]) & (position < spans[0, 1])
    keep = jnp.where(inside, 0.0, 1.0).astype(F32)[:, None]
    count = lax.dynamic_slice_in_dim(lengths, own, 1)
    lane = jnp.arange(block, dtype=jnp.int32)
    pair = ((lane % HD) // 2).astype(F32)
    angle = position.astype(F32)[:, None] * (10000.0 ** (-2.0 * pair / HD))[None, :]
    cosine = jnp.cos(angle)
    sine = jnp.sin(angle) * jnp.where(lane % 2 == 0, -1.0, 1.0)[None, :]

    cond_low = (cond_mel.astype(F32) * keep).astype(BF16)
    mel = jnp.concatenate([noisy_mel, cond_low], axis=1)
    mels = mel.shape[1]
    text_width = text_embed.shape[1]
    gain = text_gain[None, :]

    def block_of(array):
        return (whole(array.shape), array)

    normed_text, pre_act, energy, mixed_text, refined, state_zero = run_kernel(
        text_forward,
        1,
        [
            block_of(member)
            for member in (
                text_embed,
                mel,
                dw_kernel,
                text_bias,
                gain,
                text_hidden,
                pw_in,
                pw_out,
                in_proj,
                frame_bias,
            )
        ],
        [
            (whole(shape), shape, kind)
            for shape, kind in (
                ((rows, text_width), BF16),
                ((rows, pw_in.shape[1]), F32),
                ((8, pw_in.shape[1]), F32),
                ((rows, pw_in.shape[1]), BF16),
                ((rows, text_width), BF16),
                (full, F32),
            )
        ],
        [pltpu.VMEM((rows + 16, text_width), F32), pltpu.VMEM((rows, pw_in.shape[1]), F32)],
    )

    def semaphores(number, pieces=2):
        shape = (number, pieces) if pieces > 1 else (number,)
        return pltpu.SemaphoreType.DMA(shape)

    def attn_buffers(number, pieces=2):
        return [
            pltpu.VMEM((number, 3, model_width, width), BF16),
            pltpu.VMEM((number, width, model_width), BF16),
            semaphores(number, pieces),
            semaphores(number, pieces),
        ]

    def ffn_buffers(number, pieces=2):
        return [
            pltpu.VMEM((number, model_width, units), BF16),
            pltpu.VMEM((number, units, model_width), BF16),
            semaphores(number, pieces),
            semaphores(number, pieces),
        ]

    half_index = (own_data % 2).astype(jnp.int32).reshape(1)

    def pieces_of(slots):
        return tuple(len(pieces) for pieces in slots)

    for fetch in fetches[2:]:
        fetch.send(state_zero)
    for fetch in fetches[:2]:
        fetch.share()
        fetch.cores(2, parts)
    kept = []
    for turn in range(2):
        first, last = turn == 0, turn == 1
        if last:
            for fetch in fetches[:2]:
                fetch.cores(parts, group, normed)
            for fetch in fetches[2:]:
                fetch.share(normed)
                fetch.core(0, normed)
            (before,) = after([before], *[fetch.slots[2][0] for fetch in fetches[2:]])
        chosen = range(turn * parts, (turn + 1) * parts)
        qkv_here = [fetches[0].slots[slot] for slot in chosen]
        out_here = [fetches[1].slots[slot] for slot in chosen]
        inputs = [
            (SMEM, count),
            (SMEM, half_index),
            (whole(full), state_zero),
            (whole((6, model_width)), mod_rows),
            (held((3, width)), qkv_bias_all[chosen[0] : chosen[-1] + 1]),
            (whole((3, model_width)), frame_bias),
            (whole((rows, block)), cosine),
            (whole((rows, block)), sine),
        ]
        inputs += [(ANY, member) for member in flat(qkv_here) + flat(out_here)]
        if not first:
            inputs += [(whole(full), normed), (whole(full), before)]
        outputs = [(held((rows, width)), (parts, rows, width), BF16)] * 4
        outputs += [(held((8, rows)), (parts, 8, rows), F32)]
        if first:
            outputs += [(whole(full), full, BF16)]
        outputs += [(whole(full), full, F32)]
        if last:
            outputs += [(whole(full), full, F32), (whole(full), full, BF16)]
        results = run_kernel(
            partial(attention_forward, pieces_of(qkv_here), first, last),
            parts,
            inputs,
            outputs,
            attn_buffers(parts) + ([pltpu.VMEM(full, F32)] if last else []),
        )
        kept.append(results[:5])
        if first:
            normed, before = results[5:]
        else:
            branch, state_one, ffn_in = results[5:]

    qkv_all, out_all = fetches[0].listed(), fetches[1].listed()
    fetches[2].cores(2, group, ffn_in)
    fetches[3].cores(2, group, ffn_in)
    up_all, down_all = fetches[2].listed()[::-1], fetches[3].listed()[::-1]
    inputs = [
        (SMEM, half_index),
        (whole(full), cotangent),
        (whole(full), state_one),
        (whole(full), branch),
        (whole(full), ffn_in),
        (whole((6, model_width)), mod_rows),
        (held((1, units), group), up_bias_all),
        (whole((3, model_width)), frame_bias),
    ]
    inputs += [(ANY, member) for member in flat(up_all) + flat(down_all)]
    merged = (2 * units, model_width)
    outputs = [(held((1, units), group), (group, 1, units), F32)]
    outputs += [(whole((8, model_width)), (8, model_width), F32)]
    outputs += [(ANY, merged, BF16)] * group
    outputs += [(whole(full), full, BF16)] * 2 + [(whole(full), full, F32)]
    outputs += [(whole(full), full, BF16)]
    results = run_kernel(
        partial(feed_forward, pieces_of(up_all), True, True),
        group,
        inputs,
        outputs,
        [
            pltpu.VMEM((group, model_width, units), BF16),
            pltpu.VMEM((group, units, model_width), BF16),
            semaphores(group),
            semaphores(group),
            pltpu.VMEM((group,) + merged, BF16),
            semaphores(group, 1),
            pltpu.VMEM((model_width, rows), BF16),
            pltpu.VMEM((rows, units), BF16),
            pltpu.VMEM((rows, units), BF16),
        ]
        + [pltpu.VMEM(full, F32)] * 2,
    )
    grad_up_bias, ffn_sums = results[:2]
    output, grad_one, grad_attn = results[3 + group :]
    ffn_grads = results[2 : 2 + group][::-1]

    attn_grads = []
    merged = (4 * width, model_width)
    qkv_bias_parts = []
    for turn in range(2):
        first, last = turn == 0, turn == 1
        chosen = [group - 1 - turn * parts - at for at in range(parts)]
        inputs = [
            (SMEM, count),
            (SMEM, half_index),
            (whole(full), grad_attn),
            (whole(full), normed),
            (whole((6, model_width)), mod_rows),
            (whole((rows, block)), cosine),
            (whole((rows, block)), sine),
        ]
        inputs += [(held((rows, width), parts), member) for member in kept[1 - turn][:4]]
        inputs += [(held((8, rows), parts), kept[1 - turn][4])]
        inputs += [(ANY, member) for member in flat([qkv_all[slot] for slot in chosen])]
        inputs += [(ANY, member) for member in flat([out_all[slot] for slot in chosen])]
        if not first:
            inputs += [(whole(full), back)]
        if last:
            inputs += [(whole(full), state_zero), (whole(full), grad_one)]
        outputs = [(held((3, width), parts), (parts, 3, width), F32)]
        outputs += [(ANY, merged, BF16)] * parts
        if last:
            outputs += [(whole(full), full, BF16), (whole((8, model_width)), (8, model_width), F32)]
        else:
            outputs += [(whole(full), full, F32)]
        results = run_kernel(
            partial(attention_backward, pieces_of([qkv_all[slot] for slot in chosen]), first, last),
            parts,
            inputs,
            outputs,
            attn_buffers(parts)
            + [pltpu.VMEM((parts,) + merged, BF16), semaphores(parts, 1)]
            + [pltpu.VMEM((model_width, rows), BF16), pltpu.VMEM((rows, width), BF16)]
            + ([pltpu.VMEM(full, F32)] if last else []),
        )
        qkv_bias_parts.append(results[0])
        attn_grads = list(results[1 : 1 + parts])[::-1] + attn_grads
        if first:
            back = results[1 + parts]
            ffn_sum = GroupSum()
            for slot in range(group - 1, 0, -1):
                token = ffn_sum.put(slot, ffn_grads[slot], back)
                if slot % 2 == 0:
                    (back,) = after([back], token)
        else:
            grad_zero, attn_sums = results[1 + parts :]
    attn_sum = GroupSum()
    for slot in range(group - 1, 0, -1):
        token = attn_sum.put(slot, attn_grads[slot], grad_zero)
        if slot % 2 == 0:
            (grad_zero,) = after([grad_zero], token)

    stack_rows = 3 * text_width + mels
    stack_rows += -stack_rows % 16 + small_rows(group)
    stack_rows += -stack_rows % (16 * group)
    own_index = own.astype(jnp.int32).reshape(1)
    results = run_kernel(
        partial(text_backward, group),
        1,
        [(SMEM, own_index)]
        + [
            block_of(member)
            for member in (
                grad_zero,
                text_embed,
                mel,
                refined,
                mixed_text,
                normed_text,
                pre_act,
                energy,
                dw_kernel,
                text_bias,
                gain,
                text_hidden,
                pw_in,
                pw_out,
                in_proj,
                attn_sums,
                ffn_sums,
                qkv_bias_parts[0],
                qkv_bias_parts[1],
                grad_up_bias,
            )
        ],
        [
            (whole((rows, text_width)), (rows, text_width), F32),
            (whole((6, model_width)), (6, model_width), F32),
        ]
        + [(ANY, (stack_rows // group, model_width), BF16)] * group,
        [
            pltpu.VMEM((stack_rows, model_width), BF16),
            semaphores(group, 1),
            pltpu.VMEM((rows + 16, text_width), F32),
            pltpu.VMEM((rows + 16, text_width), F32),
            pltpu.VMEM((rows, text_width), F32),
            pltpu.VMEM((rows, text_width), BF16),
            pltpu.VMEM((rows, pw_in.shape[1]), F32),
            pltpu.VMEM((rows, pw_in.shape[1]), BF16),
            pltpu.VMEM((rows, text_width), F32),
            pltpu.VMEM((small_rows(group), model_width), F32),
        ],
    )
    grad_text, grad_mod = results[:2]
    text_sum = GroupSum()
    bits = axis_bits("dp")
    ffn_data = DataSum(ffn_sum.put(0, ffn_grads[0]), bits)
    token = ffn_data.step(grad_mod)
    for slot in range(group - 1, 0, -1):
        total = text_sum.put(slot, results[2 + slot], token)
        if slot % 2 == 0:
            token = total
    attn_data = DataSum(attn_sum.put(0, attn_grads[0]), bits)
    text_data = DataSum(text_sum.put(0, results[2]), bits)
    (grad_mod,) = after([grad_mod], token)
    steps = [(at, ffn_data) for at in range(1, len(bits) + 1)]
    for at in range(len(bits) + 1):
        steps.append((at + 2.2 if at else 1.5, attn_data))
        steps.append((at + 2.25, text_data))
    for _, member in sorted(steps, key=lambda step: step[0]):
        token = member.step(token)
    text_pieces = [[text_data.pieces[mask] for mask in text_data.pieces]]
    for slot in range(1, group):
        bit = low_bit(slot)
        text_pieces.append([swap(piece, "heads", bit) for piece in text_pieces[slot - bit]])
    slot_rows = stack_rows // group
    text_starts = [
        slot_owner[slot] * slot_rows + start
        for slot in range(group)
        for start in text_data.starts()
    ]
    text_pieces = [piece for pieces in text_pieces for piece in pieces]
    unpacked = (
        in_proj.shape,
        pw_in.shape,
        pw_out.shape,
        dw_kernel.shape,
        text_bias.shape,
        gain.shape,
        text_hidden.shape,
        frame_bias.shape,
        (3, width),
        (1, units),
    )
    unpacked = run_kernel(
        partial(text_unpack, len(text_pieces), group),
        1,
        [(SMEM, jnp.stack(text_starts).astype(jnp.int32)), (SMEM, own_index)]
        + [(ANY, member) for member in text_pieces],
        [(whole(shape), shape, F32) for shape in unpacked],
        [
            pltpu.VMEM((stack_rows, model_width), BF16),
            semaphores(len(text_pieces), 1),
            pltpu.VMEM((small_rows(group), model_width), F32),
        ],
    )
    def unpack(data, kernel, first, second):
        pieces = list(data.pieces.values())
        return run_kernel(
            partial(kernel, len(pieces)),
            1,
            [(SMEM, jnp.stack(data.starts()).astype(jnp.int32))]
            + [(ANY, member) for member in pieces],
            [(whole(first.shape), first.shape, F32), (whole(second.shape), second.shape, F32)],
            [pltpu.VMEM((data.rows, model_width), BF16), semaphores(len(pieces), 1)],
        )

    weight_up, weight_down = unpack(ffn_data, ffn_unpack, ff_in, ff_out)
    weight_qkv, weight_out = unpack(attn_data, attn_unpack, qkv_weight, out_weight)

    grad_mod = grad_mod.astype(BF16).reshape(1, -1)
    grad_mod_cols = lax.all_to_all(grad_mod, "heads", split_axis=1, concat_axis=0, tiled=True)
    seen = jnp.concatenate([activated_low, grad_mod_cols], axis=1)
    for bit in bits:
        seen = jnp.concatenate([seen, swap(seen, "dp", bit)], axis=0)
    grad_mod_weight = inner_rows(seen[:, :model_width], seen[:, model_width:])
    grad_mod_bias = jnp.sum(seen[:, model_width:].astype(F32), axis=0)
    (grad_time,) = silu_back(inner_cols(grad_mod_cols, mod_weight))
    for bit in axis_bits("heads"):
        rounded = grad_time.astype(BF16)
        grad_time = rounded.astype(F32) + swap(rounded, "heads", bit).astype(F32)
    return (
        output,
        grad_text,
        grad_time,
        unpacked[3],
        unpacked[4],
        unpacked[5][0],
        unpacked[6],
        unpacked[1],
        unpacked[2],
        unpacked[0],
        unpacked[7],
        grad_mod_weight,
        grad_mod_bias,
        weight_qkv,
        unpacked[8],
        weight_out,
        weight_up,
        unpacked[9][0],
        weight_down,
    )


def solution(mesh):
    in_specs = (
        P(("dp", "heads"), None),
        P(("dp", "heads"), None),
        P(("dp", "heads"), None),
        P("dp", None),
        P("dp"),
        P(("dp", "heads"), None),
        P(),
        P(),
        P(),
        P(),
        P(),
        P(),
        P(),
        P(),
        P(None, "heads"),
        P("heads"),
        P(None, None, "heads"),
        P(None, "heads"),
        P("heads", None),
        P(None, "heads"),
        P("heads"),
        P("heads", None),
        P(("dp", "heads"), None),
    )
    out_specs = (
        P(("dp", "heads"), None),
        P(("dp", "heads"), None),
        P("dp", None),
        P(),
        P(),
        P(),
        P(),
        P(),
        P(),
        P(),
        P(),
        P(None, "heads"),
        P("heads"),
        P(None, None, "heads"),
        P(None, "heads"),
        P("heads", None),
        P(None, "heads"),
        P("heads"),
        P("heads", None),
    )
    return jax.shard_map(
        on_device, mesh=mesh, in_specs=in_specs, out_specs=out_specs, check_vma=False
    )
```

```python
from functools import partial

import jax
import jax.numpy as jnp
from jax import lax
from jax.experimental import pallas as pl
from jax.experimental.pallas import tpu as pltpu
from jax.sharding import PartitionSpec as P

HD = 64


def inner_rows(left, right):
    return lax.dot_general(
        left, right, (((0,), (0,)), ((), ())), preferred_element_type=jnp.float32
    )


def inner_cols(left, right):
    return lax.dot_general(
        left, right, (((1,), (1,)), ((), ())), preferred_element_type=jnp.float32
    )


F32 = jnp.float32
BF16 = jnp.bfloat16
CHUNK = 64
SPAN = 256
VMEM = 60 * 1024 * 1024


def mm(left, right):
    return jnp.dot(left, right, preferred_element_type=F32)


def fold(values):
    return jnp.sum(values.reshape(values.shape[0] // 8, 8, values.shape[1]), axis=0)


def norm_parts(values):
    mean = jnp.mean(values, axis=-1, keepdims=True)
    centred = values - mean
    root = lax.rsqrt(jnp.mean(centred * centred, axis=-1, keepdims=True) + 1e-06)
    return centred * root, root


def norm_pull(grad, scale, xhat, root):
    entry = grad * (1.0 + scale)
    mean = jnp.mean(entry, axis=-1, keepdims=True)
    along = jnp.mean(entry * xhat, axis=-1, keepdims=True)
    return root * (entry - mean - xhat * along)


def swap_pairs(block):
    width = block.shape[1]
    lane = lax.broadcasted_iota(jnp.int32, block.shape, 1)
    if width % 128 == 0:
        after = pltpu.roll(block, width - 1, 1)
        before = pltpu.roll(block, 1, 1)
    else:
        after = jnp.concatenate([block[:, 1:], block[:, :1]], axis=1)
        before = jnp.concatenate([block[:, width - 1 :], block[:, : width - 1]], axis=1)
    return jnp.where(lane % 2 == 0, after, before)


def head_lanes(block, head):
    if block.shape[1] == HD:
        return block
    lane = lax.broadcasted_iota(jnp.int32, block.shape, 1)
    return jnp.where((lane >= head * HD) & (lane < (head + 1) * HD), block, jnp.zeros_like(block))


def slot_copies(pieces, target, sems, at, axis, half):
    if len(pieces) == 1:
        return [pltpu.make_async_copy(pieces[0], target.at[at], sems.at[at, 0])]
    copies = []
    for which, piece in enumerate(pieces):
        size = piece.shape[axis]
        start = pl.multiple_of((half if which == 0 else 1 - half) * size, size)
        index = (at,) + (slice(None),) * axis + (pl.ds(start, size),)
        copies.append(pltpu.make_async_copy(piece, target.at[index], sems.at[at, which]))
    return copies


def start_all(step, copies):
    @pl.when(step == 0)
    def _():
        for members in copies:
            for copy in members:
                copy.start()


def wait_own(step, copies):
    for at, members in enumerate(copies):

        @pl.when(step == at)
        def _(members=members):
            for copy in members:
                copy.wait()


def send_own(step, results):
    for at, members in enumerate(results):

        @pl.when(step == at)
        def _(members=members):
            for copy in members:
                copy.start()


def wait_all(step, results):
    @pl.when(step == len(results) - 1)
    def _():
        for members in results:
            for copy in members:
                copy.wait()


def attention_forward(pieces, first, last, *refs):
    parts = len(pieces)
    refs = list(refs)

    def take(count=1):
        taken = [refs.pop(0) for _ in range(count)]
        return taken[0] if count == 1 else taken

    count_ref, half_ref, state_ref, mod_ref, bias_ref, frame_ref, cosine_ref, sine_ref = take(8)
    weights = [[take() for _ in range(number)] for number in pieces]
    outs = [[take() for _ in range(number)] for number in pieces]
    if not first:
        normed_ref, before_ref = take(2)
    query_ref, key_ref, value_ref, attended_ref, log_ref = take(5)
    if first:
        normed_ref = take()
    if last:
        branch_ref, one_ref, ffn_ref = take(3)
    else:
        total_ref = take()
    weight_ref, out_ref, weight_sem, out_sem = take(4)
    if last:
        total_ref = take()
    step = pl.program_id(0)
    rows = state_ref.shape[0]
    width = weight_ref.shape[3]
    block = cosine_ref.shape[1]
    count = count_ref[0]
    half = half_ref[0]
    copies = [
        slot_copies(weights[at], weight_ref, weight_sem, at, 1, half)
        + slot_copies(outs[at], out_ref, out_sem, at, 0, half)
        for at in range(parts)
    ]
    start_all(step, copies)

    @pl.when(step == 0)
    def _():
        if first:

            def chunk(at, carry):
                here = pl.ds(at * CHUNK, CHUNK)
                xhat, _ = norm_parts(state_ref[here, :])
                normed_ref[here, :] = (xhat * (1.0 + mod_ref[1:2, :]) + mod_ref[0:1, :]).astype(
                    BF16
                )
                return carry

            lax.fori_loop(0, rows // CHUNK, chunk, 0)
            total_ref[...] = jnp.zeros_like(total_ref)
        else:
            total_ref[...] = before_ref[...]

    wait_own(step, copies)
    normed = normed_ref[...]
    cosine = cosine_ref[...]
    sine = sine_ref[...]
    logs = jnp.zeros((rows, 128), F32)
    lane = lax.broadcasted_iota(jnp.int32, (rows, 128), 1)
    query_lin = mm(normed, weight_ref[step, 0]) + bias_ref[0, 0:1, :]
    key_lin = mm(normed, weight_ref[step, 1]) + bias_ref[0, 1:2, :]
    value_ref[0] = (mm(normed, weight_ref[step, 2]) + bias_ref[0, 2:3, :]).astype(BF16)
    for at in range(width // block):
        cut = slice(at * block, (at + 1) * block)
        piece = query_lin[:, cut]
        turned = piece * cosine + swap_pairs(piece) * sine
        query_ref[0, :, cut] = (turned * HD**-0.5).astype(BF16)
        piece = key_lin[:, cut]
        key_ref[0, :, cut] = (piece * cosine + swap_pairs(piece) * sine).astype(BF16)
    live = lax.broadcasted_iota(jnp.int32, (1, rows), 1) < count
    for at in range(width // block):
        cut = slice(at * block, (at + 1) * block)
        keys = key_ref[0, :, cut]
        values = value_ref[0, :, cut]
        results = [None] * (rows // SPAN)
        pieces = [[] for _ in range(rows // SPAN)]
        for head in range(block // HD):
            own_values = head_lanes(values, head)
            for part in range(rows // SPAN):
                queries = head_lanes(query_ref[0, part * SPAN : (part + 1) * SPAN, cut], head)
                scores = jnp.where(live, inner_cols(queries, keys), -1e30)
                top = jnp.max(scores, axis=1, keepdims=True)
                expo = jnp.exp(scores - top)
                total = jnp.sum(expo, axis=1, keepdims=True)
                weights = (expo * (1.0 / total)).astype(BF16)
                result = mm(weights, own_values)
                results[part] = result if head == 0 else results[part] + result
                pieces[part].append(top + jnp.log(total))
        for head in range(block // HD):
            column = jnp.concatenate([pieces[part][head] for part in range(rows // SPAN)], axis=0)
            logs = jnp.where(lane == at * (block // HD) + head, column, logs)
        for part in range(rows // SPAN):
            place = part * SPAN + lax.broadcasted_iota(jnp.int32, (SPAN, block), 0)
            attended_ref[0, part * SPAN : (part + 1) * SPAN, cut] = jnp.where(
                place < count, results[part], 0.0
            ).astype(BF16)
    log_ref[0] = jnp.transpose(logs)[0:8, :]
    total_ref[...] += mm(attended_ref[0], out_ref[step])

    if last:

        @pl.when(step == parts - 1)
        def _():
            def chunk(at, carry):
                here = pl.ds(at * CHUNK, CHUNK)
                branch = total_ref[here, :] + frame_ref[1:2, :]
                branch_ref[here, :] = branch
                state_one = state_ref[here, :] + mod_ref[2:3, :] * branch
                one_ref[here, :] = state_one
                xhat, _ = norm_parts(state_one)
                ffn_ref[here, :] = (xhat * (1.0 + mod_ref[4:5, :]) + mod_ref[3:4, :]).astype(BF16)
                return carry

            lax.fori_loop(0, rows // CHUNK, chunk, 0)


def lay(target_ref, at, start, value):
    model, width = value.shape
    for block in range(model // width):
        target_ref[at, start : start + width, block * width : (block + 1) * width] = value[
            block * width : (block + 1) * width, :
        ]


def feed_forward(pieces, first, last, *refs):
    parts = len(pieces)
    refs = list(refs)

    def take(count=1):
        taken = [refs.pop(0) for _ in range(count)]
        return taken[0] if count == 1 else taken

    half_ref, cotangent_ref, one_ref, branch_ref, source_ref, mod_ref, bias_ref, frame_ref = take(8)
    ups = [[take() for _ in range(number)] for number in pieces]
    downs = [[take() for _ in range(number)] for number in pieces]
    if not first:
        grad_ref, total_in_ref, back_in_ref = take(3)
    grad_bias_ref, sums_ref = take(2)
    grads = [take() for _ in range(parts)]
    if first:
        grad_ref = take()
    if last:
        output_ref, grad_one_ref, grad_attn_ref = take(3)
    else:
        total_ref, back_ref = take(2)
    up_ref, down_ref, up_sem, down_sem = take(4)
    grads_ref, grads_sem = take(2)
    turned_ref, hidden_ref, pre_ref = take(3)
    if last:
        total_ref, back_ref = take(2)
    step = pl.program_id(0)
    rows, wide = one_ref.shape
    inner = 0.7978845608028654
    cubic = 0.044715
    half = half_ref[0]
    copies = [
        slot_copies(ups[at], up_ref, up_sem, at, 0, half)
        + slot_copies(downs[at], down_ref, down_sem, at, 0, half)
        for at in range(parts)
    ]
    results = [
        (pltpu.make_async_copy(grads_ref.at[at], grads[at], grads_sem.at[at]),)
        for at in range(parts)
    ]
    start_all(step, copies)

    @pl.when(step == 0)
    def _():
        if first:

            def chunk(at, carry):
                here = pl.ds(at * CHUNK, CHUNK)
                grad = cotangent_ref[here, :].astype(F32) * mod_ref[5:6, :]
                grad_ref[here, :] = grad.astype(BF16)
                return carry + fold(grad)

            lanes = lax.fori_loop(0, rows // CHUNK, chunk, jnp.zeros((8, wide), F32))
            sums_ref[0:1, :] = jnp.sum(lanes, axis=0, keepdims=True)
            total_ref[...] = jnp.zeros_like(total_ref)
            back_ref[...] = jnp.zeros_like(back_ref)
        else:
            total_ref[...] = total_in_ref[...]
            back_ref[...] = back_in_ref[...]
        turned_ref[...] = jnp.transpose(source_ref[...])

    wait_own(step, copies)
    up = up_ref[step]
    down = down_ref[step]
    lanes = jnp.zeros((8, up.shape[1]), F32)
    for part in range(rows // SPAN):
        here = slice(part * SPAN, (part + 1) * SPAN)
        pre = mm(source_ref[here, :], up) + bias_ref[0]
        grad_hidden = inner_cols(grad_ref[here, :], down)
        square = pre * pre
        bend = jnp.tanh(pre * (inner + inner * cubic * square))
        half = 0.5 * (1.0 + bend)
        hidden = (pre * half).astype(BF16)
        slope = half + 0.5 * pre * (1.0 - bend * bend) * (inner + 3.0 * inner * cubic * square)
        grad_pre = grad_hidden * slope
        lanes = lanes + fold(grad_pre)
        grad_pre = grad_pre.astype(BF16)
        hidden_ref[here, :] = hidden
        pre_ref[here, :] = grad_pre
        total_ref[here, :] += mm(hidden, down)
        back_ref[here, :] += inner_cols(grad_pre, up)
    grad_bias_ref[0] = jnp.sum(lanes, axis=0, keepdims=True)
    width = up_ref.shape[2]
    grads_ref[step, width:, :] = inner_rows(hidden_ref[...], grad_ref[...]).astype(BF16)
    lay(grads_ref, step, 0, mm(turned_ref[...], pre_ref[...]).astype(BF16))
    send_own(step, results)

    if last:

        @pl.when(step == parts - 1)
        def _():
            def chunk(at, carry):
                gate_ffn, scale_ffn, shift_ffn, bias_attn, gate_attn = carry
                here = pl.ds(at * CHUNK, CHUNK)
                branch = total_ref[here, :] + frame_ref[2:3, :]
                state_one = one_ref[here, :]
                output_ref[here, :] = (state_one + mod_ref[5:6, :] * branch).astype(BF16)
                cotangent = cotangent_ref[here, :].astype(F32)
                xhat, root = norm_parts(state_one)
                back = back_ref[here, :]
                grad_one = cotangent + norm_pull(back, mod_ref[4:5, :], xhat, root)
                grad_one_ref[here, :] = grad_one
                grad_attn = grad_one * mod_ref[2:3, :]
                grad_attn_ref[here, :] = grad_attn.astype(BF16)
                return (
                    gate_ffn + fold(cotangent * branch),
                    scale_ffn + fold(back * xhat),
                    shift_ffn + fold(back),
                    bias_attn + fold(grad_attn),
                    gate_attn + fold(grad_one * branch_ref[here, :]),
                )

            start = tuple(jnp.zeros((8, wide), F32) for _ in range(5))
            lanes = lax.fori_loop(0, rows // CHUNK, chunk, start)
            for at, member in enumerate(lanes):
                sums_ref[at + 1 : at + 2, :] = jnp.sum(member, axis=0, keepdims=True)

    wait_all(step, results)


def attention_backward(pieces, first, last, *refs):
    parts = len(pieces)
    refs = list(refs)

    def take(count=1):
        taken = [refs.pop(0) for _ in range(count)]
        return taken[0] if count == 1 else taken

    count_ref, half_ref, grad_attn_ref, normed_ref, mod_ref, cosine_ref, sine_ref = take(7)
    query_ref, key_ref, value_ref, attended_ref, log_ref = take(5)
    weights = [[take() for _ in range(number)] for number in pieces]
    outs = [[take() for _ in range(number)] for number in pieces]
    if not first:
        before_ref = take()
    if last:
        state_ref, grad_one_ref = take(2)
    grad_bias_ref = take()
    grads = [take() for _ in range(parts)]
    if last:
        grad_zero_ref, sums_ref = take(2)
    else:
        back_ref = take()
    weight_ref, out_ref, weight_sem, out_sem = take(4)
    grads_ref, grads_sem = take(2)
    turned_ref, item_ref = take(2)
    if last:
        back_ref = take()
    step = pl.program_id(0)
    rows, wide = normed_ref.shape
    width = weight_ref.shape[3]
    block = cosine_ref.shape[1]
    count = count_ref[0]
    half = half_ref[0]
    copies = [
        slot_copies(weights[at], weight_ref, weight_sem, at, 1, half)
        + slot_copies(outs[at], out_ref, out_sem, at, 0, half)
        for at in range(parts)
    ]
    results = [
        (pltpu.make_async_copy(grads_ref.at[at], grads[at], grads_sem.at[at]),)
        for at in range(parts)
    ]
    start_all(step, copies)

    @pl.when(step == 0)
    def _():
        turned_ref[...] = jnp.transpose(normed_ref[...])
        back_ref[...] = jnp.zeros_like(back_ref) if first else before_ref[...]

    wait_own(step, copies)
    grad_attn = grad_attn_ref[...]
    place = lax.broadcasted_iota(jnp.int32, (rows, width), 0)
    item_ref[...] = jnp.where(place < count, inner_cols(grad_attn, out_ref[step]), 0.0).astype(BF16)
    grads_ref[step, 3 * width :, :] = inner_rows(attended_ref[0], grad_attn).astype(BF16)
    cosine = cosine_ref[...]
    sine = sine_ref[...]
    live = lax.broadcasted_iota(jnp.int32, (rows, 1), 0) < count
    linear = [[], [], []]
    for at in range(width // block):
        cut = slice(at * block, (at + 1) * block)
        keys = key_ref[0, :, cut]
        values = value_ref[0, :, cut]
        keys_turned = jnp.transpose(keys)
        grad_keys = jnp.zeros((rows, block), F32)
        grad_values = jnp.zeros((rows, block), F32)
        grad_queries = [[] for _ in range(rows // SPAN)]
        for head in range(block // HD):
            index = at * (block // HD) + head
            for part in range(rows // SPAN):
                here = slice(part * SPAN, (part + 1) * SPAN)
                queries = head_lanes(query_ref[0, here, cut], head)
                items = head_lanes(item_ref[here, cut], head)
                scores = jnp.where(live, inner_cols(keys, queries), -1e30)
                weights = jnp.exp(scores - log_ref[0, index : index + 1, here])
                grad_weights = inner_cols(values, items)
                along = jnp.sum(grad_weights * weights, axis=0, keepdims=True)
                grad_scores = (weights * (grad_weights - along)).astype(BF16)
                grad_values = grad_values + mm(weights.astype(BF16), items)
                grad_keys = grad_keys + mm(grad_scores, queries)
                grad_queries[part].append(
                    mm(keys_turned[head * HD : (head + 1) * HD, :], grad_scores)
                )
        grad_query = jnp.concatenate(
            [jnp.concatenate(grad_queries[part], axis=0) for part in range(rows // SPAN)], axis=1
        )
        grad_query = jnp.transpose(grad_query) * HD**-0.5
        for which, member in enumerate((grad_query, grad_keys)):
            linear[which].append(member * cosine - swap_pairs(member) * sine)
        linear[2].append(grad_values)
    for which in range(3):
        member = jnp.concatenate(linear[which], axis=1) if width > block else linear[which][0]
        grad_bias_ref[0, which : which + 1, :] = jnp.sum(member, axis=0, keepdims=True)
        member = member.astype(BF16)
        lay(grads_ref, step, which * width, mm(turned_ref[...], member).astype(BF16))
        back_ref[...] += inner_cols(member, weight_ref[step, which])

    send_own(step, results)

    if last:

        @pl.when(step == parts - 1)
        def _():
            def chunk(at, carry):
                scale_attn, shift_attn, bias_in = carry
                here = pl.ds(at * CHUNK, CHUNK)
                xhat, root = norm_parts(state_ref[here, :])
                back = back_ref[here, :]
                grad_zero = grad_one_ref[here, :] + norm_pull(back, mod_ref[1:2, :], xhat, root)
                grad_zero_ref[here, :] = grad_zero.astype(BF16)
                return (
                    scale_attn + fold(back * xhat),
                    shift_attn + fold(back),
                    bias_in + fold(grad_zero),
                )

            start = tuple(jnp.zeros((8, wide), F32) for _ in range(3))
            lanes = lax.fori_loop(0, rows // CHUNK, chunk, start)
            for at, member in enumerate(lanes):
                sums_ref[at : at + 1, :] = jnp.sum(member, axis=0, keepdims=True)

    wait_all(step, results)


def total_of(refs):
    total = refs[0][...].astype(F32)
    for ref in refs[1:]:
        total = total + ref[...].astype(F32)
    return total.astype(BF16)


def sum_kernel(count, *refs):
    refs[count][...] = total_of(refs[:count])


def split_kernel(count, parts, *refs):
    own = refs[0][0]
    sums = [total_of(refs[1 + at * count : 1 + (at + 1) * count]) for at in range(parts)]
    for mask, ref in enumerate(refs[1 + parts * count :]):
        value = sums[mask]
        for at in range(1, parts):
            value = jnp.where(own == at, sums[at ^ mask], value)
        ref[...] = value


def merge_kernel(count, starts_ref, *refs):
    bring(starts_ref, refs[:count], refs[count], refs[count + 1])


def bring(starts_ref, pieces, stack_ref, sems):
    size = pieces[0].shape[0]
    copies = []
    for at, piece in enumerate(pieces):
        start = pl.multiple_of(starts_ref[at], 16)
        copies.append(
            pltpu.make_async_copy(piece, stack_ref.at[pl.ds(start, size), :], sems.at[at])
        )
    for copy in copies:
        copy.start()
    for copy in copies:
        copy.wait()


def unlay(target, stack_ref, start, width):
    for block in range(target.shape[0] // width):
        target[block * width : (block + 1) * width, :] = stack_ref[
            start : start + width, block * width : (block + 1) * width
        ].astype(F32)


def ffn_unpack(count, starts_ref, *refs):
    pieces = refs[:count]
    up_ref, down_ref, stack_ref, sems = refs[count:]
    bring(starts_ref, pieces, stack_ref, sems)
    width = up_ref.shape[1]
    unlay(up_ref, stack_ref, 0, width)
    down_ref[...] = stack_ref[width:, :].astype(F32)


def attn_unpack(count, starts_ref, *refs):
    pieces = refs[:count]
    weight_ref, out_ref, stack_ref, sems = refs[count:]
    bring(starts_ref, pieces, stack_ref, sems)
    width = weight_ref.shape[2]
    for which in range(3):
        unlay(weight_ref.at[which], stack_ref, which * width, width)
    out_ref[...] = stack_ref[3 * width :, :].astype(F32)


def gelu_parts(pre):
    share = 0.5 * (1.0 + lax.erf(pre * 0.7071067811865476))
    slope = share + pre * (0.3989422804014327 * jnp.exp(-0.5 * pre * pre))
    return pre * share, slope


def fill_padded(padded_ref, text_ref):
    rows, wide = text_ref.shape
    edge = jnp.zeros((8, wide), F32)
    padded_ref[0:8, :] = edge
    padded_ref[rows + 8 : rows + 16, :] = edge
    for at in range(rows // CHUNK):
        here = slice(at * CHUNK, (at + 1) * CHUNK)
        padded_ref[at * CHUNK + 8 : (at + 1) * CHUNK + 8, :] = text_ref[here, :].astype(F32)


def text_forward(
    text_ref,
    mel_ref,
    kernel_ref,
    bias_ref,
    gain_ref,
    hidden_bias_ref,
    in_ref,
    out_ref,
    project_ref,
    frame_ref,
    normed_ref,
    pre_ref,
    energy_ref,
    mixed_ref,
    refined_ref,
    state_ref,
    padded_ref,
    hidden_ref,
):
    rows, wide = text_ref.shape
    taps = kernel_ref.shape[0]
    fill_padded(padded_ref, text_ref)

    def front(at, carry):
        start = pl.multiple_of(at * CHUNK, CHUNK)
        near = padded_ref[pl.ds(start, CHUNK + 16), :]
        conv = bias_ref[0:1, :]
        for tap in range(taps):
            shift = 8 + tap - taps // 2
            conv = conv + near[shift : shift + CHUNK, :] * kernel_ref[tap : tap + 1, :]
        xhat, _ = norm_parts(conv)
        normed_ref[pl.ds(start, CHUNK), :] = (xhat * gain_ref[...] + bias_ref[1:2, :]).astype(BF16)
        return carry

    lax.fori_loop(0, rows // CHUNK, front, 0)
    pre_ref[...] = mm(normed_ref[...], in_ref[...]) + hidden_bias_ref[0:1, :]

    def gelu(at, carry):
        here = pl.ds(at * CHUNK, CHUNK)
        hidden, _ = gelu_parts(pre_ref[here, :])
        hidden_ref[here, :] = hidden
        return carry + fold(hidden * hidden)

    squares = lax.fori_loop(0, rows // CHUNK, gelu, jnp.zeros((8, pre_ref.shape[1]), F32))
    energy = jnp.sqrt(jnp.sum(squares, axis=0, keepdims=True))
    energy_ref[0:1, :] = energy
    ratio = energy / (jnp.mean(energy, axis=1, keepdims=True) + 1e-06)

    def mix(at, carry):
        here = pl.ds(at * CHUNK, CHUNK)
        hidden = hidden_ref[here, :]
        mixed = hidden_bias_ref[1:2, :] * (hidden * ratio) + hidden_bias_ref[2:3, :] + hidden
        mixed_ref[here, :] = mixed.astype(BF16)
        return carry

    lax.fori_loop(0, rows // CHUNK, mix, 0)
    refined_ref[...] = (
        text_ref[...].astype(F32) + mm(mixed_ref[...], out_ref[...]) + bias_ref[2:3, :]
    ).astype(BF16)
    state_ref[...] = (
        mm(mel_ref[...], project_ref[0 : mel_ref.shape[1], :])
        + mm(refined_ref[...], project_ref[mel_ref.shape[1] :, :])
        + frame_ref[0:1, :]
    )


def full_line(members, wide):
    have = sum(member.shape[1] for member in members)
    return jnp.concatenate(list(members) + [jnp.zeros((1, wide - have), F32)], axis=1)


def small_rows(group):
    count = 12 + 2 * group
    return count + -count % 16


def text_backward(group, *refs):
    refs = list(refs)

    def take(count=1):
        taken = [refs.pop(0) for _ in range(count)]
        return taken[0] if count == 1 else taken

    own_ref, grad_zero_ref, text_ref, mel_ref, refined_ref, mixed_ref, normed_ref = take(7)
    pre_ref, energy_ref, kernel_ref, bias_ref, gain_ref, hidden_bias_ref = take(6)
    in_ref, out_ref, project_ref, attn_sums_ref, ffn_sums_ref = take(5)
    high_bias_ref, low_bias_ref, up_bias_ref, active_ref = take(4)
    grad_text_ref, mods_ref = take(2)
    slots = [take() for _ in range(group)]
    stack_ref, sems, padded_ref, outer_ref, refined_grad_ref, low_ref, mixed_grad_ref = take(7)
    pre_low_ref, normed_grad_ref, lines_ref = take(3)
    small = small_rows(group)
    own = own_ref[0]
    rows, wide = text_ref.shape
    model = grad_zero_ref.shape[1]
    taps = kernel_ref.shape[0]
    mel_at = 3 * wide
    small_at = mel_at + mel_ref.shape[1] + (-(mel_at + mel_ref.shape[1])) % 16

    lines = [attn_sums_ref[1:2, :], attn_sums_ref[0:1, :]]
    lines += [ffn_sums_ref[row : row + 1, :] for row in (5, 3, 2, 1)]
    mods_at = small_at + small
    stack_ref[mods_at:, :] = jnp.zeros((stack_ref.shape[0] - mods_at, model), BF16)
    for at, member in enumerate(lines):
        mods_ref[at : at + 1, :] = member.astype(BF16)
    lines += [active_ref[...].astype(F32), jnp.zeros((1, model), F32)]
    lines = jnp.concatenate(lines, axis=0)
    empty = jnp.zeros_like(lines)
    odd = own_ref[1] % 2 == 1
    lines = jnp.where(
        odd, jnp.concatenate([empty, lines], axis=0), jnp.concatenate([lines, empty], axis=0)
    )
    place = pl.multiple_of(mods_at + own_ref[1] // 2 * 16, 16)
    stack_ref[pl.ds(place, 16), :] = lines.astype(BF16)

    grad_zero = grad_zero_ref[...]
    grad_refined = inner_cols(grad_zero, project_ref[mel_ref.shape[1] :, :])
    refined_grad_ref[...] = grad_refined
    low_ref[...] = grad_refined.astype(BF16)
    sum_out = jnp.sum(fold(grad_refined), axis=0, keepdims=True)
    mixed_grad_ref[...] = inner_cols(low_ref[...], out_ref[...])
    stack_ref[0:wide, :] = inner_rows(refined_ref[...], grad_zero).astype(BF16)
    spare = jnp.zeros((small_at - mel_at - mel_ref.shape[1], model), F32)
    grad_mel = inner_rows(mel_ref[...], grad_zero)
    stack_ref[mel_at:small_at, :] = jnp.concatenate([grad_mel, spare], axis=0).astype(BF16)
    grad_out = inner_rows(mixed_ref[...], low_ref[...]).astype(BF16)
    stack_ref[2 * wide : 3 * wide, 0:wide] = grad_out[0:wide, :]
    stack_ref[2 * wide : 3 * wide, wide:] = grad_out[wide:, :]

    energy = energy_ref[0:1, :]
    mean = jnp.mean(energy, axis=1, keepdims=True) + 1e-06
    ratio = energy / mean

    def first_pass(at, carry):
        along, plain = carry
        here = pl.ds(at * CHUNK, CHUNK)
        hidden, _ = gelu_parts(pre_ref[here, :])
        grad = mixed_grad_ref[here, :]
        return along + fold(grad * hidden), plain + fold(grad)

    zero = jnp.zeros((8, model), F32)
    along, plain = lax.fori_loop(0, rows // CHUNK, first_pass, (zero, zero))
    along = jnp.sum(along, axis=0, keepdims=True)
    sum_beta = jnp.sum(plain, axis=0, keepdims=True)
    gamma = hidden_bias_ref[1:2, :]
    grad_ratio = gamma * along
    grad_mean = jnp.sum(grad_ratio * energy, axis=1, keepdims=True) / (mean * mean)
    grad_energy = grad_ratio / mean - grad_mean / model
    spread = grad_energy / energy
    factor = 1.0 + gamma * ratio

    def second_pass(at, carry):
        here = pl.ds(at * CHUNK, CHUNK)
        hidden, slope = gelu_parts(pre_ref[here, :])
        grad = (mixed_grad_ref[here, :] * factor + hidden * spread) * slope
        pre_low_ref[here, :] = grad.astype(BF16)
        return carry + fold(grad)

    sum_in = jnp.sum(lax.fori_loop(0, rows // CHUNK, second_pass, zero), axis=0, keepdims=True)
    normed_grad_ref[...] = inner_cols(pre_low_ref[...], in_ref[...])
    stack_ref[wide : 2 * wide, :] = inner_rows(normed_ref[...], pre_low_ref[...]).astype(BF16)

    fill_padded(padded_ref, text_ref)
    edge = jnp.zeros((8, wide), F32)
    outer_ref[0:8, :] = edge
    outer_ref[rows + 8 : rows + 16, :] = edge
    narrow = jnp.zeros((8, wide), F32)
    step = CHUNK // 2

    def conv_back(at, carry):
        sum_gain, sum_norm, sum_conv, sum_taps = carry
        start = pl.multiple_of(at * step, step)
        near = padded_ref[pl.ds(start, step + 16), :]
        conv = bias_ref[0:1, :]
        for tap in range(taps):
            shift = 8 + tap - taps // 2
            conv = conv + near[shift : shift + step, :] * kernel_ref[tap : tap + 1, :]
        xhat, root = norm_parts(conv)
        grad = normed_grad_ref[pl.ds(start, step), :]
        entry = grad * gain_ref[...]
        entry_mean = jnp.mean(entry, axis=-1, keepdims=True)
        entry_along = jnp.mean(entry * xhat, axis=-1, keepdims=True)
        grad_conv = root * (entry - entry_mean - xhat * entry_along)
        outer_ref[pl.ds(start + 8, step), :] = grad_conv
        sum_taps = tuple(
            member
            + fold(grad_conv * near[8 + tap - taps // 2 : 8 + tap - taps // 2 + step, :])
            for tap, member in enumerate(sum_taps)
        )
        return (
            sum_gain + fold(grad * xhat),
            sum_norm + fold(grad),
            sum_conv + fold(grad_conv),
            sum_taps,
        )

    sum_gain, sum_norm, sum_conv, sum_taps = lax.fori_loop(
        0, rows // step, conv_back, (narrow, narrow, narrow, (narrow,) * taps)
    )

    def text_grad(at, carry):
        start = pl.multiple_of(at * CHUNK, CHUNK)
        near = outer_ref[pl.ds(start, CHUNK + 16), :]
        total = refined_grad_ref[pl.ds(start, CHUNK), :]
        for tap in range(taps):
            shift = 8 + taps // 2 - tap
            total = total + near[shift : shift + CHUNK, :] * kernel_ref[tap : tap + 1, :]
        grad_text_ref[pl.ds(start, CHUNK), :] = total
        return carry

    lax.fori_loop(0, rows // CHUNK, text_grad, 0)

    def line(member):
        return jnp.sum(member, axis=0, keepdims=True)

    halves = [line(member) for member in sum_taps] + [line(sum_gain)]
    halves += [line(sum_conv), line(sum_norm), sum_out, jnp.zeros((1, wide), F32)]
    lines = [
        jnp.concatenate(halves[at : at + 2], axis=1) for at in range(0, len(halves), 2)
    ]
    lines += [sum_in, ratio * along, sum_beta]
    lines += [attn_sums_ref[2:3, :], ffn_sums_ref[4:5, :], ffn_sums_ref[0:1, :]]
    lines_ref[...] = jnp.zeros_like(lines_ref)
    for at, member in enumerate(lines):
        lines_ref[at : at + 1, :] = member
    parts = group // 2
    row = lax.broadcasted_iota(jnp.int32, lines_ref.shape, 0)
    total = lines_ref[...]
    for slot in range(group):
        source_ref = low_bias_ref if slot < parts else high_bias_ref
        owner = jnp.bitwise_xor(own, slot)
        members = [source_ref[slot % parts, which : which + 1, :] for which in range(3)]
        total = jnp.where(row == 12 + owner, full_line(members, model), total)
        total = jnp.where(row == 12 + group + owner, full_line([up_bias_ref[slot]], model), total)
    lines_ref[...] = total
    stack_ref[small_at : small_at + small, :] = lines_ref[...].astype(BF16)

    size = stack_ref.shape[0] // group
    copies = []
    for slot in range(group):
        start = pl.multiple_of(jnp.bitwise_xor(own, slot) * size, size)
        copies.append(
            pltpu.make_async_copy(stack_ref.at[pl.ds(start, size), :], slots[slot], sems.at[slot])
        )
    for copy in copies:
        copy.start()
    for copy in copies:
        copy.wait()


def text_unpack(count, group, starts_ref, own_ref, *refs):
    pieces = refs[:count]
    project_ref, in_ref, out_ref, taps_ref, bias_ref, gain_ref = refs[count : count + 6]
    hidden_ref, frame_ref, qkv_bias_ref, up_bias_ref, mods_ref = refs[count + 6 : count + 11]
    stack_ref, sems, lines_ref = refs[count + 11 :]
    bring(starts_ref, pieces, stack_ref, sems)
    own = own_ref[0]
    wide = in_ref.shape[0]
    taps = taps_ref.shape[0]
    mels = project_ref.shape[0] - wide
    mel_at = 3 * wide
    small_at = mel_at + mels + (-(mel_at + mels)) % 16
    project_ref[0:mels, :] = stack_ref[mel_at : mel_at + mels, :].astype(F32)
    project_ref[mels:, :] = stack_ref[0:wide, :].astype(F32)
    in_ref[...] = stack_ref[wide : 2 * wide, :].astype(F32)
    out_ref[0:wide, :] = stack_ref[2 * wide : 3 * wide, 0:wide].astype(F32)
    out_ref[wide:, :] = stack_ref[2 * wide : 3 * wide, wide:].astype(F32)
    lines_ref[...] = stack_ref[small_at : small_at + small_rows(group), :].astype(F32)
    mods_at = small_at + small_rows(group)
    mods_ref[...] = stack_ref[mods_at : mods_at + mods_ref.shape[0], :]

    def half(at):
        return lines_ref[at // 2 : at // 2 + 1, (at % 2) * wide : (at % 2 + 1) * wide]

    for tap in range(taps):
        taps_ref[tap : tap + 1, :] = half(tap)
    gain_ref[...] = half(taps)
    for at in range(3):
        bias_ref[at : at + 1, :] = half(taps + 1 + at)
    first = (taps + 5) // 2
    hidden_ref[...] = lines_ref[first : first + 3, :]
    frame_ref[...] = lines_ref[first + 3 : first + 6, :]
    row = lax.broadcasted_iota(jnp.int32, lines_ref.shape, 0)

    def pick(at):
        return jnp.sum(jnp.where(row == at, lines_ref[...], 0.0), axis=0, keepdims=True)

    line = pick(12 + own)
    width = qkv_bias_ref.shape[1]
    for which in range(3):
        qkv_bias_ref[which : which + 1, :] = line[:, which * width : (which + 1) * width]
    up_bias_ref[...] = pick(12 + group + own)[:, 0 : up_bias_ref.shape[1]]


ANY = pl.BlockSpec(memory_space=pl.ANY)
SMEM = pl.BlockSpec(memory_space=pltpu.SMEM)


def whole(shape):
    return pl.BlockSpec(shape, lambda g: (0,) * len(shape))


def held(shape, parts=None):
    if parts is None:
        return pl.BlockSpec((1,) + shape, lambda g: (g,) + (0,) * len(shape))
    return pl.BlockSpec((1,) + shape, lambda g: (parts - 1 - g,) + (0,) * len(shape))


def run_kernel(kernel, parts, inputs, outputs, scratch):
    return pl.pallas_call(
        kernel,
        grid=(parts,),
        in_specs=[spec for spec, _ in inputs],
        out_specs=[spec for spec, _, _ in outputs],
        out_shape=[jax.ShapeDtypeStruct(shape, kind) for _, shape, kind in outputs],
        scratch_shapes=scratch,
        compiler_params=pltpu.CompilerParams(vmem_limit_bytes=VMEM),
        cost_estimate=pl.CostEstimate(flops=1024, bytes_accessed=1024, transcendentals=0),
    )(*[array for _, array in inputs])


def after(arrays, *others):
    arrays = tuple(arrays)
    return lax.optimization_barrier(arrays + others)[: len(arrays)]


def swap(array, axis, bit):
    return lax.ppermute(array, axis, [(at, at ^ bit) for at in range(lax.axis_size(axis))])


def low_bit(slot):
    return slot & -slot


def tile_rows(rows):
    return next(size for size in (256, 224, 128, 112, 96, 80, 64, 48, 32, 16) if rows % size == 0)


def add_arrays(arrays):
    rows, wide = arrays[0].shape
    tile = tile_rows(rows)
    spec = pl.BlockSpec((tile, wide), lambda g: (g, 0))
    return run_kernel(
        partial(sum_kernel, len(arrays)),
        rows // tile,
        [(spec, array) for array in arrays],
        [(spec, (rows, wide), BF16)],
        [],
    )[0]


def add_and_split(arrays, own, parts):
    rows, wide = arrays[0].shape
    size = rows // parts
    tile = tile_rows(size)
    steps = size // tile

    def block_at(part):
        return pl.BlockSpec((tile, wide), lambda g: (g + part * steps, 0))

    return run_kernel(
        partial(split_kernel, len(arrays), parts),
        steps,
        [(SMEM, own.astype(jnp.int32).reshape(1))]
        + [(block_at(part), array) for part in range(parts) for array in arrays],
        [(block_at(0), (size, wide), BF16)] * parts,
        [],
    )


def merge(pieces, starts, rows):
    return run_kernel(
        partial(merge_kernel, len(pieces)),
        1,
        [(SMEM, jnp.stack(starts).astype(jnp.int32))] + [(ANY, piece) for piece in pieces],
        [(whole((rows, pieces[0].shape[1])), (rows, pieces[0].shape[1]), BF16)],
        [pltpu.SemaphoreType.DMA((len(pieces),))],
    )[0]


class Fetch:
    def __init__(self, array, axis):
        size = array.shape[axis] // 2
        start = lax.axis_index("dp") % 2 * size
        self.half = lax.dynamic_slice_in_dim(array, start, size, axis=axis)
        self.group = lax.axis_size("heads")
        self.slots = {0: [array]}
        self.sent = {}

    def core(self, slot, *others):
        pieces = after(self.slots[slot], *others)
        self.slots[slot + 1] = [swap(piece, "heads", 1) for piece in pieces]

    def send(self, *others):
        (self.half,) = after([self.half], *others)
        for slot in range(2, self.group, 2):
            bit = low_bit(slot)
            if slot == bit:
                self.sent[slot] = swap(self.half, "heads", bit)

    def share(self, *others):
        for slot in range(2, self.group, 2):
            bit = low_bit(slot)
            if slot == bit:
                (came,) = after([self.sent[slot]], *others)
            else:
                came = swap(self.slots[slot - bit][0], "heads", bit)
            self.slots[slot] = [came, swap(came, "dp", 1)]

    def cores(self, first, last, *others):
        for slot in range(first, last, 2):
            self.core(slot, *others)

    def listed(self):
        return [self.slots[slot] for slot in range(self.group)]


def flat(slots):
    return [piece for pieces in slots for piece in pieces]


class GroupSum:
    def __init__(self):
        self.arrived = {}

    def put(self, slot, array, *others):
        arrays = [array] + self.arrived.pop(slot, [])
        if slot == 0:
            return arrays
        total = add_arrays(after(arrays, *others)) if len(arrays) > 1 else array
        bit = low_bit(slot)
        self.arrived.setdefault(slot - bit, []).append(swap(total, "heads", bit))
        return total


class DataSum:
    def __init__(self, arrays, bits, merged=False):
        self.merged = merged
        self.arrays = list(arrays)
        self.bits = list(bits)
        self.halved = []
        self.rows = arrays[0].shape[0]
        self.pieces = None

    def step(self, *others):
        arrays = after(self.arrays, *others)
        if not self.bits:
            total = add_arrays(arrays)
            self.gather(total)
            return total
        bit = self.bits.pop(0)
        keep, send = add_and_split(arrays, lax.axis_index("dp") // bit % 2, 2)
        self.halved.append(bit)
        self.arrays = [keep, swap(send, "dp", bit)]
        return keep

    def gather(self, total):
        self.pieces = {0: total}
        for bit in self.halved[: 0 if self.merged else None : -1]:
            for mask, piece in list(self.pieces.items()):
                self.pieces[mask | bit] = swap(piece, "dp", bit)

    def half(self, *others):
        starts = [start % (self.rows // 2) for start in self.starts()]
        return merge(after(self.pieces.values(), *others), starts, self.rows // 2)

    def starts(self):
        own = lax.axis_index("dp")
        return [
            sum(
                (own ^ mask) // bit % 2 * (self.rows >> (at + 1))
                for at, bit in enumerate(self.halved)
            )
            for mask in self.pieces
        ]


def axis_bits(axis):
    size = lax.axis_size(axis)
    return [1 << at for at in range(size.bit_length() - 1)]


def on_device(
    noisy_mel,
    cond_mel,
    text_embed,
    time_embed,
    lengths,
    spans,
    dw_kernel,
    text_bias,
    text_gain,
    text_hidden,
    pw_in,
    pw_out,
    in_proj,
    frame_bias,
    mod_weight,
    mod_bias,
    qkv_weight,
    qkv_bias,
    out_weight,
    ff_in,
    ff_in_bias,
    ff_out,
    cotangent,
):
    group = lax.axis_size("heads")
    own = lax.axis_index("heads")
    own_data = lax.axis_index("dp")
    rows = text_embed.shape[0]
    model_width = in_proj.shape[1]
    width = qkv_weight.shape[2]
    units = ff_in.shape[1]
    block = min(128, width)
    parts = group // 2
    full = (rows, model_width)

    fetches = [Fetch(qkv_weight, 1), Fetch(out_weight, 0), Fetch(ff_in, 0), Fetch(ff_out, 0)]
    for fetch in fetches[:2]:
        fetch.send()
        fetch.core(0)

    position = jnp.arange(rows, dtype=jnp.int32)
    inside = (position >= spans[0, 0]) & (position < spans[0, 1])
    keep = jnp.where(inside, 0.0, 1.0).astype(F32)[:, None]
    count = lax.dynamic_slice_in_dim(lengths, own, 1)
    lane = jnp.arange(block, dtype=jnp.int32)
    pair = ((lane % HD) // 2).astype(F32)
    angle = position.astype(F32)[:, None] * (10000.0 ** (-2.0 * pair / HD))[None, :]
    cosine = jnp.cos(angle)
    sine = jnp.sin(angle) * jnp.where(lane % 2 == 0, -1.0, 1.0)[None, :]

    cond_low = (cond_mel.astype(F32) * keep).astype(BF16)
    mel = jnp.concatenate([noisy_mel, cond_low], axis=1)
    mels = mel.shape[1]
    text_width = text_embed.shape[1]
    gain = text_gain[None, :]

    def block_of(array):
        return (whole(array.shape), array)

    normed_text, pre_act, energy, mixed_text, refined, state_zero = run_kernel(
        text_forward,
        1,
        [
            block_of(member)
            for member in (
                text_embed,
                mel,
                dw_kernel,
                text_bias,
                gain,
                text_hidden,
                pw_in,
                pw_out,
                in_proj,
                frame_bias,
            )
        ],
        [
            (whole(shape), shape, kind)
            for shape, kind in (
                ((rows, text_width), BF16),
                ((rows, pw_in.shape[1]), F32),
                ((8, pw_in.shape[1]), F32),
                ((rows, pw_in.shape[1]), BF16),
                ((rows, text_width), BF16),
                (full, F32),
            )
        ],
        [pltpu.VMEM((rows + 16, text_width), F32), pltpu.VMEM((rows, pw_in.shape[1]), F32)],
    )

    def semaphores(number, pieces=2):
        shape = (number, pieces) if pieces > 1 else (number,)
        return pltpu.SemaphoreType.DMA(shape)

    def attn_buffers(number, pieces=2):
        return [
            pltpu.VMEM((number, 3, model_width, width), BF16),
            pltpu.VMEM((number, width, model_width), BF16),
            semaphores(number, pieces),
            semaphores(number, pieces),
        ]

    def ffn_buffers(number, pieces=2):
        return [
            pltpu.VMEM((number, model_width, units), BF16),
            pltpu.VMEM((number, units, model_width), BF16),
            semaphores(number, pieces),
            semaphores(number, pieces),
        ]

    half_index = (own_data % 2).astype(jnp.int32).reshape(1)

    def pieces_of(slots):
        return tuple(len(pieces) for pieces in slots)

    (time_late,) = after([time_embed], state_zero)
    time_rows = time_late.astype(F32)
    activated, silu_back = jax.vjp(jax.nn.silu, time_rows)
    activated_low = activated.astype(BF16)
    modulation = (mm(activated_low, mod_weight) + mod_bias).astype(BF16)
    biases = jnp.concatenate([qkv_bias.reshape(-1), ff_in_bias])
    riders = jnp.broadcast_to(biases[None, :], (group, biases.size))
    sent = jnp.concatenate([modulation, riders], axis=1)
    came = lax.all_to_all(sent, "heads", split_axis=0, concat_axis=1, tiled=True)
    came = came.reshape(group, sent.shape[1]).astype(F32)
    mod_rows = came[:, : modulation.shape[1]].reshape(6, model_width)
    slot_owner = jnp.bitwise_xor(jnp.arange(group, dtype=jnp.int32), own)
    biases_all = jnp.take(came[:, modulation.shape[1] :], slot_owner, axis=0)
    qkv_bias_all = biases_all[:, : 3 * width].reshape(group, 3, width)
    up_bias_all = biases_all[:, 3 * width :].reshape(group, 1, units)

    for fetch in fetches[2:]:
        fetch.send(came)
    for fetch in fetches[:2]:
        fetch.share()
        fetch.cores(2, parts)
    (mod_rows,) = after([mod_rows], *[fetch.sent[2] for fetch in fetches[:2]])
    kept = []
    for turn in range(2):
        first, last = turn == 0, turn == 1
        if last:
            for fetch in fetches[:2]:
                fetch.cores(parts, group, normed)
            for fetch in fetches[2:]:
                fetch.share(normed)
                fetch.core(0, normed)
            (before,) = after([before], *[fetch.slots[2][0] for fetch in fetches[2:]])
        chosen = range(turn * parts, (turn + 1) * parts)
        qkv_here = [fetches[0].slots[slot] for slot in chosen]
        out_here = [fetches[1].slots[slot] for slot in chosen]
        inputs = [
            (SMEM, count),
            (SMEM, half_index),
            (whole(full), state_zero),
            (whole((6, model_width)), mod_rows),
            (held((3, width)), qkv_bias_all[chosen[0] : chosen[-1] + 1]),
            (whole((3, model_width)), frame_bias),
            (whole((rows, block)), cosine),
            (whole((rows, block)), sine),
        ]
        inputs += [(ANY, member) for member in flat(qkv_here) + flat(out_here)]
        if not first:
            inputs += [(whole(full), normed), (whole(full), before)]
        outputs = [(held((rows, width)), (parts, rows, width), BF16)] * 4
        outputs += [(held((8, rows)), (parts, 8, rows), F32)]
        if first:
            outputs += [(whole(full), full, BF16)]
        outputs += [(whole(full), full, F32)]
        if last:
            outputs += [(whole(full), full, F32), (whole(full), full, BF16)]
        results = run_kernel(
            partial(attention_forward, pieces_of(qkv_here), first, last),
            parts,
            inputs,
            outputs,
            attn_buffers(parts) + ([pltpu.VMEM(full, F32)] if last else []),
        )
        kept.append(results[:5])
        if first:
            normed, before = results[5:]
        else:
            branch, state_one, ffn_in = results[5:]

    qkv_all, out_all = fetches[0].listed(), fetches[1].listed()
    fetches[2].cores(2, group, ffn_in)
    fetches[3].cores(2, group, ffn_in)
    up_all, down_all = fetches[2].listed()[::-1], fetches[3].listed()[::-1]
    inputs = [
        (SMEM, half_index),
        (whole(full), cotangent),
        (whole(full), state_one),
        (whole(full), branch),
        (whole(full), ffn_in),
        (whole((6, model_width)), mod_rows),
        (held((1, units), group), up_bias_all),
        (whole((3, model_width)), frame_bias),
    ]
    inputs += [(ANY, member) for member in flat(up_all) + flat(down_all)]
    merged = (2 * units, model_width)
    outputs = [(held((1, units), group), (group, 1, units), F32)]
    outputs += [(whole((8, model_width)), (8, model_width), F32)]
    outputs += [(ANY, merged, BF16)] * group
    outputs += [(whole(full), full, BF16)] * 2 + [(whole(full), full, F32)]
    outputs += [(whole(full), full, BF16)]
    results = run_kernel(
        partial(feed_forward, pieces_of(up_all), True, True),
        group,
        inputs,
        outputs,
        [
            pltpu.VMEM((group, model_width, units), BF16),
            pltpu.VMEM((group, units, model_width), BF16),
            semaphores(group),
            semaphores(group),
            pltpu.VMEM((group,) + merged, BF16),
            semaphores(group, 1),
            pltpu.VMEM((model_width, rows), BF16),
            pltpu.VMEM((rows, units), BF16),
            pltpu.VMEM((rows, units), BF16),
        ]
        + [pltpu.VMEM(full, F32)] * 2,
    )
    grad_up_bias, ffn_sums = results[:2]
    output, grad_one, grad_attn = results[3 + group :]
    ffn_grads = results[2 : 2 + group][::-1]

    attn_grads = []
    merged = (4 * width, model_width)
    qkv_bias_parts = []
    for turn in range(2):
        first, last = turn == 0, turn == 1
        chosen = [group - 1 - turn * parts - at for at in range(parts)]
        inputs = [
            (SMEM, count),
            (SMEM, half_index),
            (whole(full), grad_attn),
            (whole(full), normed),
            (whole((6, model_width)), mod_rows),
            (whole((rows, block)), cosine),
            (whole((rows, block)), sine),
        ]
        inputs += [(held((rows, width), parts), member) for member in kept[1 - turn][:4]]
        inputs += [(held((8, rows), parts), kept[1 - turn][4])]
        inputs += [(ANY, member) for member in flat([qkv_all[slot] for slot in chosen])]
        inputs += [(ANY, member) for member in flat([out_all[slot] for slot in chosen])]
        if not first:
            inputs += [(whole(full), back)]
        if last:
            inputs += [(whole(full), state_zero), (whole(full), grad_one)]
        outputs = [(held((3, width), parts), (parts, 3, width), F32)]
        outputs += [(ANY, merged, BF16)] * parts
        if last:
            outputs += [(whole(full), full, BF16), (whole((8, model_width)), (8, model_width), F32)]
        else:
            outputs += [(whole(full), full, F32)]
        results = run_kernel(
            partial(attention_backward, pieces_of([qkv_all[slot] for slot in chosen]), first, last),
            parts,
            inputs,
            outputs,
            attn_buffers(parts)
            + [pltpu.VMEM((parts,) + merged, BF16), semaphores(parts, 1)]
            + [pltpu.VMEM((model_width, rows), BF16), pltpu.VMEM((rows, width), BF16)]
            + ([pltpu.VMEM(full, F32)] if last else []),
        )
        qkv_bias_parts.append(results[0])
        attn_grads = list(results[1 : 1 + parts])[::-1] + attn_grads
        if first:
            back = results[1 + parts]
            ffn_sum = GroupSum()
            token = back
            for slot in range(group - 1, 0, -1):
                total = ffn_sum.put(slot, ffn_grads[slot], token)
                if slot % 2 == 0:
                    token = total
            (back,) = after([back], token)
        else:
            grad_zero, attn_sums = results[1 + parts :]
    token = grad_zero
    attn_sum = GroupSum()
    for slot in range(group - 1, 0, -1):
        total = attn_sum.put(slot, attn_grads[slot], token)
        if slot % 2 == 0:
            token = total
    (grad_zero,) = after([grad_zero], token)

    data = lax.axis_size("dp")
    stack_rows = 3 * text_width + mels
    stack_rows += -stack_rows % 16 + small_rows(group) + 8 * group * data
    stack_rows += -stack_rows % (16 * group * data)
    own_index = jnp.stack([own, own_data * group + own]).astype(jnp.int32)
    own_active = lax.dynamic_index_in_dim(activated_low, own, 0)
    results = run_kernel(
        partial(text_backward, group),
        1,
        [(SMEM, own_index)]
        + [
            block_of(member)
            for member in (
                grad_zero,
                text_embed,
                mel,
                refined,
                mixed_text,
                normed_text,
                pre_act,
                energy,
                dw_kernel,
                text_bias,
                gain,
                text_hidden,
                pw_in,
                pw_out,
                in_proj,
                attn_sums,
                ffn_sums,
                qkv_bias_parts[0],
                qkv_bias_parts[1],
                grad_up_bias,
                own_active,
            )
        ],
        [
            (whole((rows, text_width)), (rows, text_width), F32),
            (whole((6, model_width)), (6, model_width), BF16),
        ]
        + [(ANY, (stack_rows // group, model_width), BF16)] * group,
        [
            pltpu.VMEM((stack_rows, model_width), BF16),
            semaphores(group, 1),
            pltpu.VMEM((rows + 16, text_width), F32),
            pltpu.VMEM((rows + 16, text_width), F32),
            pltpu.VMEM((rows, text_width), F32),
            pltpu.VMEM((rows, text_width), BF16),
            pltpu.VMEM((rows, pw_in.shape[1]), F32),
            pltpu.VMEM((rows, pw_in.shape[1]), BF16),
            pltpu.VMEM((rows, text_width), F32),
            pltpu.VMEM((small_rows(group), model_width), F32),
        ],
    )
    grad_text, grad_mod = results[:2]
    def unpack(kernel, data, first, second, *others):
        pieces = after(data.pieces.values(), *others)
        return run_kernel(
            partial(kernel, len(pieces)),
            1,
            [(SMEM, jnp.stack(data.starts()).astype(jnp.int32))]
            + [(ANY, member) for member in pieces],
            [(whole(first.shape), first.shape, F32), (whole(second.shape), second.shape, F32)],
            [pltpu.VMEM((data.rows, model_width), BF16), semaphores(len(pieces), 1)],
        )

    bits = axis_bits("dp")
    ffn_data = DataSum(ffn_sum.put(0, ffn_grads[0]), bits)
    token = ffn_data.step(grad_mod)
    text_sum = GroupSum()
    for slot in range(group - 1, 0, -1):
        total = text_sum.put(slot, results[2 + slot], token)
        if slot % 2 == 0:
            token = total
    attn_data = DataSum(attn_sum.put(0, attn_grads[0]), bits)
    text_data = DataSum(text_sum.put(0, results[2]), bits, merged=True)
    steps = [(at, ffn_data) for at in range(1, len(bits) + 1)]
    for at in range(len(bits) + 1):
        steps.append((at + 2.2 if at else 1.5, attn_data))
        steps.append((at + 2.25, text_data))
    for at, member in sorted(steps, key=lambda step: step[0]):
        token = member.step(token)

    weight_up, weight_down = unpack(ffn_unpack, ffn_data, ff_in, ff_out, attn_data.pieces[0])
    text_half = text_data.half(weight_up, *list(attn_data.pieces.values())[1:])
    weight_qkv, weight_out = unpack(attn_unpack, attn_data, qkv_weight, out_weight, text_half)
    text_halves = {0: [text_half]}
    for slot in range(2, group, 2):
        bit = low_bit(slot)
        text_halves[slot] = [swap(text_halves[slot - bit][0], "heads", bit)]
    for slot in range(0, group, 2):
        text_halves[slot].append(swap(text_halves[slot][0], "dp", 1))
        text_halves[slot + 1] = [swap(piece, "heads", 1) for piece in text_halves[slot]]
    (grad_mod,) = after([grad_mod], text_halves[2][0])
    columns = mod_weight.shape[1]
    grad_mod = grad_mod.reshape(1, group * columns)
    grad_mod_cols = lax.all_to_all(grad_mod, "heads", split_axis=1, concat_axis=0, tiled=True)
    (grad_time,) = silu_back(inner_cols(grad_mod_cols, mod_weight))
    grad_time = jnp.broadcast_to(grad_time.astype(BF16), (group,) + grad_time.shape)
    grad_time = lax.all_to_all(grad_time, "heads", split_axis=0, concat_axis=0)
    grad_time = jnp.sum(grad_time.astype(F32), axis=0)

    slot_rows = stack_rows // group
    text_pieces, text_starts = [], []
    for slot, pieces in text_halves.items():
        for which, piece in enumerate(pieces):
            text_pieces.append(piece)
            text_starts.append(
                slot_owner[slot] * slot_rows + ((own_data + which) % 2) * (slot_rows // 2)
            )
    unpacked = (
        in_proj.shape,
        pw_in.shape,
        pw_out.shape,
        dw_kernel.shape,
        text_bias.shape,
        gain.shape,
        text_hidden.shape,
        frame_bias.shape,
        (3, width),
        (1, units),
    )
    mods_shape = (8 * group * data, model_width)
    unpacked = run_kernel(
        partial(text_unpack, len(text_pieces), group),
        1,
        [(SMEM, jnp.stack(text_starts).astype(jnp.int32)), (SMEM, own_index)]
        + [(ANY, member) for member in text_pieces],
        [(whole(shape), shape, F32) for shape in unpacked]
        + [(whole(mods_shape), mods_shape, BF16)],
        [
            pltpu.VMEM((stack_rows, model_width), BF16),
            semaphores(len(text_pieces), 1),
            pltpu.VMEM((small_rows(group), model_width), F32),
        ],
    )
    seen = unpacked[10].reshape(group * data, 8, model_width)
    grad_mod_all = seen[:, :6].reshape(group * data, 6 * model_width)
    grad_mod_all = lax.dynamic_slice_in_dim(grad_mod_all, own * columns, columns, axis=1)
    grad_mod_weight = inner_rows(seen[:, 6], grad_mod_all)
    grad_mod_bias = jnp.sum(grad_mod_all.astype(F32), axis=0)
    return (
        output,
        grad_text,
        grad_time,
        unpacked[3],
        unpacked[4],
        unpacked[5][0],
        unpacked[6],
        unpacked[1],
        unpacked[2],
        unpacked[0],
        unpacked[7],
        grad_mod_weight,
        grad_mod_bias,
        weight_qkv,
        unpacked[8],
        weight_out,
        weight_up,
        unpacked[9][0],
        weight_down,
    )


def solution(mesh):
    in_specs = (
        P(("dp", "heads"), None),
        P(("dp", "heads"), None),
        P(("dp", "heads"), None),
        P("dp", None),
        P("dp"),
        P(("dp", "heads"), None),
        P(),
        P(),
        P(),
        P(),
        P(),
        P(),
        P(),
        P(),
        P(None, "heads"),
        P("heads"),
        P(None, None, "heads"),
        P(None, "heads"),
        P("heads", None),
        P(None, "heads"),
        P("heads"),
        P("heads", None),
        P(("dp", "heads"), None),
    )
    out_specs = (
        P(("dp", "heads"), None),
        P(("dp", "heads"), None),
        P("dp", None),
        P(),
        P(),
        P(),
        P(),
        P(),
        P(),
        P(),
        P(),
        P(None, "heads"),
        P("heads"),
        P(None, None, "heads"),
        P(None, "heads"),
        P("heads", None),
        P(None, "heads"),
        P("heads"),
        P("heads", None),
    )
    return jax.shard_map(
        on_device, mesh=mesh, in_specs=in_specs, out_specs=out_specs, check_vma=False
    )
```

```python
from functools import partial

import jax
import jax.numpy as jnp
from jax import lax
from jax.experimental import pallas as pl
from jax.experimental.pallas import tpu as pltpu
from jax.sharding import PartitionSpec as P

HD = 64


def inner_rows(left, right):
    return lax.dot_general(
        left, right, (((0,), (0,)), ((), ())), preferred_element_type=jnp.float32
    )


def inner_cols(left, right):
    return lax.dot_general(
        left, right, (((1,), (1,)), ((), ())), preferred_element_type=jnp.float32
    )


F32 = jnp.float32
BF16 = jnp.bfloat16
CHUNK = 64
SPAN = 256
VMEM = 60 * 1024 * 1024


def mm(left, right):
    return jnp.dot(left, right, preferred_element_type=F32)


def fold(values):
    return jnp.sum(values.reshape(values.shape[0] // 8, 8, values.shape[1]), axis=0)


def norm_parts(values):
    mean = jnp.mean(values, axis=-1, keepdims=True)
    centred = values - mean
    root = lax.rsqrt(jnp.mean(centred * centred, axis=-1, keepdims=True) + 1e-06)
    return centred * root, root


def norm_pull(grad, scale, xhat, root):
    entry = grad * (1.0 + scale)
    mean = jnp.mean(entry, axis=-1, keepdims=True)
    along = jnp.mean(entry * xhat, axis=-1, keepdims=True)
    return root * (entry - mean - xhat * along)


def swap_pairs(block):
    width = block.shape[1]
    lane = lax.broadcasted_iota(jnp.int32, block.shape, 1)
    if width % 128 == 0:
        after = pltpu.roll(block, width - 1, 1)
        before = pltpu.roll(block, 1, 1)
    else:
        after = jnp.concatenate([block[:, 1:], block[:, :1]], axis=1)
        before = jnp.concatenate([block[:, width - 1 :], block[:, : width - 1]], axis=1)
    return jnp.where(lane % 2 == 0, after, before)


def head_lanes(block, head):
    if block.shape[1] == HD:
        return block
    lane = lax.broadcasted_iota(jnp.int32, block.shape, 1)
    return jnp.where((lane >= head * HD) & (lane < (head + 1) * HD), block, jnp.zeros_like(block))


def slot_copies(pieces, target, sems, at, axis, half):
    if len(pieces) == 1:
        return [pltpu.make_async_copy(pieces[0], target.at[at], sems.at[at, 0])]
    copies = []
    for which, piece in enumerate(pieces):
        size = piece.shape[axis]
        start = pl.multiple_of((half if which == 0 else 1 - half) * size, size)
        index = (at,) + (slice(None),) * axis + (pl.ds(start, size),)
        copies.append(pltpu.make_async_copy(piece, target.at[index], sems.at[at, which]))
    return copies


def start_all(step, copies):
    @pl.when(step == 0)
    def _():
        for members in copies:
            for copy in members:
                copy.start()


def wait_own(step, copies):
    for at, members in enumerate(copies):

        @pl.when(step == at)
        def _(members=members):
            for copy in members:
                copy.wait()


def send_own(step, results):
    for at, members in enumerate(results):

        @pl.when(step == at)
        def _(members=members):
            for copy in members:
                copy.start()


def wait_all(step, results):
    @pl.when(step == len(results) - 1)
    def _():
        for members in results:
            for copy in members:
                copy.wait()


def attention_forward(pieces, first, last, *refs):
    parts = len(pieces)
    refs = list(refs)

    def take(count=1):
        taken = [refs.pop(0) for _ in range(count)]
        return taken[0] if count == 1 else taken

    count_ref, half_ref, state_ref, mod_ref, bias_ref, frame_ref, cosine_ref, sine_ref = take(8)
    weights = [[take() for _ in range(number)] for number in pieces]
    outs = [[take() for _ in range(number)] for number in pieces]
    if not first:
        normed_ref, before_ref = take(2)
    query_ref, key_ref, value_ref, attended_ref, log_ref = take(5)
    if first:
        normed_ref = take()
    if last:
        branch_ref, one_ref, ffn_ref = take(3)
    else:
        total_ref = take()
    weight_ref, out_ref, weight_sem, out_sem = take(4)
    if last:
        total_ref = take()
    step = pl.program_id(0)
    rows = state_ref.shape[0]
    width = weight_ref.shape[3]
    block = cosine_ref.shape[1]
    count = count_ref[0]
    half = half_ref[0]
    copies = [
        slot_copies(weights[at], weight_ref, weight_sem, at, 1, half)
        + slot_copies(outs[at], out_ref, out_sem, at, 0, half)
        for at in range(parts)
    ]
    start_all(step, copies)

    @pl.when(step == 0)
    def _():
        if first:

            def chunk(at, carry):
                here = pl.ds(at * CHUNK, CHUNK)
                xhat, _ = norm_parts(state_ref[here, :])
                normed_ref[here, :] = (xhat * (1.0 + mod_ref[1:2, :]) + mod_ref[0:1, :]).astype(
                    BF16
                )
                return carry

            lax.fori_loop(0, rows // CHUNK, chunk, 0)
            total_ref[...] = jnp.zeros_like(total_ref)
        else:
            total_ref[...] = before_ref[...]

    wait_own(step, copies)
    normed = normed_ref[...]
    cosine = cosine_ref[...]
    sine = sine_ref[...]
    logs = jnp.zeros((rows, 128), F32)
    lane = lax.broadcasted_iota(jnp.int32, (rows, 128), 1)
    query_lin = mm(normed, weight_ref[step, 0]) + bias_ref[0, 0:1, :]
    key_lin = mm(normed, weight_ref[step, 1]) + bias_ref[0, 1:2, :]
    value_ref[0] = (mm(normed, weight_ref[step, 2]) + bias_ref[0, 2:3, :]).astype(BF16)
    for at in range(width // block):
        cut = slice(at * block, (at + 1) * block)
        piece = query_lin[:, cut]
        turned = piece * cosine + swap_pairs(piece) * sine
        query_ref[0, :, cut] = (turned * HD**-0.5).astype(BF16)
        piece = key_lin[:, cut]
        key_ref[0, :, cut] = (piece * cosine + swap_pairs(piece) * sine).astype(BF16)
    live = lax.broadcasted_iota(jnp.int32, (1, rows), 1) < count
    for at in range(width // block):
        cut = slice(at * block, (at + 1) * block)
        keys = key_ref[0, :, cut]
        values = value_ref[0, :, cut]
        results = [None] * (rows // SPAN)
        pieces = [[] for _ in range(rows // SPAN)]
        for head in range(block // HD):
            own_values = head_lanes(values, head)
            for part in range(rows // SPAN):
                queries = head_lanes(query_ref[0, part * SPAN : (part + 1) * SPAN, cut], head)
                scores = jnp.where(live, inner_cols(queries, keys), -1e30)
                top = jnp.max(scores, axis=1, keepdims=True)
                expo = jnp.exp(scores - top)
                total = jnp.sum(expo, axis=1, keepdims=True)
                weights = (expo * (1.0 / total)).astype(BF16)
                result = mm(weights, own_values)
                results[part] = result if head == 0 else results[part] + result
                pieces[part].append(top + jnp.log(total))
        for head in range(block // HD):
            column = jnp.concatenate([pieces[part][head] for part in range(rows // SPAN)], axis=0)
            logs = jnp.where(lane == at * (block // HD) + head, column, logs)
        for part in range(rows // SPAN):
            place = part * SPAN + lax.broadcasted_iota(jnp.int32, (SPAN, block), 0)
            attended_ref[0, part * SPAN : (part + 1) * SPAN, cut] = jnp.where(
                place < count, results[part], 0.0
            ).astype(BF16)
    log_ref[0] = jnp.transpose(logs)[0:8, :]
    total_ref[...] += mm(attended_ref[0], out_ref[step])

    if last:

        @pl.when(step == parts - 1)
        def _():
            def chunk(at, carry):
                here = pl.ds(at * CHUNK, CHUNK)
                branch = total_ref[here, :] + frame_ref[1:2, :]
                branch_ref[here, :] = branch
                state_one = state_ref[here, :] + mod_ref[2:3, :] * branch
                one_ref[here, :] = state_one
                xhat, _ = norm_parts(state_one)
                ffn_ref[here, :] = (xhat * (1.0 + mod_ref[4:5, :]) + mod_ref[3:4, :]).astype(BF16)
                return carry

            lax.fori_loop(0, rows // CHUNK, chunk, 0)


def lay(target_ref, at, start, value):
    model, width = value.shape
    for block in range(model // width):
        target_ref[at, start : start + width, block * width : (block + 1) * width] = value[
            block * width : (block + 1) * width, :
        ]


def feed_forward(pieces, first, last, *refs):
    parts = len(pieces)
    refs = list(refs)

    def take(count=1):
        taken = [refs.pop(0) for _ in range(count)]
        return taken[0] if count == 1 else taken

    half_ref, cotangent_ref, one_ref, branch_ref, source_ref, mod_ref, bias_ref, frame_ref = take(8)
    ups = [[take() for _ in range(number)] for number in pieces]
    downs = [[take() for _ in range(number)] for number in pieces]
    if not first:
        grad_ref, total_in_ref, back_in_ref = take(3)
    grad_bias_ref, sums_ref = take(2)
    grads = [take() for _ in range(parts)]
    if first:
        grad_ref = take()
    if last:
        output_ref, grad_one_ref, grad_attn_ref = take(3)
    else:
        total_ref, back_ref = take(2)
    up_ref, down_ref, up_sem, down_sem = take(4)
    grads_ref, grads_sem = take(2)
    turned_ref, hidden_ref, pre_ref = take(3)
    if last:
        total_ref, back_ref = take(2)
    step = pl.program_id(0)
    rows, wide = one_ref.shape
    inner = 0.7978845608028654
    cubic = 0.044715
    half = half_ref[0]
    copies = [
        slot_copies(ups[at], up_ref, up_sem, at, 0, half)
        + slot_copies(downs[at], down_ref, down_sem, at, 0, half)
        for at in range(parts)
    ]
    results = [
        (pltpu.make_async_copy(grads_ref.at[at], grads[at], grads_sem.at[at]),)
        for at in range(parts)
    ]
    start_all(step, copies)

    @pl.when(step == 0)
    def _():
        if first:

            def chunk(at, carry):
                here = pl.ds(at * CHUNK, CHUNK)
                grad = cotangent_ref[here, :].astype(F32) * mod_ref[5:6, :]
                grad_ref[here, :] = grad.astype(BF16)
                return carry + fold(grad)

            lanes = lax.fori_loop(0, rows // CHUNK, chunk, jnp.zeros((8, wide), F32))
            sums_ref[0:1, :] = jnp.sum(lanes, axis=0, keepdims=True)
            total_ref[...] = jnp.zeros_like(total_ref)
            back_ref[...] = jnp.zeros_like(back_ref)
        else:
            total_ref[...] = total_in_ref[...]
            back_ref[...] = back_in_ref[...]
        turned_ref[...] = jnp.transpose(source_ref[...])

    wait_own(step, copies)
    up = up_ref[step]
    down = down_ref[step]
    lanes = jnp.zeros((8, up.shape[1]), F32)
    for part in range(rows // SPAN):
        here = slice(part * SPAN, (part + 1) * SPAN)
        pre = mm(source_ref[here, :], up) + bias_ref[0]
        grad_hidden = inner_cols(grad_ref[here, :], down)
        square = pre * pre
        bend = jnp.tanh(pre * (inner + inner * cubic * square))
        half = 0.5 * (1.0 + bend)
        hidden = (pre * half).astype(BF16)
        slope = half + 0.5 * pre * (1.0 - bend * bend) * (inner + 3.0 * inner * cubic * square)
        grad_pre = grad_hidden * slope
        lanes = lanes + fold(grad_pre)
        grad_pre = grad_pre.astype(BF16)
        hidden_ref[here, :] = hidden
        pre_ref[here, :] = grad_pre
        total_ref[here, :] += mm(hidden, down)
        back_ref[here, :] += inner_cols(grad_pre, up)
    grad_bias_ref[0] = jnp.sum(lanes, axis=0, keepdims=True)
    width = up_ref.shape[2]
    grads_ref[step, width:, :] = inner_rows(hidden_ref[...], grad_ref[...]).astype(BF16)
    lay(grads_ref, step, 0, mm(turned_ref[...], pre_ref[...]).astype(BF16))
    send_own(step, results)

    if last:

        @pl.when(step == parts - 1)
        def _():
            def chunk(at, carry):
                gate_ffn, scale_ffn, shift_ffn, bias_attn, gate_attn = carry
                here = pl.ds(at * CHUNK, CHUNK)
                branch = total_ref[here, :] + frame_ref[2:3, :]
                state_one = one_ref[here, :]
                output_ref[here, :] = (state_one + mod_ref[5:6, :] * branch).astype(BF16)
                cotangent = cotangent_ref[here, :].astype(F32)
                xhat, root = norm_parts(state_one)
                back = back_ref[here, :]
                grad_one = cotangent + norm_pull(back, mod_ref[4:5, :], xhat, root)
                grad_one_ref[here, :] = grad_one
                grad_attn = grad_one * mod_ref[2:3, :]
                grad_attn_ref[here, :] = grad_attn.astype(BF16)
                return (
                    gate_ffn + fold(cotangent * branch),
                    scale_ffn + fold(back * xhat),
                    shift_ffn + fold(back),
                    bias_attn + fold(grad_attn),
                    gate_attn + fold(grad_one * branch_ref[here, :]),
                )

            start = tuple(jnp.zeros((8, wide), F32) for _ in range(5))
            lanes = lax.fori_loop(0, rows // CHUNK, chunk, start)
            for at, member in enumerate(lanes):
                sums_ref[at + 1 : at + 2, :] = jnp.sum(member, axis=0, keepdims=True)

    wait_all(step, results)


def attention_backward(pieces, first, last, *refs):
    parts = len(pieces)
    refs = list(refs)

    def take(count=1):
        taken = [refs.pop(0) for _ in range(count)]
        return taken[0] if count == 1 else taken

    count_ref, half_ref, grad_attn_ref, normed_ref, mod_ref, cosine_ref, sine_ref = take(7)
    query_ref, key_ref, value_ref, attended_ref, log_ref = take(5)
    weights = [[take() for _ in range(number)] for number in pieces]
    outs = [[take() for _ in range(number)] for number in pieces]
    if not first:
        before_ref = take()
    if last:
        state_ref, grad_one_ref = take(2)
    grad_bias_ref = take()
    grads = [take() for _ in range(parts)]
    if last:
        grad_zero_ref, sums_ref = take(2)
    else:
        back_ref = take()
    weight_ref, out_ref, weight_sem, out_sem = take(4)
    grads_ref, grads_sem = take(2)
    turned_ref, item_ref = take(2)
    if last:
        back_ref = take()
    step = pl.program_id(0)
    rows, wide = normed_ref.shape
    width = weight_ref.shape[3]
    block = cosine_ref.shape[1]
    count = count_ref[0]
    half = half_ref[0]
    copies = [
        slot_copies(weights[at], weight_ref, weight_sem, at, 1, half)
        + slot_copies(outs[at], out_ref, out_sem, at, 0, half)
        for at in range(parts)
    ]
    results = [
        (pltpu.make_async_copy(grads_ref.at[at], grads[at], grads_sem.at[at]),)
        for at in range(parts)
    ]
    start_all(step, copies)

    @pl.when(step == 0)
    def _():
        turned_ref[...] = jnp.transpose(normed_ref[...])
        back_ref[...] = jnp.zeros_like(back_ref) if first else before_ref[...]

    wait_own(step, copies)
    grad_attn = grad_attn_ref[...]
    place = lax.broadcasted_iota(jnp.int32, (rows, width), 0)
    item_ref[...] = jnp.where(place < count, inner_cols(grad_attn, out_ref[step]), 0.0).astype(BF16)
    grads_ref[step, 3 * width :, :] = inner_rows(attended_ref[0], grad_attn).astype(BF16)
    cosine = cosine_ref[...]
    sine = sine_ref[...]
    live = lax.broadcasted_iota(jnp.int32, (rows, 1), 0) < count
    linear = [[], [], []]
    for at in range(width // block):
        cut = slice(at * block, (at + 1) * block)
        keys = key_ref[0, :, cut]
        values = value_ref[0, :, cut]
        keys_turned = jnp.transpose(keys)
        grad_keys = jnp.zeros((rows, block), F32)
        grad_values = jnp.zeros((rows, block), F32)
        grad_queries = [[] for _ in range(rows // SPAN)]
        for head in range(block // HD):
            index = at * (block // HD) + head
            for part in range(rows // SPAN):
                here = slice(part * SPAN, (part + 1) * SPAN)
                queries = head_lanes(query_ref[0, here, cut], head)
                items = head_lanes(item_ref[here, cut], head)
                scores = jnp.where(live, inner_cols(keys, queries), -1e30)
                weights = jnp.exp(scores - log_ref[0, index : index + 1, here])
                grad_weights = inner_cols(values, items)
                along = jnp.sum(grad_weights * weights, axis=0, keepdims=True)
                grad_scores = (weights * (grad_weights - along)).astype(BF16)
                grad_values = grad_values + mm(weights.astype(BF16), items)
                grad_keys = grad_keys + mm(grad_scores, queries)
                grad_queries[part].append(
                    mm(keys_turned[head * HD : (head + 1) * HD, :], grad_scores)
                )
        grad_query = jnp.concatenate(
            [jnp.concatenate(grad_queries[part], axis=0) for part in range(rows // SPAN)], axis=1
        )
        grad_query = jnp.transpose(grad_query) * HD**-0.5
        for which, member in enumerate((grad_query, grad_keys)):
            linear[which].append(member * cosine - swap_pairs(member) * sine)
        linear[2].append(grad_values)
    for which in range(3):
        member = jnp.concatenate(linear[which], axis=1) if width > block else linear[which][0]
        grad_bias_ref[0, which : which + 1, :] = jnp.sum(member, axis=0, keepdims=True)
        member = member.astype(BF16)
        lay(grads_ref, step, which * width, mm(turned_ref[...], member).astype(BF16))
        back_ref[...] += inner_cols(member, weight_ref[step, which])

    send_own(step, results)

    if last:

        @pl.when(step == parts - 1)
        def _():
            def chunk(at, carry):
                scale_attn, shift_attn, bias_in = carry
                here = pl.ds(at * CHUNK, CHUNK)
                xhat, root = norm_parts(state_ref[here, :])
                back = back_ref[here, :]
                grad_zero = grad_one_ref[here, :] + norm_pull(back, mod_ref[1:2, :], xhat, root)
                grad_zero_ref[here, :] = grad_zero.astype(BF16)
                return (
                    scale_attn + fold(back * xhat),
                    shift_attn + fold(back),
                    bias_in + fold(grad_zero),
                )

            start = tuple(jnp.zeros((8, wide), F32) for _ in range(3))
            lanes = lax.fori_loop(0, rows // CHUNK, chunk, start)
            for at, member in enumerate(lanes):
                sums_ref[at : at + 1, :] = jnp.sum(member, axis=0, keepdims=True)

    wait_all(step, results)


def total_of(refs):
    total = refs[0][...].astype(F32)
    for ref in refs[1:]:
        total = total + ref[...].astype(F32)
    return total.astype(BF16)


def sum_kernel(count, *refs):
    refs[count][...] = total_of(refs[:count])


def split_kernel(count, parts, *refs):
    own = refs[0][0]
    sums = [total_of(refs[1 + at * count : 1 + (at + 1) * count]) for at in range(parts)]
    for mask, ref in enumerate(refs[1 + parts * count :]):
        value = sums[mask]
        for at in range(1, parts):
            value = jnp.where(own == at, sums[at ^ mask], value)
        ref[...] = value


def merge_kernel(count, starts_ref, *refs):
    bring(starts_ref, refs[:count], refs[count], refs[count + 1])


def bring(starts_ref, pieces, stack_ref, sems):
    size = pieces[0].shape[0]
    copies = []
    for at, piece in enumerate(pieces):
        start = pl.multiple_of(starts_ref[at], 16)
        copies.append(
            pltpu.make_async_copy(piece, stack_ref.at[pl.ds(start, size), :], sems.at[at])
        )
    for copy in copies:
        copy.start()
    for copy in copies:
        copy.wait()


def unlay(target, stack_ref, start, width):
    for block in range(target.shape[0] // width):
        target[block * width : (block + 1) * width, :] = stack_ref[
            start : start + width, block * width : (block + 1) * width
        ].astype(F32)


def ffn_unpack(count, starts_ref, *refs):
    pieces = refs[:count]
    up_ref, down_ref, stack_ref, sems = refs[count:]
    bring(starts_ref, pieces, stack_ref, sems)
    width = up_ref.shape[1]
    unlay(up_ref, stack_ref, 0, width)
    down_ref[...] = stack_ref[width:, :].astype(F32)


def attn_unpack(count, starts_ref, *refs):
    pieces = refs[:count]
    weight_ref, out_ref, stack_ref, sems = refs[count:]
    bring(starts_ref, pieces, stack_ref, sems)
    width = weight_ref.shape[2]
    for which in range(3):
        unlay(weight_ref.at[which], stack_ref, which * width, width)
    out_ref[...] = stack_ref[3 * width :, :].astype(F32)


def gelu_parts(pre):
    share = 0.5 * (1.0 + lax.erf(pre * 0.7071067811865476))
    slope = share + pre * (0.3989422804014327 * jnp.exp(-0.5 * pre * pre))
    return pre * share, slope


def fill_padded(padded_ref, text_ref):
    rows, wide = text_ref.shape
    edge = jnp.zeros((8, wide), F32)
    padded_ref[0:8, :] = edge
    padded_ref[rows + 8 : rows + 16, :] = edge
    for at in range(rows // CHUNK):
        here = slice(at * CHUNK, (at + 1) * CHUNK)
        padded_ref[at * CHUNK + 8 : (at + 1) * CHUNK + 8, :] = text_ref[here, :].astype(F32)


def text_forward(
    text_ref,
    mel_ref,
    kernel_ref,
    bias_ref,
    gain_ref,
    hidden_bias_ref,
    in_ref,
    out_ref,
    project_ref,
    frame_ref,
    normed_ref,
    pre_ref,
    energy_ref,
    mixed_ref,
    refined_ref,
    state_ref,
    padded_ref,
    hidden_ref,
):
    rows, wide = text_ref.shape
    taps = kernel_ref.shape[0]
    fill_padded(padded_ref, text_ref)

    def front(at, carry):
        start = pl.multiple_of(at * CHUNK, CHUNK)
        near = padded_ref[pl.ds(start, CHUNK + 16), :]
        conv = bias_ref[0:1, :]
        for tap in range(taps):
            shift = 8 + tap - taps // 2
            conv = conv + near[shift : shift + CHUNK, :] * kernel_ref[tap : tap + 1, :]
        xhat, _ = norm_parts(conv)
        normed_ref[pl.ds(start, CHUNK), :] = (xhat * gain_ref[...] + bias_ref[1:2, :]).astype(BF16)
        return carry

    lax.fori_loop(0, rows // CHUNK, front, 0)
    pre_ref[...] = mm(normed_ref[...], in_ref[...]) + hidden_bias_ref[0:1, :]

    def gelu(at, carry):
        here = pl.ds(at * CHUNK, CHUNK)
        hidden, _ = gelu_parts(pre_ref[here, :])
        hidden_ref[here, :] = hidden
        return carry + fold(hidden * hidden)

    squares = lax.fori_loop(0, rows // CHUNK, gelu, jnp.zeros((8, pre_ref.shape[1]), F32))
    energy = jnp.sqrt(jnp.sum(squares, axis=0, keepdims=True))
    energy_ref[0:1, :] = energy
    ratio = energy / (jnp.mean(energy, axis=1, keepdims=True) + 1e-06)

    def mix(at, carry):
        here = pl.ds(at * CHUNK, CHUNK)
        hidden = hidden_ref[here, :]
        mixed = hidden_bias_ref[1:2, :] * (hidden * ratio) + hidden_bias_ref[2:3, :] + hidden
        mixed_ref[here, :] = mixed.astype(BF16)
        return carry

    lax.fori_loop(0, rows // CHUNK, mix, 0)
    refined_ref[...] = (
        text_ref[...].astype(F32) + mm(mixed_ref[...], out_ref[...]) + bias_ref[2:3, :]
    ).astype(BF16)
    state_ref[...] = (
        mm(mel_ref[...], project_ref[0 : mel_ref.shape[1], :])
        + mm(refined_ref[...], project_ref[mel_ref.shape[1] :, :])
        + frame_ref[0:1, :]
    )


def full_line(members, wide):
    have = sum(member.shape[1] for member in members)
    return jnp.concatenate(list(members) + [jnp.zeros((1, wide - have), F32)], axis=1)


def small_rows(group):
    count = 12 + 2 * group
    return count + -count % 16


def text_backward(group, *refs):
    refs = list(refs)

    def take(count=1):
        taken = [refs.pop(0) for _ in range(count)]
        return taken[0] if count == 1 else taken

    own_ref, grad_zero_ref, text_ref, mel_ref, refined_ref, mixed_ref, normed_ref = take(7)
    pre_ref, energy_ref, kernel_ref, bias_ref, gain_ref, hidden_bias_ref = take(6)
    in_ref, out_ref, project_ref, attn_sums_ref, ffn_sums_ref = take(5)
    high_bias_ref, low_bias_ref, up_bias_ref, active_ref = take(4)
    grad_text_ref, mods_ref = take(2)
    slots = [take() for _ in range(group)]
    stack_ref, sems, padded_ref, outer_ref, refined_grad_ref, low_ref, mixed_grad_ref = take(7)
    pre_low_ref, normed_grad_ref, lines_ref = take(3)
    small = small_rows(group)
    own = own_ref[0]
    rows, wide = text_ref.shape
    model = grad_zero_ref.shape[1]
    taps = kernel_ref.shape[0]
    mel_at = 3 * wide
    small_at = mel_at + mel_ref.shape[1] + (-(mel_at + mel_ref.shape[1])) % 16

    lines = [attn_sums_ref[1:2, :], attn_sums_ref[0:1, :]]
    lines += [ffn_sums_ref[row : row + 1, :] for row in (5, 3, 2, 1)]
    mods_at = small_at + small
    stack_ref[mods_at:, :] = jnp.zeros((stack_ref.shape[0] - mods_at, model), BF16)
    for at, member in enumerate(lines):
        mods_ref[at : at + 1, :] = member.astype(BF16)
    lines += [active_ref[...].astype(F32), jnp.zeros((1, model), F32)]
    lines = jnp.concatenate(lines, axis=0)
    empty = jnp.zeros_like(lines)
    odd = own_ref[1] % 2 == 1
    lines = jnp.where(
        odd, jnp.concatenate([empty, lines], axis=0), jnp.concatenate([lines, empty], axis=0)
    )
    place = pl.multiple_of(mods_at + own_ref[1] // 2 * 16, 16)
    stack_ref[pl.ds(place, 16), :] = lines.astype(BF16)

    grad_zero = grad_zero_ref[...]
    grad_refined = inner_cols(grad_zero, project_ref[mel_ref.shape[1] :, :])
    refined_grad_ref[...] = grad_refined
    low_ref[...] = grad_refined.astype(BF16)
    sum_out = jnp.sum(fold(grad_refined), axis=0, keepdims=True)
    mixed_grad_ref[...] = inner_cols(low_ref[...], out_ref[...])
    stack_ref[0:wide, :] = inner_rows(refined_ref[...], grad_zero).astype(BF16)
    spare = jnp.zeros((small_at - mel_at - mel_ref.shape[1], model), F32)
    grad_mel = inner_rows(mel_ref[...], grad_zero)
    stack_ref[mel_at:small_at, :] = jnp.concatenate([grad_mel, spare], axis=0).astype(BF16)
    grad_out = inner_rows(mixed_ref[...], low_ref[...]).astype(BF16)
    stack_ref[2 * wide : 3 * wide, 0:wide] = grad_out[0:wide, :]
    stack_ref[2 * wide : 3 * wide, wide:] = grad_out[wide:, :]

    energy = energy_ref[0:1, :]
    mean = jnp.mean(energy, axis=1, keepdims=True) + 1e-06
    ratio = energy / mean

    def first_pass(at, carry):
        along, plain = carry
        here = pl.ds(at * CHUNK, CHUNK)
        hidden, _ = gelu_parts(pre_ref[here, :])
        grad = mixed_grad_ref[here, :]
        return along + fold(grad * hidden), plain + fold(grad)

    zero = jnp.zeros((8, model), F32)
    along, plain = lax.fori_loop(0, rows // CHUNK, first_pass, (zero, zero))
    along = jnp.sum(along, axis=0, keepdims=True)
    sum_beta = jnp.sum(plain, axis=0, keepdims=True)
    gamma = hidden_bias_ref[1:2, :]
    grad_ratio = gamma * along
    grad_mean = jnp.sum(grad_ratio * energy, axis=1, keepdims=True) / (mean * mean)
    grad_energy = grad_ratio / mean - grad_mean / model
    spread = grad_energy / energy
    factor = 1.0 + gamma * ratio

    def second_pass(at, carry):
        here = pl.ds(at * CHUNK, CHUNK)
        hidden, slope = gelu_parts(pre_ref[here, :])
        grad = (mixed_grad_ref[here, :] * factor + hidden * spread) * slope
        pre_low_ref[here, :] = grad.astype(BF16)
        return carry + fold(grad)

    sum_in = jnp.sum(lax.fori_loop(0, rows // CHUNK, second_pass, zero), axis=0, keepdims=True)
    normed_grad_ref[...] = inner_cols(pre_low_ref[...], in_ref[...])
    stack_ref[wide : 2 * wide, :] = inner_rows(normed_ref[...], pre_low_ref[...]).astype(BF16)

    fill_padded(padded_ref, text_ref)
    edge = jnp.zeros((8, wide), F32)
    outer_ref[0:8, :] = edge
    outer_ref[rows + 8 : rows + 16, :] = edge
    narrow = jnp.zeros((8, wide), F32)
    step = CHUNK // 2

    def conv_back(at, carry):
        sum_gain, sum_norm, sum_conv, sum_taps = carry
        start = pl.multiple_of(at * step, step)
        near = padded_ref[pl.ds(start, step + 16), :]
        conv = bias_ref[0:1, :]
        for tap in range(taps):
            shift = 8 + tap - taps // 2
            conv = conv + near[shift : shift + step, :] * kernel_ref[tap : tap + 1, :]
        xhat, root = norm_parts(conv)
        grad = normed_grad_ref[pl.ds(start, step), :]
        entry = grad * gain_ref[...]
        entry_mean = jnp.mean(entry, axis=-1, keepdims=True)
        entry_along = jnp.mean(entry * xhat, axis=-1, keepdims=True)
        grad_conv = root * (entry - entry_mean - xhat * entry_along)
        outer_ref[pl.ds(start + 8, step), :] = grad_conv
        sum_taps = tuple(
            member
            + fold(grad_conv * near[8 + tap - taps // 2 : 8 + tap - taps // 2 + step, :])
            for tap, member in enumerate(sum_taps)
        )
        return (
            sum_gain + fold(grad * xhat),
            sum_norm + fold(grad),
            sum_conv + fold(grad_conv),
            sum_taps,
        )

    sum_gain, sum_norm, sum_conv, sum_taps = lax.fori_loop(
        0, rows // step, conv_back, (narrow, narrow, narrow, (narrow,) * taps)
    )

    def text_grad(at, carry):
        start = pl.multiple_of(at * CHUNK, CHUNK)
        near = outer_ref[pl.ds(start, CHUNK + 16), :]
        total = refined_grad_ref[pl.ds(start, CHUNK), :]
        for tap in range(taps):
            shift = 8 + taps // 2 - tap
            total = total + near[shift : shift + CHUNK, :] * kernel_ref[tap : tap + 1, :]
        grad_text_ref[pl.ds(start, CHUNK), :] = total
        return carry

    lax.fori_loop(0, rows // CHUNK, text_grad, 0)

    def line(member):
        return jnp.sum(member, axis=0, keepdims=True)

    halves = [line(member) for member in sum_taps] + [line(sum_gain)]
    halves += [line(sum_conv), line(sum_norm), sum_out, jnp.zeros((1, wide), F32)]
    lines = [
        jnp.concatenate(halves[at : at + 2], axis=1) for at in range(0, len(halves), 2)
    ]
    lines += [sum_in, ratio * along, sum_beta]
    lines += [attn_sums_ref[2:3, :], ffn_sums_ref[4:5, :], ffn_sums_ref[0:1, :]]
    lines_ref[...] = jnp.zeros_like(lines_ref)
    for at, member in enumerate(lines):
        lines_ref[at : at + 1, :] = member
    parts = group // 2
    row = lax.broadcasted_iota(jnp.int32, lines_ref.shape, 0)
    total = lines_ref[...]
    for slot in range(group):
        source_ref = low_bias_ref if slot < parts else high_bias_ref
        owner = jnp.bitwise_xor(own, slot)
        members = [source_ref[slot % parts, which : which + 1, :] for which in range(3)]
        total = jnp.where(row == 12 + owner, full_line(members, model), total)
        total = jnp.where(row == 12 + group + owner, full_line([up_bias_ref[slot]], model), total)
    lines_ref[...] = total
    stack_ref[small_at : small_at + small, :] = lines_ref[...].astype(BF16)

    size = stack_ref.shape[0] // group
    copies = []
    for slot in range(group):
        start = pl.multiple_of(jnp.bitwise_xor(own, slot) * size, size)
        copies.append(
            pltpu.make_async_copy(stack_ref.at[pl.ds(start, size), :], slots[slot], sems.at[slot])
        )
    for copy in copies:
        copy.start()
    for copy in copies:
        copy.wait()


def text_unpack(count, group, starts_ref, own_ref, *refs):
    pieces = refs[:count]
    project_ref, in_ref, out_ref, taps_ref, bias_ref, gain_ref = refs[count : count + 6]
    hidden_ref, frame_ref, qkv_bias_ref, up_bias_ref, mods_ref = refs[count + 6 : count + 11]
    stack_ref, sems, lines_ref = refs[count + 11 :]
    bring(starts_ref, pieces, stack_ref, sems)
    own = own_ref[0]
    wide = in_ref.shape[0]
    taps = taps_ref.shape[0]
    mels = project_ref.shape[0] - wide
    mel_at = 3 * wide
    small_at = mel_at + mels + (-(mel_at + mels)) % 16
    project_ref[0:mels, :] = stack_ref[mel_at : mel_at + mels, :].astype(F32)
    project_ref[mels:, :] = stack_ref[0:wide, :].astype(F32)
    in_ref[...] = stack_ref[wide : 2 * wide, :].astype(F32)
    out_ref[0:wide, :] = stack_ref[2 * wide : 3 * wide, 0:wide].astype(F32)
    out_ref[wide:, :] = stack_ref[2 * wide : 3 * wide, wide:].astype(F32)
    lines_ref[...] = stack_ref[small_at : small_at + small_rows(group), :].astype(F32)
    mods_at = small_at + small_rows(group)
    mods_ref[...] = stack_ref[mods_at : mods_at + mods_ref.shape[0], :]

    def half(at):
        return lines_ref[at // 2 : at // 2 + 1, (at % 2) * wide : (at % 2 + 1) * wide]

    for tap in range(taps):
        taps_ref[tap : tap + 1, :] = half(tap)
    gain_ref[...] = half(taps)
    for at in range(3):
        bias_ref[at : at + 1, :] = half(taps + 1 + at)
    first = (taps + 5) // 2
    hidden_ref[...] = lines_ref[first : first + 3, :]
    frame_ref[...] = lines_ref[first + 3 : first + 6, :]
    row = lax.broadcasted_iota(jnp.int32, lines_ref.shape, 0)

    def pick(at):
        return jnp.sum(jnp.where(row == at, lines_ref[...], 0.0), axis=0, keepdims=True)

    line = pick(12 + own)
    width = qkv_bias_ref.shape[1]
    for which in range(3):
        qkv_bias_ref[which : which + 1, :] = line[:, which * width : (which + 1) * width]
    up_bias_ref[...] = pick(12 + group + own)[:, 0 : up_bias_ref.shape[1]]


ANY = pl.BlockSpec(memory_space=pl.ANY)
SMEM = pl.BlockSpec(memory_space=pltpu.SMEM)


def whole(shape):
    return pl.BlockSpec(shape, lambda g: (0,) * len(shape))


def held(shape, parts=None):
    if parts is None:
        return pl.BlockSpec((1,) + shape, lambda g: (g,) + (0,) * len(shape))
    return pl.BlockSpec((1,) + shape, lambda g: (parts - 1 - g,) + (0,) * len(shape))


def run_kernel(kernel, parts, inputs, outputs, scratch):
    return pl.pallas_call(
        kernel,
        grid=(parts,),
        in_specs=[spec for spec, _ in inputs],
        out_specs=[spec for spec, _, _ in outputs],
        out_shape=[jax.ShapeDtypeStruct(shape, kind) for _, shape, kind in outputs],
        scratch_shapes=scratch,
        compiler_params=pltpu.CompilerParams(vmem_limit_bytes=VMEM),
        cost_estimate=pl.CostEstimate(flops=1024, bytes_accessed=1024, transcendentals=0),
    )(*[array for _, array in inputs])


def after(arrays, *others):
    arrays = tuple(arrays)
    return lax.optimization_barrier(arrays + others)[: len(arrays)]


def swap(array, axis, bit):
    return lax.ppermute(array, axis, [(at, at ^ bit) for at in range(lax.axis_size(axis))])


def low_bit(slot):
    return slot & -slot


def tile_rows(rows):
    return next(size for size in (256, 224, 128, 112, 96, 80, 64, 48, 32, 16) if rows % size == 0)


def add_arrays(arrays):
    rows, wide = arrays[0].shape
    tile = tile_rows(rows)
    spec = pl.BlockSpec((tile, wide), lambda g: (g, 0))
    return run_kernel(
        partial(sum_kernel, len(arrays)),
        rows // tile,
        [(spec, array) for array in arrays],
        [(spec, (rows, wide), BF16)],
        [],
    )[0]


def add_and_split(arrays, own, parts):
    rows, wide = arrays[0].shape
    size = rows // parts
    tile = tile_rows(size)
    steps = size // tile

    def block_at(part):
        return pl.BlockSpec((tile, wide), lambda g: (g + part * steps, 0))

    return run_kernel(
        partial(split_kernel, len(arrays), parts),
        steps,
        [(SMEM, own.astype(jnp.int32).reshape(1))]
        + [(block_at(part), array) for part in range(parts) for array in arrays],
        [(block_at(0), (size, wide), BF16)] * parts,
        [],
    )


def merge(pieces, starts, rows):
    return run_kernel(
        partial(merge_kernel, len(pieces)),
        1,
        [(SMEM, jnp.stack(starts).astype(jnp.int32))] + [(ANY, piece) for piece in pieces],
        [(whole((rows, pieces[0].shape[1])), (rows, pieces[0].shape[1]), BF16)],
        [pltpu.SemaphoreType.DMA((len(pieces),))],
    )[0]


class Fetch:
    def __init__(self, array, axis):
        size = array.shape[axis] // 2
        start = lax.axis_index("dp") % 2 * size
        self.half = lax.dynamic_slice_in_dim(array, start, size, axis=axis)
        self.group = lax.axis_size("heads")
        self.slots = {0: [array]}
        self.sent = {}

    def core(self, slot, *others):
        pieces = after(self.slots[slot], *others)
        self.slots[slot + 1] = [swap(piece, "heads", 1) for piece in pieces]

    def send(self, *others):
        (self.half,) = after([self.half], *others)
        for slot in range(2, self.group, 2):
            bit = low_bit(slot)
            if slot == bit:
                self.sent[slot] = swap(self.half, "heads", bit)

    def share(self, *others):
        for slot in range(2, self.group, 2):
            bit = low_bit(slot)
            if slot == bit:
                (came,) = after([self.sent[slot]], *others)
            else:
                came = swap(self.slots[slot - bit][0], "heads", bit)
            self.slots[slot] = [came, swap(came, "dp", 1)]

    def cores(self, first, last, *others):
        for slot in range(first, last, 2):
            self.core(slot, *others)

    def listed(self):
        return [self.slots[slot] for slot in range(self.group)]


def flat(slots):
    return [piece for pieces in slots for piece in pieces]


class GroupSum:
    def __init__(self):
        self.arrived = {}

    def put(self, slot, array, *others):
        arrays = [array] + self.arrived.pop(slot, [])
        if slot == 0:
            return arrays
        total = add_arrays(after(arrays, *others)) if len(arrays) > 1 else array
        bit = low_bit(slot)
        self.arrived.setdefault(slot - bit, []).append(swap(total, "heads", bit))
        return total


class DataSum:
    def __init__(self, arrays, bits, merged=False):
        self.merged = merged
        self.arrays = list(arrays)
        self.bits = list(bits)
        self.halved = []
        self.rows = arrays[0].shape[0]
        self.pieces = None

    def step(self, *others):
        arrays = after(self.arrays, *others)
        if not self.bits:
            total = add_arrays(arrays)
            self.gather(total)
            return total
        bit = self.bits.pop(0)
        keep, send = add_and_split(arrays, lax.axis_index("dp") // bit % 2, 2)
        self.halved.append(bit)
        self.arrays = [keep, swap(send, "dp", bit)]
        return keep

    def gather(self, total):
        self.pieces = {0: total}
        for bit in self.halved[: 0 if self.merged else None : -1]:
            for mask, piece in list(self.pieces.items()):
                self.pieces[mask | bit] = swap(piece, "dp", bit)

    def half(self, *others):
        starts = [start % (self.rows // 2) for start in self.starts()]
        return merge(after(self.pieces.values(), *others), starts, self.rows // 2)

    def starts(self):
        own = lax.axis_index("dp")
        return [
            sum(
                (own ^ mask) // bit % 2 * (self.rows >> (at + 1))
                for at, bit in enumerate(self.halved)
            )
            for mask in self.pieces
        ]


def axis_bits(axis):
    size = lax.axis_size(axis)
    return [1 << at for at in range(size.bit_length() - 1)]


def on_device(
    noisy_mel,
    cond_mel,
    text_embed,
    time_embed,
    lengths,
    spans,
    dw_kernel,
    text_bias,
    text_gain,
    text_hidden,
    pw_in,
    pw_out,
    in_proj,
    frame_bias,
    mod_weight,
    mod_bias,
    qkv_weight,
    qkv_bias,
    out_weight,
    ff_in,
    ff_in_bias,
    ff_out,
    cotangent,
):
    group = lax.axis_size("heads")
    own = lax.axis_index("heads")
    own_data = lax.axis_index("dp")
    rows = text_embed.shape[0]
    model_width = in_proj.shape[1]
    width = qkv_weight.shape[2]
    units = ff_in.shape[1]
    block = min(128, width)
    parts = group // 2
    full = (rows, model_width)

    fetches = [Fetch(qkv_weight, 1), Fetch(out_weight, 0), Fetch(ff_in, 0), Fetch(ff_out, 0)]
    for fetch in fetches[:2]:
        fetch.send()
        fetch.core(0)

    position = jnp.arange(rows, dtype=jnp.int32)
    inside = (position >= spans[0, 0]) & (position < spans[0, 1])
    keep = jnp.where(inside, 0.0, 1.0).astype(F32)[:, None]
    count = lax.dynamic_slice_in_dim(lengths, own, 1)
    lane = jnp.arange(block, dtype=jnp.int32)
    pair = ((lane % HD) // 2).astype(F32)
    angle = position.astype(F32)[:, None] * (10000.0 ** (-2.0 * pair / HD))[None, :]
    cosine = jnp.cos(angle)
    sine = jnp.sin(angle) * jnp.where(lane % 2 == 0, -1.0, 1.0)[None, :]

    cond_low = (cond_mel.astype(F32) * keep).astype(BF16)
    mel = jnp.concatenate([noisy_mel, cond_low], axis=1)
    mels = mel.shape[1]
    text_width = text_embed.shape[1]
    gain = text_gain[None, :]

    def block_of(array):
        return (whole(array.shape), array)

    normed_text, pre_act, energy, mixed_text, refined, state_zero = run_kernel(
        text_forward,
        1,
        [
            block_of(member)
            for member in (
                text_embed,
                mel,
                dw_kernel,
                text_bias,
                gain,
                text_hidden,
                pw_in,
                pw_out,
                in_proj,
                frame_bias,
            )
        ],
        [
            (whole(shape), shape, kind)
            for shape, kind in (
                ((rows, text_width), BF16),
                ((rows, pw_in.shape[1]), F32),
                ((8, pw_in.shape[1]), F32),
                ((rows, pw_in.shape[1]), BF16),
                ((rows, text_width), BF16),
                (full, F32),
            )
        ],
        [pltpu.VMEM((rows + 16, text_width), F32), pltpu.VMEM((rows, pw_in.shape[1]), F32)],
    )

    def semaphores(number, pieces=2):
        shape = (number, pieces) if pieces > 1 else (number,)
        return pltpu.SemaphoreType.DMA(shape)

    def attn_buffers(number, pieces=2):
        return [
            pltpu.VMEM((number, 3, model_width, width), BF16),
            pltpu.VMEM((number, width, model_width), BF16),
            semaphores(number, pieces),
            semaphores(number, pieces),
        ]

    def ffn_buffers(number, pieces=2):
        return [
            pltpu.VMEM((number, model_width, units), BF16),
            pltpu.VMEM((number, units, model_width), BF16),
            semaphores(number, pieces),
            semaphores(number, pieces),
        ]

    half_index = (own_data % 2).astype(jnp.int32).reshape(1)

    def pieces_of(slots):
        return tuple(len(pieces) for pieces in slots)

    (time_late,) = after([time_embed], state_zero)
    time_rows = time_late.astype(F32)
    activated, silu_back = jax.vjp(jax.nn.silu, time_rows)
    activated_low = activated.astype(BF16)
    modulation = (mm(activated_low, mod_weight) + mod_bias).astype(BF16)
    biases = jnp.concatenate([qkv_bias.reshape(-1), ff_in_bias])
    riders = jnp.broadcast_to(biases[None, :], (group, biases.size))
    sent = jnp.concatenate([modulation, riders], axis=1)
    came = lax.all_to_all(sent, "heads", split_axis=0, concat_axis=1, tiled=True)
    came = came.reshape(group, sent.shape[1]).astype(F32)
    mod_rows = came[:, : modulation.shape[1]].reshape(6, model_width)
    slot_owner = jnp.bitwise_xor(jnp.arange(group, dtype=jnp.int32), own)
    biases_all = jnp.take(came[:, modulation.shape[1] :], slot_owner, axis=0)
    qkv_bias_all = biases_all[:, : 3 * width].reshape(group, 3, width)
    up_bias_all = biases_all[:, 3 * width :].reshape(group, 1, units)

    for fetch in fetches[2:]:
        fetch.send(came)
    for fetch in fetches[:2]:
        fetch.share()
        fetch.cores(2, parts)
    (mod_rows,) = after([mod_rows], *[fetch.sent[2] for fetch in fetches[:2]])
    kept = []
    for turn in range(2):
        first, last = turn == 0, turn == 1
        if last:
            for fetch in fetches[:2]:
                fetch.cores(parts, group, normed)
            for fetch in fetches[2:]:
                fetch.share(normed)
                fetch.core(0, normed)
            (before,) = after([before], *[fetch.slots[2][0] for fetch in fetches[2:]])
        chosen = range(turn * parts, (turn + 1) * parts)
        qkv_here = [fetches[0].slots[slot] for slot in chosen]
        out_here = [fetches[1].slots[slot] for slot in chosen]
        inputs = [
            (SMEM, count),
            (SMEM, half_index),
            (whole(full), state_zero),
            (whole((6, model_width)), mod_rows),
            (held((3, width)), qkv_bias_all[chosen[0] : chosen[-1] + 1]),
            (whole((3, model_width)), frame_bias),
            (whole((rows, block)), cosine),
            (whole((rows, block)), sine),
        ]
        inputs += [(ANY, member) for member in flat(qkv_here) + flat(out_here)]
        if not first:
            inputs += [(whole(full), normed), (whole(full), before)]
        outputs = [(held((rows, width)), (parts, rows, width), BF16)] * 4
        outputs += [(held((8, rows)), (parts, 8, rows), F32)]
        if first:
            outputs += [(whole(full), full, BF16)]
        outputs += [(whole(full), full, F32)]
        if last:
            outputs += [(whole(full), full, F32), (whole(full), full, BF16)]
        results = run_kernel(
            partial(attention_forward, pieces_of(qkv_here), first, last),
            parts,
            inputs,
            outputs,
            attn_buffers(parts) + ([pltpu.VMEM(full, F32)] if last else []),
        )
        kept.append(results[:5])
        if first:
            normed, before = results[5:]
        else:
            branch, state_one, ffn_in = results[5:]

    qkv_all, out_all = fetches[0].listed(), fetches[1].listed()
    fetches[2].cores(2, group, ffn_in)
    fetches[3].cores(2, group, ffn_in)
    up_all, down_all = fetches[2].listed()[::-1], fetches[3].listed()[::-1]
    inputs = [
        (SMEM, half_index),
        (whole(full), cotangent),
        (whole(full), state_one),
        (whole(full), branch),
        (whole(full), ffn_in),
        (whole((6, model_width)), mod_rows),
        (held((1, units), group), up_bias_all),
        (whole((3, model_width)), frame_bias),
    ]
    inputs += [(ANY, member) for member in flat(up_all) + flat(down_all)]
    merged = (2 * units, model_width)
    outputs = [(held((1, units), group), (group, 1, units), F32)]
    outputs += [(whole((8, model_width)), (8, model_width), F32)]
    outputs += [(ANY, merged, BF16)] * group
    outputs += [(whole(full), full, BF16)] * 2 + [(whole(full), full, F32)]
    outputs += [(whole(full), full, BF16)]
    results = run_kernel(
        partial(feed_forward, pieces_of(up_all), True, True),
        group,
        inputs,
        outputs,
        [
            pltpu.VMEM((group, model_width, units), BF16),
            pltpu.VMEM((group, units, model_width), BF16),
            semaphores(group),
            semaphores(group),
            pltpu.VMEM((group,) + merged, BF16),
            semaphores(group, 1),
            pltpu.VMEM((model_width, rows), BF16),
            pltpu.VMEM((rows, units), BF16),
            pltpu.VMEM((rows, units), BF16),
        ]
        + [pltpu.VMEM(full, F32)] * 2,
    )
    grad_up_bias, ffn_sums = results[:2]
    output, grad_one, grad_attn = results[3 + group :]
    ffn_grads = results[2 : 2 + group][::-1]

    attn_grads = []
    merged = (4 * width, model_width)
    qkv_bias_parts = []
    for turn in range(2):
        first, last = turn == 0, turn == 1
        chosen = [group - 1 - turn * parts - at for at in range(parts)]
        inputs = [
            (SMEM, count),
            (SMEM, half_index),
            (whole(full), grad_attn),
            (whole(full), normed),
            (whole((6, model_width)), mod_rows),
            (whole((rows, block)), cosine),
            (whole((rows, block)), sine),
        ]
        inputs += [(held((rows, width), parts), member) for member in kept[1 - turn][:4]]
        inputs += [(held((8, rows), parts), kept[1 - turn][4])]
        inputs += [(ANY, member) for member in flat([qkv_all[slot] for slot in chosen])]
        inputs += [(ANY, member) for member in flat([out_all[slot] for slot in chosen])]
        if not first:
            inputs += [(whole(full), back)]
        if last:
            inputs += [(whole(full), state_zero), (whole(full), grad_one)]
        outputs = [(held((3, width), parts), (parts, 3, width), F32)]
        outputs += [(ANY, merged, BF16)] * parts
        if last:
            outputs += [(whole(full), full, BF16), (whole((8, model_width)), (8, model_width), F32)]
        else:
            outputs += [(whole(full), full, F32)]
        results = run_kernel(
            partial(attention_backward, pieces_of([qkv_all[slot] for slot in chosen]), first, last),
            parts,
            inputs,
            outputs,
            attn_buffers(parts)
            + [pltpu.VMEM((parts,) + merged, BF16), semaphores(parts, 1)]
            + [pltpu.VMEM((model_width, rows), BF16), pltpu.VMEM((rows, width), BF16)]
            + ([pltpu.VMEM(full, F32)] if last else []),
        )
        qkv_bias_parts.append(results[0])
        attn_grads = list(results[1 : 1 + parts])[::-1] + attn_grads
        if first:
            back = results[1 + parts]
            ffn_sum = GroupSum()
            token = back
            for slot in range(group - 1, 0, -1):
                total = ffn_sum.put(slot, ffn_grads[slot], token)
                if slot % 2 == 0:
                    token = total
            (back,) = after([back], token)
        else:
            grad_zero, attn_sums = results[1 + parts :]
    token = grad_zero
    attn_sum = GroupSum()
    for slot in range(group - 1, 0, -1):
        total = attn_sum.put(slot, attn_grads[slot], token)
        if slot % 2 == 0:
            token = total
    (grad_zero,) = after([grad_zero], token)

    data = lax.axis_size("dp")
    stack_rows = 3 * text_width + mels
    stack_rows += -stack_rows % 16 + small_rows(group) + 8 * group * data
    stack_rows += -stack_rows % (16 * group * data)
    own_index = jnp.stack([own, own_data * group + own]).astype(jnp.int32)
    own_active = lax.dynamic_index_in_dim(activated_low, own, 0)
    results = run_kernel(
        partial(text_backward, group),
        1,
        [(SMEM, own_index)]
        + [
            block_of(member)
            for member in (
                grad_zero,
                text_embed,
                mel,
                refined,
                mixed_text,
                normed_text,
                pre_act,
                energy,
                dw_kernel,
                text_bias,
                gain,
                text_hidden,
                pw_in,
                pw_out,
                in_proj,
                attn_sums,
                ffn_sums,
                qkv_bias_parts[0],
                qkv_bias_parts[1],
                grad_up_bias,
                own_active,
            )
        ],
        [
            (whole((rows, text_width)), (rows, text_width), F32),
            (whole((6, model_width)), (6, model_width), BF16),
        ]
        + [(ANY, (stack_rows // group, model_width), BF16)] * group,
        [
            pltpu.VMEM((stack_rows, model_width), BF16),
            semaphores(group, 1),
            pltpu.VMEM((rows + 16, text_width), F32),
            pltpu.VMEM((rows + 16, text_width), F32),
            pltpu.VMEM((rows, text_width), F32),
            pltpu.VMEM((rows, text_width), BF16),
            pltpu.VMEM((rows, pw_in.shape[1]), F32),
            pltpu.VMEM((rows, pw_in.shape[1]), BF16),
            pltpu.VMEM((rows, text_width), F32),
            pltpu.VMEM((small_rows(group), model_width), F32),
        ],
    )
    grad_text, grad_mod = results[:2]
    def unpack(kernel, data, first, second, *others):
        pieces = after(data.pieces.values(), *others)
        return run_kernel(
            partial(kernel, len(pieces)),
            1,
            [(SMEM, jnp.stack(data.starts()).astype(jnp.int32))]
            + [(ANY, member) for member in pieces],
            [(whole(first.shape), first.shape, F32), (whole(second.shape), second.shape, F32)],
            [pltpu.VMEM((data.rows, model_width), BF16), semaphores(len(pieces), 1)],
        )

    bits = axis_bits("dp")
    ffn_data = DataSum(ffn_sum.put(0, ffn_grads[0]), bits)
    token = ffn_data.step(grad_mod)
    text_sum = GroupSum()
    for slot in range(group - 1, 0, -1):
        total = text_sum.put(slot, results[2 + slot], token)
        if slot % 2 == 0:
            token = total
    attn_data = DataSum(attn_sum.put(0, attn_grads[0]), bits)
    text_data = DataSum(text_sum.put(0, results[2]), bits, merged=True)
    steps = [(at, ffn_data) for at in range(1, len(bits) + 1)]
    for at in range(len(bits) + 1):
        steps.append((at + 1.9 if at else 1.5, attn_data))
        steps.append((at + 2.25, text_data))
    steps.sort(key=lambda step: step[0])
    columns = mod_weight.shape[1]
    grad_time = None
    for at, member in steps:
        if at > len(bits) and member is attn_data and grad_time is None:
            (grad_mod,) = after([grad_mod], token)
            grad_mod = grad_mod.reshape(1, group * columns)
            grad_cols = lax.all_to_all(grad_mod, "heads", split_axis=1, concat_axis=0, tiled=True)
            (grad_time,) = silu_back(inner_cols(grad_cols, mod_weight))
            token = member.step(token, grad_time)
        elif at == steps[-1][0]:
            (grad_time,) = after([grad_time], token)
            grad_time = jnp.broadcast_to(grad_time.astype(BF16), (group,) + grad_time.shape)
            grad_time = lax.all_to_all(grad_time, "heads", split_axis=0, concat_axis=0)
            grad_time = jnp.sum(grad_time.astype(F32), axis=0)
            token = member.step(token, grad_time)
        else:
            token = member.step(token)

    weight_up, weight_down = unpack(ffn_unpack, ffn_data, ff_in, ff_out, attn_data.pieces[0])
    text_half = text_data.half(weight_up, *list(attn_data.pieces.values())[1:])
    weight_qkv, weight_out = unpack(attn_unpack, attn_data, qkv_weight, out_weight, text_half)
    text_halves = {0: [text_half]}
    for slot in range(2, group, 2):
        bit = low_bit(slot)
        text_halves[slot] = [swap(text_halves[slot - bit][0], "heads", bit)]
        text_halves[slot] = list(after(text_halves[slot], weight_qkv))
    for slot in range(0, group, 2):
        text_halves[slot].append(swap(text_halves[slot][0], "dp", 1))
        text_halves[slot + 1] = [swap(piece, "heads", 1) for piece in text_halves[slot]]
    slot_rows = stack_rows // group
    text_pieces, text_starts = [], []
    for slot, pieces in text_halves.items():
        for which, piece in enumerate(pieces):
            text_pieces.append(piece)
            text_starts.append(
                slot_owner[slot] * slot_rows + ((own_data + which) % 2) * (slot_rows // 2)
            )
    unpacked = (
        in_proj.shape,
        pw_in.shape,
        pw_out.shape,
        dw_kernel.shape,
        text_bias.shape,
        gain.shape,
        text_hidden.shape,
        frame_bias.shape,
        (3, width),
        (1, units),
    )
    mods_shape = (8 * group * data, model_width)
    unpacked = run_kernel(
        partial(text_unpack, len(text_pieces), group),
        1,
        [(SMEM, jnp.stack(text_starts).astype(jnp.int32)), (SMEM, own_index)]
        + [(ANY, member) for member in text_pieces],
        [(whole(shape), shape, F32) for shape in unpacked]
        + [(whole(mods_shape), mods_shape, BF16)],
        [
            pltpu.VMEM((stack_rows, model_width), BF16),
            semaphores(len(text_pieces), 1),
            pltpu.VMEM((small_rows(group), model_width), F32),
        ],
    )
    seen = unpacked[10].reshape(group * data, 8, model_width)
    grad_mod_all = seen[:, :6].reshape(group * data, 6 * model_width)
    grad_mod_all = lax.dynamic_slice_in_dim(grad_mod_all, own * columns, columns, axis=1)
    grad_mod_weight = inner_rows(seen[:, 6], grad_mod_all)
    grad_mod_bias = jnp.sum(grad_mod_all.astype(F32), axis=0)
    return (
        output,
        grad_text,
        grad_time,
        unpacked[3],
        unpacked[4],
        unpacked[5][0],
        unpacked[6],
        unpacked[1],
        unpacked[2],
        unpacked[0],
        unpacked[7],
        grad_mod_weight,
        grad_mod_bias,
        weight_qkv,
        unpacked[8],
        weight_out,
        weight_up,
        unpacked[9][0],
        weight_down,
    )


def solution(mesh):
    in_specs = (
        P(("dp", "heads"), None),
        P(("dp", "heads"), None),
        P(("dp", "heads"), None),
        P("dp", None),
        P("dp"),
        P(("dp", "heads"), None),
        P(),
        P(),
        P(),
        P(),
        P(),
        P(),
        P(),
        P(),
        P(None, "heads"),
        P("heads"),
        P(None, None, "heads"),
        P(None, "heads"),
        P("heads", None),
        P(None, "heads"),
        P("heads"),
        P("heads", None),
        P(("dp", "heads"), None),
    )
    out_specs = (
        P(("dp", "heads"), None),
        P(("dp", "heads"), None),
        P("dp", None),
        P(),
        P(),
        P(),
        P(),
        P(),
        P(),
        P(),
        P(),
        P(None, "heads"),
        P("heads"),
        P(None, None, "heads"),
        P(None, "heads"),
        P("heads", None),
        P(None, "heads"),
        P("heads"),
        P("heads", None),
    )
    return jax.shard_map(
        on_device, mesh=mesh, in_specs=in_specs, out_specs=out_specs, check_vma=False
    )
```

```python
from functools import partial

import jax
import jax.numpy as jnp
from jax import lax
from jax.experimental import pallas as pl
from jax.experimental.pallas import tpu as pltpu
from jax.sharding import PartitionSpec as P

HD = 64


def inner_rows(left, right):
    return lax.dot_general(
        left, right, (((0,), (0,)), ((), ())), preferred_element_type=jnp.float32
    )


def inner_cols(left, right):
    return lax.dot_general(
        left, right, (((1,), (1,)), ((), ())), preferred_element_type=jnp.float32
    )


F32 = jnp.float32
BF16 = jnp.bfloat16
CHUNK = 64
SPAN = 256
VMEM = 60 * 1024 * 1024


def mm(left, right):
    return jnp.dot(left, right, preferred_element_type=F32)


def fold(values):
    return jnp.sum(values.reshape(values.shape[0] // 8, 8, values.shape[1]), axis=0)


def norm_parts(values):
    mean = jnp.mean(values, axis=-1, keepdims=True)
    centred = values - mean
    root = lax.rsqrt(jnp.mean(centred * centred, axis=-1, keepdims=True) + 1e-06)
    return centred * root, root


def norm_pull(grad, scale, xhat, root):
    entry = grad * (1.0 + scale)
    mean = jnp.mean(entry, axis=-1, keepdims=True)
    along = jnp.mean(entry * xhat, axis=-1, keepdims=True)
    return root * (entry - mean - xhat * along)


def swap_pairs(block):
    width = block.shape[1]
    lane = lax.broadcasted_iota(jnp.int32, block.shape, 1)
    if width % 128 == 0:
        after = pltpu.roll(block, width - 1, 1)
        before = pltpu.roll(block, 1, 1)
    else:
        after = jnp.concatenate([block[:, 1:], block[:, :1]], axis=1)
        before = jnp.concatenate([block[:, width - 1 :], block[:, : width - 1]], axis=1)
    return jnp.where(lane % 2 == 0, after, before)


def head_lanes(block, head):
    if block.shape[1] == HD:
        return block
    lane = lax.broadcasted_iota(jnp.int32, block.shape, 1)
    return jnp.where((lane >= head * HD) & (lane < (head + 1) * HD), block, jnp.zeros_like(block))


def slot_copies(pieces, target, sems, at, axis, half):
    if len(pieces) == 1:
        return [pltpu.make_async_copy(pieces[0], target.at[at], sems.at[at, 0])]
    copies = []
    for which, piece in enumerate(pieces):
        size = piece.shape[axis]
        start = pl.multiple_of((half if which == 0 else 1 - half) * size, size)
        index = (at,) + (slice(None),) * axis + (pl.ds(start, size),)
        copies.append(pltpu.make_async_copy(piece, target.at[index], sems.at[at, which]))
    return copies


def start_all(step, copies):
    @pl.when(step == 0)
    def _():
        for members in copies:
            for copy in members:
                copy.start()


def wait_own(step, copies):
    for at, members in enumerate(copies):

        @pl.when(step == at)
        def _(members=members):
            for copy in members:
                copy.wait()


def send_own(step, results):
    for at, members in enumerate(results):

        @pl.when(step == at)
        def _(members=members):
            for copy in members:
                copy.start()


def wait_all(step, results):
    @pl.when(step == len(results) - 1)
    def _():
        for members in results:
            for copy in members:
                copy.wait()


def attention_forward(pieces, first, last, *refs):
    parts = len(pieces)
    refs = list(refs)

    def take(count=1):
        taken = [refs.pop(0) for _ in range(count)]
        return taken[0] if count == 1 else taken

    count_ref, half_ref, state_ref, mod_ref, bias_ref, frame_ref, cosine_ref, sine_ref = take(8)
    weights = [[take() for _ in range(number)] for number in pieces]
    outs = [[take() for _ in range(number)] for number in pieces]
    if not first:
        normed_ref, before_ref = take(2)
    query_ref, key_ref, value_ref, attended_ref, log_ref = take(5)
    if first:
        normed_ref = take()
    if last:
        branch_ref, one_ref, ffn_ref = take(3)
    else:
        total_ref = take()
    weight_ref, out_ref, weight_sem, out_sem = take(4)
    if last:
        total_ref = take()
    step = pl.program_id(0)
    rows = state_ref.shape[0]
    width = weight_ref.shape[3]
    block = cosine_ref.shape[1]
    count = count_ref[0]
    half = half_ref[0]
    copies = [
        slot_copies(weights[at], weight_ref, weight_sem, at, 1, half)
        + slot_copies(outs[at], out_ref, out_sem, at, 0, half)
        for at in range(parts)
    ]
    start_all(step, copies)

    @pl.when(step == 0)
    def _():
        if first:

            def chunk(at, carry):
                here = pl.ds(at * CHUNK, CHUNK)
                xhat, _ = norm_parts(state_ref[here, :])
                normed_ref[here, :] = (xhat * (1.0 + mod_ref[1:2, :]) + mod_ref[0:1, :]).astype(
                    BF16
                )
                return carry

            lax.fori_loop(0, rows // CHUNK, chunk, 0)
            total_ref[...] = jnp.zeros_like(total_ref)
        else:
            total_ref[...] = before_ref[...]

    wait_own(step, copies)
    normed = normed_ref[...]
    cosine = cosine_ref[...]
    sine = sine_ref[...]
    logs = jnp.zeros((rows, 128), F32)
    lane = lax.broadcasted_iota(jnp.int32, (rows, 128), 1)
    query_lin = mm(normed, weight_ref[step, 0]) + bias_ref[0, 0:1, :]
    key_lin = mm(normed, weight_ref[step, 1]) + bias_ref[0, 1:2, :]
    value_ref[0] = (mm(normed, weight_ref[step, 2]) + bias_ref[0, 2:3, :]).astype(BF16)
    for at in range(width // block):
        cut = slice(at * block, (at + 1) * block)
        piece = query_lin[:, cut]
        turned = piece * cosine + swap_pairs(piece) * sine
        query_ref[0, :, cut] = (turned * HD**-0.5).astype(BF16)
        piece = key_lin[:, cut]
        key_ref[0, :, cut] = (piece * cosine + swap_pairs(piece) * sine).astype(BF16)
    live = lax.broadcasted_iota(jnp.int32, (1, rows), 1) < count
    for at in range(width // block):
        cut = slice(at * block, (at + 1) * block)
        keys = key_ref[0, :, cut]
        values = value_ref[0, :, cut]
        results = [None] * (rows // SPAN)
        pieces = [[] for _ in range(rows // SPAN)]
        for head in range(block // HD):
            own_values = head_lanes(values, head)
            for part in range(rows // SPAN):
                queries = head_lanes(query_ref[0, part * SPAN : (part + 1) * SPAN, cut], head)
                scores = jnp.where(live, inner_cols(queries, keys), -1e30)
                top = jnp.max(scores, axis=1, keepdims=True)
                expo = jnp.exp(scores - top)
                total = jnp.sum(expo, axis=1, keepdims=True)
                weights = (expo * (1.0 / total)).astype(BF16)
                result = mm(weights, own_values)
                results[part] = result if head == 0 else results[part] + result
                pieces[part].append(top + jnp.log(total))
        for head in range(block // HD):
            column = jnp.concatenate([pieces[part][head] for part in range(rows // SPAN)], axis=0)
            logs = jnp.where(lane == at * (block // HD) + head, column, logs)
        for part in range(rows // SPAN):
            place = part * SPAN + lax.broadcasted_iota(jnp.int32, (SPAN, block), 0)
            attended_ref[0, part * SPAN : (part + 1) * SPAN, cut] = jnp.where(
                place < count, results[part], 0.0
            ).astype(BF16)
    log_ref[0] = jnp.transpose(logs)[0:8, :]
    total_ref[...] += mm(attended_ref[0], out_ref[step])

    if last:

        @pl.when(step == parts - 1)
        def _():
            def chunk(at, carry):
                here = pl.ds(at * CHUNK, CHUNK)
                branch = total_ref[here, :] + frame_ref[1:2, :]
                branch_ref[here, :] = branch
                state_one = state_ref[here, :] + mod_ref[2:3, :] * branch
                one_ref[here, :] = state_one
                xhat, _ = norm_parts(state_one)
                ffn_ref[here, :] = (xhat * (1.0 + mod_ref[4:5, :]) + mod_ref[3:4, :]).astype(BF16)
                return carry

            lax.fori_loop(0, rows // CHUNK, chunk, 0)


def lay(target_ref, at, start, value):
    model, width = value.shape
    for block in range(model // width):
        target_ref[at, start : start + width, block * width : (block + 1) * width] = value[
            block * width : (block + 1) * width, :
        ]


def feed_forward(pieces, first, last, *refs):
    parts = len(pieces)
    refs = list(refs)

    def take(count=1):
        taken = [refs.pop(0) for _ in range(count)]
        return taken[0] if count == 1 else taken

    half_ref, cotangent_ref, one_ref, branch_ref, source_ref, mod_ref, bias_ref, frame_ref = take(8)
    ups = [[take() for _ in range(number)] for number in pieces]
    downs = [[take() for _ in range(number)] for number in pieces]
    if not first:
        grad_ref, total_in_ref, back_in_ref = take(3)
    grad_bias_ref, sums_ref = take(2)
    grads = [take() for _ in range(parts)]
    if first:
        grad_ref = take()
    if last:
        output_ref, grad_one_ref, grad_attn_ref = take(3)
    else:
        total_ref, back_ref = take(2)
    up_ref, down_ref, up_sem, down_sem = take(4)
    grads_ref, grads_sem = take(2)
    turned_ref, hidden_ref, pre_ref = take(3)
    if last:
        total_ref, back_ref = take(2)
    step = pl.program_id(0)
    rows, wide = one_ref.shape
    inner = 0.7978845608028654
    cubic = 0.044715
    half = half_ref[0]
    copies = [
        slot_copies(ups[at], up_ref, up_sem, at, 0, half)
        + slot_copies(downs[at], down_ref, down_sem, at, 0, half)
        for at in range(parts)
    ]
    results = [
        (pltpu.make_async_copy(grads_ref.at[at], grads[at], grads_sem.at[at]),)
        for at in range(parts)
    ]
    start_all(step, copies)

    @pl.when(step == 0)
    def _():
        if first:

            def chunk(at, carry):
                here = pl.ds(at * CHUNK, CHUNK)
                grad = cotangent_ref[here, :].astype(F32) * mod_ref[5:6, :]
                grad_ref[here, :] = grad.astype(BF16)
                return carry + fold(grad)

            lanes = lax.fori_loop(0, rows // CHUNK, chunk, jnp.zeros((8, wide), F32))
            sums_ref[0:1, :] = jnp.sum(lanes, axis=0, keepdims=True)
            total_ref[...] = jnp.zeros_like(total_ref)
            back_ref[...] = jnp.zeros_like(back_ref)
        else:
            total_ref[...] = total_in_ref[...]
            back_ref[...] = back_in_ref[...]
        turned_ref[...] = jnp.transpose(source_ref[...])

    wait_own(step, copies)
    up = up_ref[step]
    down = down_ref[step]
    lanes = jnp.zeros((8, up.shape[1]), F32)
    for part in range(rows // SPAN):
        here = slice(part * SPAN, (part + 1) * SPAN)
        pre = mm(source_ref[here, :], up) + bias_ref[0]
        grad_hidden = inner_cols(grad_ref[here, :], down)
        square = pre * pre
        bend = jnp.tanh(pre * (inner + inner * cubic * square))
        half = 0.5 * (1.0 + bend)
        hidden = (pre * half).astype(BF16)
        slope = half + 0.5 * pre * (1.0 - bend * bend) * (inner + 3.0 * inner * cubic * square)
        grad_pre = grad_hidden * slope
        lanes = lanes + fold(grad_pre)
        grad_pre = grad_pre.astype(BF16)
        hidden_ref[here, :] = hidden
        pre_ref[here, :] = grad_pre
        total_ref[here, :] += mm(hidden, down)
        back_ref[here, :] += inner_cols(grad_pre, up)
    grad_bias_ref[0] = jnp.sum(lanes, axis=0, keepdims=True)
    width = up_ref.shape[2]
    grads_ref[step, width:, :] = inner_rows(hidden_ref[...], grad_ref[...]).astype(BF16)
    lay(grads_ref, step, 0, mm(turned_ref[...], pre_ref[...]).astype(BF16))
    send_own(step, results)

    if last:

        @pl.when(step == parts - 1)
        def _():
            def chunk(at, carry):
                gate_ffn, scale_ffn, shift_ffn, bias_attn, gate_attn = carry
                here = pl.ds(at * CHUNK, CHUNK)
                branch = total_ref[here, :] + frame_ref[2:3, :]
                state_one = one_ref[here, :]
                output_ref[here, :] = (state_one + mod_ref[5:6, :] * branch).astype(BF16)
                cotangent = cotangent_ref[here, :].astype(F32)
                xhat, root = norm_parts(state_one)
                back = back_ref[here, :]
                grad_one = cotangent + norm_pull(back, mod_ref[4:5, :], xhat, root)
                grad_one_ref[here, :] = grad_one
                grad_attn = grad_one * mod_ref[2:3, :]
                grad_attn_ref[here, :] = grad_attn.astype(BF16)
                return (
                    gate_ffn + fold(cotangent * branch),
                    scale_ffn + fold(back * xhat),
                    shift_ffn + fold(back),
                    bias_attn + fold(grad_attn),
                    gate_attn + fold(grad_one * branch_ref[here, :]),
                )

            start = tuple(jnp.zeros((8, wide), F32) for _ in range(5))
            lanes = lax.fori_loop(0, rows // CHUNK, chunk, start)
            for at, member in enumerate(lanes):
                sums_ref[at + 1 : at + 2, :] = jnp.sum(member, axis=0, keepdims=True)

    wait_all(step, results)


def attention_backward(pieces, first, last, *refs):
    parts = len(pieces)
    refs = list(refs)

    def take(count=1):
        taken = [refs.pop(0) for _ in range(count)]
        return taken[0] if count == 1 else taken

    count_ref, half_ref, grad_attn_ref, normed_ref, mod_ref, cosine_ref, sine_ref = take(7)
    query_ref, key_ref, value_ref, attended_ref, log_ref = take(5)
    weights = [[take() for _ in range(number)] for number in pieces]
    outs = [[take() for _ in range(number)] for number in pieces]
    if not first:
        before_ref = take()
    if last:
        state_ref, grad_one_ref = take(2)
    grad_bias_ref = take()
    grads = [take() for _ in range(parts)]
    if last:
        grad_zero_ref, sums_ref = take(2)
    else:
        back_ref = take()
    weight_ref, out_ref, weight_sem, out_sem = take(4)
    grads_ref, grads_sem = take(2)
    turned_ref, item_ref = take(2)
    if last:
        back_ref = take()
    step = pl.program_id(0)
    rows, wide = normed_ref.shape
    width = weight_ref.shape[3]
    block = cosine_ref.shape[1]
    count = count_ref[0]
    half = half_ref[0]
    copies = [
        slot_copies(weights[at], weight_ref, weight_sem, at, 1, half)
        + slot_copies(outs[at], out_ref, out_sem, at, 0, half)
        for at in range(parts)
    ]
    results = [
        (pltpu.make_async_copy(grads_ref.at[at], grads[at], grads_sem.at[at]),)
        for at in range(parts)
    ]
    start_all(step, copies)

    @pl.when(step == 0)
    def _():
        turned_ref[...] = jnp.transpose(normed_ref[...])
        back_ref[...] = jnp.zeros_like(back_ref) if first else before_ref[...]

    wait_own(step, copies)
    grad_attn = grad_attn_ref[...]
    place = lax.broadcasted_iota(jnp.int32, (rows, width), 0)
    item_ref[...] = jnp.where(place < count, inner_cols(grad_attn, out_ref[step]), 0.0).astype(BF16)
    grads_ref[step, 3 * width :, :] = inner_rows(attended_ref[0], grad_attn).astype(BF16)
    cosine = cosine_ref[...]
    sine = sine_ref[...]
    live = lax.broadcasted_iota(jnp.int32, (rows, 1), 0) < count
    linear = [[], [], []]
    for at in range(width // block):
        cut = slice(at * block, (at + 1) * block)
        keys = key_ref[0, :, cut]
        values = value_ref[0, :, cut]
        keys_turned = jnp.transpose(keys)
        grad_keys = jnp.zeros((rows, block), F32)
        grad_values = jnp.zeros((rows, block), F32)
        grad_queries = [[] for _ in range(rows // SPAN)]
        for head in range(block // HD):
            index = at * (block // HD) + head
            for part in range(rows // SPAN):
                here = slice(part * SPAN, (part + 1) * SPAN)
                queries = head_lanes(query_ref[0, here, cut], head)
                items = head_lanes(item_ref[here, cut], head)
                scores = jnp.where(live, inner_cols(keys, queries), -1e30)
                weights = jnp.exp(scores - log_ref[0, index : index + 1, here])
                grad_weights = inner_cols(values, items)
                along = jnp.sum(grad_weights * weights, axis=0, keepdims=True)
                grad_scores = (weights * (grad_weights - along)).astype(BF16)
                grad_values = grad_values + mm(weights.astype(BF16), items)
                grad_keys = grad_keys + mm(grad_scores, queries)
                grad_queries[part].append(
                    mm(keys_turned[head * HD : (head + 1) * HD, :], grad_scores)
                )
        grad_query = jnp.concatenate(
            [jnp.concatenate(grad_queries[part], axis=0) for part in range(rows // SPAN)], axis=1
        )
        grad_query = jnp.transpose(grad_query) * HD**-0.5
        for which, member in enumerate((grad_query, grad_keys)):
            linear[which].append(member * cosine - swap_pairs(member) * sine)
        linear[2].append(grad_values)
    for which in range(3):
        member = jnp.concatenate(linear[which], axis=1) if width > block else linear[which][0]
        grad_bias_ref[0, which : which + 1, :] = jnp.sum(member, axis=0, keepdims=True)
        member = member.astype(BF16)
        lay(grads_ref, step, which * width, mm(turned_ref[...], member).astype(BF16))
        back_ref[...] += inner_cols(member, weight_ref[step, which])

    send_own(step, results)

    if last:

        @pl.when(step == parts - 1)
        def _():
            def chunk(at, carry):
                scale_attn, shift_attn, bias_in = carry
                here = pl.ds(at * CHUNK, CHUNK)
                xhat, root = norm_parts(state_ref[here, :])
                back = back_ref[here, :]
                grad_zero = grad_one_ref[here, :] + norm_pull(back, mod_ref[1:2, :], xhat, root)
                grad_zero_ref[here, :] = grad_zero.astype(BF16)
                return (
                    scale_attn + fold(back * xhat),
                    shift_attn + fold(back),
                    bias_in + fold(grad_zero),
                )

            start = tuple(jnp.zeros((8, wide), F32) for _ in range(3))
            lanes = lax.fori_loop(0, rows // CHUNK, chunk, start)
            for at, member in enumerate(lanes):
                sums_ref[at : at + 1, :] = jnp.sum(member, axis=0, keepdims=True)

    wait_all(step, results)


def total_of(refs):
    total = refs[0][...].astype(F32)
    for ref in refs[1:]:
        total = total + ref[...].astype(F32)
    return total.astype(BF16)


def sum_kernel(count, *refs):
    refs[count][...] = total_of(refs[:count])


def split_kernel(count, parts, *refs):
    own = refs[0][0]
    sums = [total_of(refs[1 + at * count : 1 + (at + 1) * count]) for at in range(parts)]
    for mask, ref in enumerate(refs[1 + parts * count :]):
        value = sums[mask]
        for at in range(1, parts):
            value = jnp.where(own == at, sums[at ^ mask], value)
        ref[...] = value


def merge_kernel(count, starts_ref, *refs):
    bring(starts_ref, refs[:count], refs[count], refs[count + 1])


def bring(starts_ref, pieces, stack_ref, sems):
    size = pieces[0].shape[0]
    copies = []
    for at, piece in enumerate(pieces):
        start = pl.multiple_of(starts_ref[at], 16)
        copies.append(
            pltpu.make_async_copy(piece, stack_ref.at[pl.ds(start, size), :], sems.at[at])
        )
    for copy in copies:
        copy.start()
    for copy in copies:
        copy.wait()


def unlay(target, stack_ref, start, width):
    for block in range(target.shape[0] // width):
        target[block * width : (block + 1) * width, :] = stack_ref[
            start : start + width, block * width : (block + 1) * width
        ].astype(F32)


def ffn_unpack(count, starts_ref, *refs):
    pieces = refs[:count]
    up_ref, down_ref, stack_ref, sems = refs[count:]
    bring(starts_ref, pieces, stack_ref, sems)
    width = up_ref.shape[1]
    unlay(up_ref, stack_ref, 0, width)
    down_ref[...] = stack_ref[width:, :].astype(F32)


def attn_unpack(count, starts_ref, *refs):
    pieces = refs[:count]
    weight_ref, out_ref, stack_ref, sems = refs[count:]
    bring(starts_ref, pieces, stack_ref, sems)
    width = weight_ref.shape[2]
    for which in range(3):
        unlay(weight_ref.at[which], stack_ref, which * width, width)
    out_ref[...] = stack_ref[3 * width :, :].astype(F32)


def gelu_parts(pre):
    share = 0.5 * (1.0 + lax.erf(pre * 0.7071067811865476))
    slope = share + pre * (0.3989422804014327 * jnp.exp(-0.5 * pre * pre))
    return pre * share, slope


def fill_padded(padded_ref, text_ref):
    rows, wide = text_ref.shape
    edge = jnp.zeros((8, wide), F32)
    padded_ref[0:8, :] = edge
    padded_ref[rows + 8 : rows + 16, :] = edge
    for at in range(rows // CHUNK):
        here = slice(at * CHUNK, (at + 1) * CHUNK)
        padded_ref[at * CHUNK + 8 : (at + 1) * CHUNK + 8, :] = text_ref[here, :].astype(F32)


def text_forward(
    text_ref,
    mel_ref,
    kernel_ref,
    bias_ref,
    gain_ref,
    hidden_bias_ref,
    in_ref,
    out_ref,
    project_ref,
    frame_ref,
    normed_ref,
    pre_ref,
    energy_ref,
    mixed_ref,
    refined_ref,
    state_ref,
    padded_ref,
    hidden_ref,
):
    rows, wide = text_ref.shape
    taps = kernel_ref.shape[0]
    fill_padded(padded_ref, text_ref)

    def front(at, carry):
        start = pl.multiple_of(at * CHUNK, CHUNK)
        near = padded_ref[pl.ds(start, CHUNK + 16), :]
        conv = bias_ref[0:1, :]
        for tap in range(taps):
            shift = 8 + tap - taps // 2
            conv = conv + near[shift : shift + CHUNK, :] * kernel_ref[tap : tap + 1, :]
        xhat, _ = norm_parts(conv)
        normed_ref[pl.ds(start, CHUNK), :] = (xhat * gain_ref[...] + bias_ref[1:2, :]).astype(BF16)
        return carry

    lax.fori_loop(0, rows // CHUNK, front, 0)
    pre_ref[...] = mm(normed_ref[...], in_ref[...]) + hidden_bias_ref[0:1, :]

    def gelu(at, carry):
        here = pl.ds(at * CHUNK, CHUNK)
        hidden, _ = gelu_parts(pre_ref[here, :])
        hidden_ref[here, :] = hidden
        return carry + fold(hidden * hidden)

    squares = lax.fori_loop(0, rows // CHUNK, gelu, jnp.zeros((8, pre_ref.shape[1]), F32))
    energy = jnp.sqrt(jnp.sum(squares, axis=0, keepdims=True))
    energy_ref[0:1, :] = energy
    ratio = energy / (jnp.mean(energy, axis=1, keepdims=True) + 1e-06)

    def mix(at, carry):
        here = pl.ds(at * CHUNK, CHUNK)
        hidden = hidden_ref[here, :]
        mixed = hidden_bias_ref[1:2, :] * (hidden * ratio) + hidden_bias_ref[2:3, :] + hidden
        mixed_ref[here, :] = mixed.astype(BF16)
        return carry

    lax.fori_loop(0, rows // CHUNK, mix, 0)
    refined_ref[...] = (
        text_ref[...].astype(F32) + mm(mixed_ref[...], out_ref[...]) + bias_ref[2:3, :]
    ).astype(BF16)
    state_ref[...] = (
        mm(mel_ref[...], project_ref[0 : mel_ref.shape[1], :])
        + mm(refined_ref[...], project_ref[mel_ref.shape[1] :, :])
        + frame_ref[0:1, :]
    )


def full_line(members, wide):
    have = sum(member.shape[1] for member in members)
    return jnp.concatenate(list(members) + [jnp.zeros((1, wide - have), F32)], axis=1)


def small_rows(group):
    count = 12 + 2 * group
    return count + -count % 16


def text_backward(group, *refs):
    refs = list(refs)

    def take(count=1):
        taken = [refs.pop(0) for _ in range(count)]
        return taken[0] if count == 1 else taken

    own_ref, grad_zero_ref, text_ref, mel_ref, refined_ref, mixed_ref, normed_ref = take(7)
    pre_ref, energy_ref, kernel_ref, bias_ref, gain_ref, hidden_bias_ref = take(6)
    in_ref, out_ref, project_ref, attn_sums_ref, ffn_sums_ref = take(5)
    high_bias_ref, low_bias_ref, up_bias_ref, active_ref = take(4)
    grad_text_ref, mods_ref = take(2)
    slots = [take() for _ in range(group)]
    stack_ref, sems, padded_ref, outer_ref, refined_grad_ref, low_ref, mixed_grad_ref = take(7)
    pre_low_ref, normed_grad_ref, lines_ref = take(3)
    small = small_rows(group)
    own = own_ref[0]
    rows, wide = text_ref.shape
    model = grad_zero_ref.shape[1]
    taps = kernel_ref.shape[0]
    mel_at = 3 * wide
    small_at = mel_at + mel_ref.shape[1] + (-(mel_at + mel_ref.shape[1])) % 16

    lines = [attn_sums_ref[1:2, :], attn_sums_ref[0:1, :]]
    lines += [ffn_sums_ref[row : row + 1, :] for row in (5, 3, 2, 1)]
    mods_at = small_at + small
    stack_ref[mods_at:, :] = jnp.zeros((stack_ref.shape[0] - mods_at, model), BF16)
    for at, member in enumerate(lines):
        mods_ref[at : at + 1, :] = member.astype(BF16)
    lines += [active_ref[...].astype(F32), jnp.zeros((1, model), F32)]
    lines = jnp.concatenate(lines, axis=0)
    empty = jnp.zeros_like(lines)
    odd = own_ref[1] % 2 == 1
    lines = jnp.where(
        odd, jnp.concatenate([empty, lines], axis=0), jnp.concatenate([lines, empty], axis=0)
    )
    place = pl.multiple_of(mods_at + own_ref[1] // 2 * 16, 16)
    stack_ref[pl.ds(place, 16), :] = lines.astype(BF16)

    grad_zero = grad_zero_ref[...]
    grad_refined = inner_cols(grad_zero, project_ref[mel_ref.shape[1] :, :])
    refined_grad_ref[...] = grad_refined
    low_ref[...] = grad_refined.astype(BF16)
    sum_out = jnp.sum(fold(grad_refined), axis=0, keepdims=True)
    mixed_grad_ref[...] = inner_cols(low_ref[...], out_ref[...])
    stack_ref[0:wide, :] = inner_rows(refined_ref[...], grad_zero).astype(BF16)
    spare = jnp.zeros((small_at - mel_at - mel_ref.shape[1], model), F32)
    grad_mel = inner_rows(mel_ref[...], grad_zero)
    stack_ref[mel_at:small_at, :] = jnp.concatenate([grad_mel, spare], axis=0).astype(BF16)
    grad_out = inner_rows(mixed_ref[...], low_ref[...]).astype(BF16)
    stack_ref[2 * wide : 3 * wide, 0:wide] = grad_out[0:wide, :]
    stack_ref[2 * wide : 3 * wide, wide:] = grad_out[wide:, :]

    energy = energy_ref[0:1, :]
    mean = jnp.mean(energy, axis=1, keepdims=True) + 1e-06
    ratio = energy / mean

    def first_pass(at, carry):
        along, plain = carry
        here = pl.ds(at * CHUNK, CHUNK)
        hidden, _ = gelu_parts(pre_ref[here, :])
        grad = mixed_grad_ref[here, :]
        return along + fold(grad * hidden), plain + fold(grad)

    zero = jnp.zeros((8, model), F32)
    along, plain = lax.fori_loop(0, rows // CHUNK, first_pass, (zero, zero))
    along = jnp.sum(along, axis=0, keepdims=True)
    sum_beta = jnp.sum(plain, axis=0, keepdims=True)
    gamma = hidden_bias_ref[1:2, :]
    grad_ratio = gamma * along
    grad_mean = jnp.sum(grad_ratio * energy, axis=1, keepdims=True) / (mean * mean)
    grad_energy = grad_ratio / mean - grad_mean / model
    spread = grad_energy / energy
    factor = 1.0 + gamma * ratio

    def second_pass(at, carry):
        here = pl.ds(at * CHUNK, CHUNK)
        hidden, slope = gelu_parts(pre_ref[here, :])
        grad = (mixed_grad_ref[here, :] * factor + hidden * spread) * slope
        pre_low_ref[here, :] = grad.astype(BF16)
        return carry + fold(grad)

    sum_in = jnp.sum(lax.fori_loop(0, rows // CHUNK, second_pass, zero), axis=0, keepdims=True)
    normed_grad_ref[...] = inner_cols(pre_low_ref[...], in_ref[...])
    stack_ref[wide : 2 * wide, :] = inner_rows(normed_ref[...], pre_low_ref[...]).astype(BF16)

    fill_padded(padded_ref, text_ref)
    edge = jnp.zeros((8, wide), F32)
    outer_ref[0:8, :] = edge
    outer_ref[rows + 8 : rows + 16, :] = edge
    narrow = jnp.zeros((8, wide), F32)
    step = CHUNK // 2

    def conv_back(at, carry):
        sum_gain, sum_norm, sum_conv, sum_taps = carry
        start = pl.multiple_of(at * step, step)
        near = padded_ref[pl.ds(start, step + 16), :]
        conv = bias_ref[0:1, :]
        for tap in range(taps):
            shift = 8 + tap - taps // 2
            conv = conv + near[shift : shift + step, :] * kernel_ref[tap : tap + 1, :]
        xhat, root = norm_parts(conv)
        grad = normed_grad_ref[pl.ds(start, step), :]
        entry = grad * gain_ref[...]
        entry_mean = jnp.mean(entry, axis=-1, keepdims=True)
        entry_along = jnp.mean(entry * xhat, axis=-1, keepdims=True)
        grad_conv = root * (entry - entry_mean - xhat * entry_along)
        outer_ref[pl.ds(start + 8, step), :] = grad_conv
        sum_taps = tuple(
            member
            + fold(grad_conv * near[8 + tap - taps // 2 : 8 + tap - taps // 2 + step, :])
            for tap, member in enumerate(sum_taps)
        )
        return (
            sum_gain + fold(grad * xhat),
            sum_norm + fold(grad),
            sum_conv + fold(grad_conv),
            sum_taps,
        )

    sum_gain, sum_norm, sum_conv, sum_taps = lax.fori_loop(
        0, rows // step, conv_back, (narrow, narrow, narrow, (narrow,) * taps)
    )

    def text_grad(at, carry):
        start = pl.multiple_of(at * CHUNK, CHUNK)
        near = outer_ref[pl.ds(start, CHUNK + 16), :]
        total = refined_grad_ref[pl.ds(start, CHUNK), :]
        for tap in range(taps):
            shift = 8 + taps // 2 - tap
            total = total + near[shift : shift + CHUNK, :] * kernel_ref[tap : tap + 1, :]
        grad_text_ref[pl.ds(start, CHUNK), :] = total
        return carry

    lax.fori_loop(0, rows // CHUNK, text_grad, 0)

    def line(member):
        return jnp.sum(member, axis=0, keepdims=True)

    halves = [line(member) for member in sum_taps] + [line(sum_gain)]
    halves += [line(sum_conv), line(sum_norm), sum_out, jnp.zeros((1, wide), F32)]
    lines = [
        jnp.concatenate(halves[at : at + 2], axis=1) for at in range(0, len(halves), 2)
    ]
    lines += [sum_in, ratio * along, sum_beta]
    lines += [attn_sums_ref[2:3, :], ffn_sums_ref[4:5, :], ffn_sums_ref[0:1, :]]
    lines_ref[...] = jnp.zeros_like(lines_ref)
    for at, member in enumerate(lines):
        lines_ref[at : at + 1, :] = member
    parts = group // 2
    row = lax.broadcasted_iota(jnp.int32, lines_ref.shape, 0)
    total = lines_ref[...]
    for slot in range(group):
        source_ref = low_bias_ref if slot < parts else high_bias_ref
        owner = jnp.bitwise_xor(own, slot)
        members = [source_ref[slot % parts, which : which + 1, :] for which in range(3)]
        total = jnp.where(row == 12 + owner, full_line(members, model), total)
        total = jnp.where(row == 12 + group + owner, full_line([up_bias_ref[slot]], model), total)
    lines_ref[...] = total
    stack_ref[small_at : small_at + small, :] = lines_ref[...].astype(BF16)

    size = stack_ref.shape[0] // group
    copies = []
    for slot in range(group):
        start = pl.multiple_of(jnp.bitwise_xor(own, slot) * size, size)
        copies.append(
            pltpu.make_async_copy(stack_ref.at[pl.ds(start, size), :], slots[slot], sems.at[slot])
        )
    for copy in copies:
        copy.start()
    for copy in copies:
        copy.wait()


def text_unpack(count, group, starts_ref, own_ref, *refs):
    pieces = refs[:count]
    project_ref, in_ref, out_ref, taps_ref, bias_ref, gain_ref = refs[count : count + 6]
    hidden_ref, frame_ref, qkv_bias_ref, up_bias_ref, mods_ref = refs[count + 6 : count + 11]
    stack_ref, sems, lines_ref = refs[count + 11 :]
    bring(starts_ref, pieces, stack_ref, sems)
    own = own_ref[0]
    wide = in_ref.shape[0]
    taps = taps_ref.shape[0]
    mels = project_ref.shape[0] - wide
    mel_at = 3 * wide
    small_at = mel_at + mels + (-(mel_at + mels)) % 16
    project_ref[0:mels, :] = stack_ref[mel_at : mel_at + mels, :].astype(F32)
    project_ref[mels:, :] = stack_ref[0:wide, :].astype(F32)
    in_ref[...] = stack_ref[wide : 2 * wide, :].astype(F32)
    out_ref[0:wide, :] = stack_ref[2 * wide : 3 * wide, 0:wide].astype(F32)
    out_ref[wide:, :] = stack_ref[2 * wide : 3 * wide, wide:].astype(F32)
    lines_ref[...] = stack_ref[small_at : small_at + small_rows(group), :].astype(F32)
    mods_at = small_at + small_rows(group)
    mods_ref[...] = stack_ref[mods_at : mods_at + mods_ref.shape[0], :]

    def half(at):
        return lines_ref[at // 2 : at // 2 + 1, (at % 2) * wide : (at % 2 + 1) * wide]

    for tap in range(taps):
        taps_ref[tap : tap + 1, :] = half(tap)
    gain_ref[...] = half(taps)
    for at in range(3):
        bias_ref[at : at + 1, :] = half(taps + 1 + at)
    first = (taps + 5) // 2
    hidden_ref[...] = lines_ref[first : first + 3, :]
    frame_ref[...] = lines_ref[first + 3 : first + 6, :]
    row = lax.broadcasted_iota(jnp.int32, lines_ref.shape, 0)

    def pick(at):
        return jnp.sum(jnp.where(row == at, lines_ref[...], 0.0), axis=0, keepdims=True)

    line = pick(12 + own)
    width = qkv_bias_ref.shape[1]
    for which in range(3):
        qkv_bias_ref[which : which + 1, :] = line[:, which * width : (which + 1) * width]
    up_bias_ref[...] = pick(12 + group + own)[:, 0 : up_bias_ref.shape[1]]


ANY = pl.BlockSpec(memory_space=pl.ANY)
SMEM = pl.BlockSpec(memory_space=pltpu.SMEM)


def whole(shape):
    return pl.BlockSpec(shape, lambda g: (0,) * len(shape))


def held(shape, parts=None):
    if parts is None:
        return pl.BlockSpec((1,) + shape, lambda g: (g,) + (0,) * len(shape))
    return pl.BlockSpec((1,) + shape, lambda g: (parts - 1 - g,) + (0,) * len(shape))


def run_kernel(kernel, parts, inputs, outputs, scratch):
    return pl.pallas_call(
        kernel,
        grid=(parts,),
        in_specs=[spec for spec, _ in inputs],
        out_specs=[spec for spec, _, _ in outputs],
        out_shape=[jax.ShapeDtypeStruct(shape, kind) for _, shape, kind in outputs],
        scratch_shapes=scratch,
        compiler_params=pltpu.CompilerParams(vmem_limit_bytes=VMEM),
        cost_estimate=pl.CostEstimate(flops=1024, bytes_accessed=1024, transcendentals=0),
    )(*[array for _, array in inputs])


def after(arrays, *others):
    arrays = tuple(arrays)
    return lax.optimization_barrier(arrays + others)[: len(arrays)]


def swap(array, axis, bit):
    return lax.ppermute(array, axis, [(at, at ^ bit) for at in range(lax.axis_size(axis))])


def low_bit(slot):
    return slot & -slot


def tile_rows(rows):
    return next(size for size in (256, 224, 128, 112, 96, 80, 64, 48, 32, 16) if rows % size == 0)


def add_arrays(arrays):
    rows, wide = arrays[0].shape
    tile = tile_rows(rows)
    spec = pl.BlockSpec((tile, wide), lambda g: (g, 0))
    return run_kernel(
        partial(sum_kernel, len(arrays)),
        rows // tile,
        [(spec, array) for array in arrays],
        [(spec, (rows, wide), BF16)],
        [],
    )[0]


def add_and_split(arrays, own, parts):
    rows, wide = arrays[0].shape
    size = rows // parts
    tile = tile_rows(size)
    steps = size // tile

    def block_at(part):
        return pl.BlockSpec((tile, wide), lambda g: (g + part * steps, 0))

    return run_kernel(
        partial(split_kernel, len(arrays), parts),
        steps,
        [(SMEM, own.astype(jnp.int32).reshape(1))]
        + [(block_at(part), array) for part in range(parts) for array in arrays],
        [(block_at(0), (size, wide), BF16)] * parts,
        [],
    )


def merge(pieces, starts, rows):
    return run_kernel(
        partial(merge_kernel, len(pieces)),
        1,
        [(SMEM, jnp.stack(starts).astype(jnp.int32))] + [(ANY, piece) for piece in pieces],
        [(whole((rows, pieces[0].shape[1])), (rows, pieces[0].shape[1]), BF16)],
        [pltpu.SemaphoreType.DMA((len(pieces),))],
    )[0]


class Fetch:
    def __init__(self, array, axis):
        size = array.shape[axis] // 2
        start = lax.axis_index("dp") % 2 * size
        self.half = lax.dynamic_slice_in_dim(array, start, size, axis=axis)
        self.group = lax.axis_size("heads")
        self.slots = {0: [array]}
        self.sent = {}

    def core(self, slot, *others):
        pieces = after(self.slots[slot], *others)
        self.slots[slot + 1] = [swap(piece, "heads", 1) for piece in pieces]

    def send(self, *others):
        (self.half,) = after([self.half], *others)
        for slot in range(2, self.group, 2):
            bit = low_bit(slot)
            if slot == bit:
                self.sent[slot] = swap(self.half, "heads", bit)

    def share(self, *others):
        for slot in range(2, self.group, 2):
            bit = low_bit(slot)
            if slot == bit:
                (came,) = after([self.sent[slot]], *others)
            else:
                came = swap(self.slots[slot - bit][0], "heads", bit)
            self.slots[slot] = [came, swap(came, "dp", 1)]

    def cores(self, first, last, *others):
        for slot in range(first, last, 2):
            self.core(slot, *others)

    def listed(self):
        return [self.slots[slot] for slot in range(self.group)]


def flat(slots):
    return [piece for pieces in slots for piece in pieces]


class GroupSum:
    def __init__(self):
        self.arrived = {}

    def put(self, slot, array, *others):
        arrays = [array] + self.arrived.pop(slot, [])
        if slot == 0:
            return arrays
        total = add_arrays(after(arrays, *others)) if len(arrays) > 1 else array
        bit = low_bit(slot)
        self.arrived.setdefault(slot - bit, []).append(swap(total, "heads", bit))
        return total


class DataSum:
    def __init__(self, arrays, bits, merged=False):
        self.merged = merged
        self.arrays = list(arrays)
        self.bits = list(bits)
        self.halved = []
        self.rows = arrays[0].shape[0]
        self.pieces = None

    def step(self, *others):
        arrays = after(self.arrays, *others)
        if not self.bits:
            total = add_arrays(arrays)
            self.gather(total)
            return total
        bit = self.bits.pop(0)
        keep, send = add_and_split(arrays, lax.axis_index("dp") // bit % 2, 2)
        self.halved.append(bit)
        self.arrays = [keep, swap(send, "dp", bit)]
        return keep

    def gather(self, total):
        self.pieces = {0: total}
        for bit in self.halved[: 0 if self.merged else None : -1]:
            for mask, piece in list(self.pieces.items()):
                self.pieces[mask | bit] = swap(piece, "dp", bit)

    def half(self, *others):
        starts = [start % (self.rows // 2) for start in self.starts()]
        return merge(after(self.pieces.values(), *others), starts, self.rows // 2)

    def starts(self):
        own = lax.axis_index("dp")
        return [
            sum(
                (own ^ mask) // bit % 2 * (self.rows >> (at + 1))
                for at, bit in enumerate(self.halved)
            )
            for mask in self.pieces
        ]


def axis_bits(axis):
    size = lax.axis_size(axis)
    return [1 << at for at in range(size.bit_length() - 1)]


def on_device(
    noisy_mel,
    cond_mel,
    text_embed,
    time_embed,
    lengths,
    spans,
    dw_kernel,
    text_bias,
    text_gain,
    text_hidden,
    pw_in,
    pw_out,
    in_proj,
    frame_bias,
    mod_weight,
    mod_bias,
    qkv_weight,
    qkv_bias,
    out_weight,
    ff_in,
    ff_in_bias,
    ff_out,
    cotangent,
):
    group = lax.axis_size("heads")
    own = lax.axis_index("heads")
    own_data = lax.axis_index("dp")
    rows = text_embed.shape[0]
    model_width = in_proj.shape[1]
    width = qkv_weight.shape[2]
    units = ff_in.shape[1]
    block = min(128, width)
    parts = group // 2
    full = (rows, model_width)

    fetches = [Fetch(qkv_weight, 1), Fetch(out_weight, 0), Fetch(ff_in, 0), Fetch(ff_out, 0)]
    for fetch in fetches[:2]:
        fetch.send()
        fetch.core(0)

    position = jnp.arange(rows, dtype=jnp.int32)
    inside = (position >= spans[0, 0]) & (position < spans[0, 1])
    keep = jnp.where(inside, 0.0, 1.0).astype(F32)[:, None]
    count = lax.dynamic_slice_in_dim(lengths, own, 1)
    lane = jnp.arange(block, dtype=jnp.int32)
    pair = ((lane % HD) // 2).astype(F32)
    angle = position.astype(F32)[:, None] * (10000.0 ** (-2.0 * pair / HD))[None, :]
    cosine = jnp.cos(angle)
    sine = jnp.sin(angle) * jnp.where(lane % 2 == 0, -1.0, 1.0)[None, :]

    cond_low = (cond_mel.astype(F32) * keep).astype(BF16)
    mel = jnp.concatenate([noisy_mel, cond_low], axis=1)
    mels = mel.shape[1]
    text_width = text_embed.shape[1]
    gain = text_gain[None, :]

    def block_of(array):
        return (whole(array.shape), array)

    normed_text, pre_act, energy, mixed_text, refined, state_zero = run_kernel(
        text_forward,
        1,
        [
            block_of(member)
            for member in (
                text_embed,
                mel,
                dw_kernel,
                text_bias,
                gain,
                text_hidden,
                pw_in,
                pw_out,
                in_proj,
                frame_bias,
            )
        ],
        [
            (whole(shape), shape, kind)
            for shape, kind in (
                ((rows, text_width), BF16),
                ((rows, pw_in.shape[1]), F32),
                ((8, pw_in.shape[1]), F32),
                ((rows, pw_in.shape[1]), BF16),
                ((rows, text_width), BF16),
                (full, F32),
            )
        ],
        [pltpu.VMEM((rows + 16, text_width), F32), pltpu.VMEM((rows, pw_in.shape[1]), F32)],
    )

    def semaphores(number, pieces=2):
        shape = (number, pieces) if pieces > 1 else (number,)
        return pltpu.SemaphoreType.DMA(shape)

    def attn_buffers(number, pieces=2):
        return [
            pltpu.VMEM((number, 3, model_width, width), BF16),
            pltpu.VMEM((number, width, model_width), BF16),
            semaphores(number, pieces),
            semaphores(number, pieces),
        ]

    def ffn_buffers(number, pieces=2):
        return [
            pltpu.VMEM((number, model_width, units), BF16),
            pltpu.VMEM((number, units, model_width), BF16),
            semaphores(number, pieces),
            semaphores(number, pieces),
        ]

    half_index = (own_data % 2).astype(jnp.int32).reshape(1)

    def pieces_of(slots):
        return tuple(len(pieces) for pieces in slots)

    (time_late,) = after([time_embed], state_zero)
    time_rows = time_late.astype(F32)
    activated, silu_back = jax.vjp(jax.nn.silu, time_rows)
    activated_low = activated.astype(BF16)
    modulation = (mm(activated_low, mod_weight) + mod_bias).astype(BF16)
    biases = jnp.concatenate([qkv_bias.reshape(-1), ff_in_bias])
    riders = jnp.broadcast_to(biases[None, :], (group, biases.size))
    sent = jnp.concatenate([modulation, riders], axis=1)
    came = lax.all_to_all(sent, "heads", split_axis=0, concat_axis=1, tiled=True)
    came = came.reshape(group, sent.shape[1]).astype(F32)
    mod_rows = came[:, : modulation.shape[1]].reshape(6, model_width)
    slot_owner = jnp.bitwise_xor(jnp.arange(group, dtype=jnp.int32), own)
    biases_all = jnp.take(came[:, modulation.shape[1] :], slot_owner, axis=0)
    qkv_bias_all = biases_all[:, : 3 * width].reshape(group, 3, width)
    up_bias_all = biases_all[:, 3 * width :].reshape(group, 1, units)

    for fetch in fetches[2:]:
        fetch.send(came)
    for fetch in fetches[:2]:
        fetch.share()
        fetch.cores(2, parts)
    (mod_rows,) = after([mod_rows], *[fetch.sent[2] for fetch in fetches[:2]])
    kept = []
    for turn in range(2):
        first, last = turn == 0, turn == 1
        if last:
            for fetch in fetches[:2]:
                fetch.cores(parts, group, normed)
            for fetch in fetches[2:]:
                fetch.share(normed)
                fetch.core(0, normed)
            (before,) = after([before], *[fetch.slots[2][0] for fetch in fetches[2:]])
        chosen = range(turn * parts, (turn + 1) * parts)
        qkv_here = [fetches[0].slots[slot] for slot in chosen]
        out_here = [fetches[1].slots[slot] for slot in chosen]
        inputs = [
            (SMEM, count),
            (SMEM, half_index),
            (whole(full), state_zero),
            (whole((6, model_width)), mod_rows),
            (held((3, width)), qkv_bias_all[chosen[0] : chosen[-1] + 1]),
            (whole((3, model_width)), frame_bias),
            (whole((rows, block)), cosine),
            (whole((rows, block)), sine),
        ]
        inputs += [(ANY, member) for member in flat(qkv_here) + flat(out_here)]
        if not first:
            inputs += [(whole(full), normed), (whole(full), before)]
        outputs = [(held((rows, width)), (parts, rows, width), BF16)] * 4
        outputs += [(held((8, rows)), (parts, 8, rows), F32)]
        if first:
            outputs += [(whole(full), full, BF16)]
        outputs += [(whole(full), full, F32)]
        if last:
            outputs += [(whole(full), full, F32), (whole(full), full, BF16)]
        results = run_kernel(
            partial(attention_forward, pieces_of(qkv_here), first, last),
            parts,
            inputs,
            outputs,
            attn_buffers(parts) + ([pltpu.VMEM(full, F32)] if last else []),
        )
        kept.append(results[:5])
        if first:
            normed, before = results[5:]
        else:
            branch, state_one, ffn_in = results[5:]

    qkv_all, out_all = fetches[0].listed(), fetches[1].listed()
    fetches[2].cores(2, group, ffn_in)
    fetches[3].cores(2, group, ffn_in)
    up_all, down_all = fetches[2].listed()[::-1], fetches[3].listed()[::-1]
    inputs = [
        (SMEM, half_index),
        (whole(full), cotangent),
        (whole(full), state_one),
        (whole(full), branch),
        (whole(full), ffn_in),
        (whole((6, model_width)), mod_rows),
        (held((1, units), group), up_bias_all),
        (whole((3, model_width)), frame_bias),
    ]
    inputs += [(ANY, member) for member in flat(up_all) + flat(down_all)]
    merged = (2 * units, model_width)
    outputs = [(held((1, units), group), (group, 1, units), F32)]
    outputs += [(whole((8, model_width)), (8, model_width), F32)]
    outputs += [(ANY, merged, BF16)] * group
    outputs += [(whole(full), full, BF16)] * 2 + [(whole(full), full, F32)]
    outputs += [(whole(full), full, BF16)]
    results = run_kernel(
        partial(feed_forward, pieces_of(up_all), True, True),
        group,
        inputs,
        outputs,
        [
            pltpu.VMEM((group, model_width, units), BF16),
            pltpu.VMEM((group, units, model_width), BF16),
            semaphores(group),
            semaphores(group),
            pltpu.VMEM((group,) + merged, BF16),
            semaphores(group, 1),
            pltpu.VMEM((model_width, rows), BF16),
            pltpu.VMEM((rows, units), BF16),
            pltpu.VMEM((rows, units), BF16),
        ]
        + [pltpu.VMEM(full, F32)] * 2,
    )
    grad_up_bias, ffn_sums = results[:2]
    output, grad_one, grad_attn = results[3 + group :]
    ffn_grads = results[2 : 2 + group][::-1]

    attn_grads = []
    merged = (4 * width, model_width)
    qkv_bias_parts = []
    for turn in range(2):
        first, last = turn == 0, turn == 1
        chosen = [group - 1 - turn * parts - at for at in range(parts)]
        inputs = [
            (SMEM, count),
            (SMEM, half_index),
            (whole(full), grad_attn),
            (whole(full), normed),
            (whole((6, model_width)), mod_rows),
            (whole((rows, block)), cosine),
            (whole((rows, block)), sine),
        ]
        inputs += [(held((rows, width), parts), member) for member in kept[1 - turn][:4]]
        inputs += [(held((8, rows), parts), kept[1 - turn][4])]
        inputs += [(ANY, member) for member in flat([qkv_all[slot] for slot in chosen])]
        inputs += [(ANY, member) for member in flat([out_all[slot] for slot in chosen])]
        if not first:
            inputs += [(whole(full), back)]
        if last:
            inputs += [(whole(full), state_zero), (whole(full), grad_one)]
        outputs = [(held((3, width), parts), (parts, 3, width), F32)]
        outputs += [(ANY, merged, BF16)] * parts
        if last:
            outputs += [(whole(full), full, BF16), (whole((8, model_width)), (8, model_width), F32)]
        else:
            outputs += [(whole(full), full, F32)]
        results = run_kernel(
            partial(attention_backward, pieces_of([qkv_all[slot] for slot in chosen]), first, last),
            parts,
            inputs,
            outputs,
            attn_buffers(parts)
            + [pltpu.VMEM((parts,) + merged, BF16), semaphores(parts, 1)]
            + [pltpu.VMEM((model_width, rows), BF16), pltpu.VMEM((rows, width), BF16)]
            + ([pltpu.VMEM(full, F32)] if last else []),
        )
        qkv_bias_parts.append(results[0])
        attn_grads = list(results[1 : 1 + parts])[::-1] + attn_grads
        if first:
            back = results[1 + parts]
            ffn_sum = GroupSum()
            token = back
            for slot in range(group - 1, 0, -1):
                total = ffn_sum.put(slot, ffn_grads[slot], token)
                if slot % 2 == 0:
                    token = total
            (back,) = after([back], token)
        else:
            grad_zero, attn_sums = results[1 + parts :]
    token = grad_zero
    attn_sum = GroupSum()
    for slot in range(group - 1, 0, -1):
        total = attn_sum.put(slot, attn_grads[slot], token)
        if slot % 2 == 0:
            token = total
    (grad_zero,) = after([grad_zero], token)

    data = lax.axis_size("dp")
    stack_rows = 3 * text_width + mels
    stack_rows += -stack_rows % 16 + small_rows(group) + 8 * group * data
    stack_rows += -stack_rows % (16 * group * data)
    own_index = jnp.stack([own, own_data * group + own]).astype(jnp.int32)
    own_active = lax.dynamic_index_in_dim(activated_low, own, 0)
    results = run_kernel(
        partial(text_backward, group),
        1,
        [(SMEM, own_index)]
        + [
            block_of(member)
            for member in (
                grad_zero,
                text_embed,
                mel,
                refined,
                mixed_text,
                normed_text,
                pre_act,
                energy,
                dw_kernel,
                text_bias,
                gain,
                text_hidden,
                pw_in,
                pw_out,
                in_proj,
                attn_sums,
                ffn_sums,
                qkv_bias_parts[0],
                qkv_bias_parts[1],
                grad_up_bias,
                own_active,
            )
        ],
        [
            (whole((rows, text_width)), (rows, text_width), F32),
            (whole((6, model_width)), (6, model_width), BF16),
        ]
        + [(ANY, (stack_rows // group, model_width), BF16)] * group,
        [
            pltpu.VMEM((stack_rows, model_width), BF16),
            semaphores(group, 1),
            pltpu.VMEM((rows + 16, text_width), F32),
            pltpu.VMEM((rows + 16, text_width), F32),
            pltpu.VMEM((rows, text_width), F32),
            pltpu.VMEM((rows, text_width), BF16),
            pltpu.VMEM((rows, pw_in.shape[1]), F32),
            pltpu.VMEM((rows, pw_in.shape[1]), BF16),
            pltpu.VMEM((rows, text_width), F32),
            pltpu.VMEM((small_rows(group), model_width), F32),
        ],
    )
    grad_text, grad_mod = results[:2]
    def unpack(kernel, data, first, second, *others):
        pieces = after(data.pieces.values(), *others)
        return run_kernel(
            partial(kernel, len(pieces)),
            1,
            [(SMEM, jnp.stack(data.starts()).astype(jnp.int32))]
            + [(ANY, member) for member in pieces],
            [(whole(first.shape), first.shape, F32), (whole(second.shape), second.shape, F32)],
            [pltpu.VMEM((data.rows, model_width), BF16), semaphores(len(pieces), 1)],
        )

    bits = axis_bits("dp")
    ffn_data = DataSum(ffn_sum.put(0, ffn_grads[0]), bits)
    token = ffn_data.step(grad_mod)
    text_sum = GroupSum()
    for slot in range(group - 1, 0, -1):
        total = text_sum.put(slot, results[2 + slot], token)
        if slot % 2 == 0:
            token = total
    attn_data = DataSum(attn_sum.put(0, attn_grads[0]), bits)
    text_data = DataSum(text_sum.put(0, results[2]), bits, merged=True)
    steps = [(1 + (at - 1) / len(bits), ffn_data) for at in range(1, len(bits))]
    steps.append((2, ffn_data))
    for at in range(len(bits) + 1):
        steps.append((at + 1.9 if at else 1.9 - 0.1, attn_data))
        steps.append((at + 2.25, text_data))
    steps.sort(key=lambda step: step[0])
    columns = mod_weight.shape[1]
    grad_time = None
    last_attn = max(at for at, member in steps if member is attn_data)
    for at, member in steps:
        if at == last_attn:
            weight_up, weight_down = unpack(ffn_unpack, ffn_data, ff_in, ff_out, token)
            token = member.step(token, weight_up)
        elif at > len(bits) and member is attn_data and grad_time is None:
            (grad_mod,) = after([grad_mod], token)
            grad_mod = grad_mod.reshape(1, group * columns)
            grad_cols = lax.all_to_all(grad_mod, "heads", split_axis=1, concat_axis=0, tiled=True)
            (grad_time,) = silu_back(inner_cols(grad_cols, mod_weight))
            token = member.step(token, grad_time)
        elif at == steps[-1][0]:
            (grad_time,) = after([grad_time], token)
            grad_time = jnp.broadcast_to(grad_time.astype(BF16), (group,) + grad_time.shape)
            grad_time = lax.all_to_all(grad_time, "heads", split_axis=0, concat_axis=0)
            grad_time = jnp.sum(grad_time.astype(F32), axis=0)
            token = member.step(token, grad_time)
        else:
            token = member.step(token)

    text_half = text_data.half(weight_up, *list(attn_data.pieces.values())[1:])
    weight_qkv, weight_out = unpack(attn_unpack, attn_data, qkv_weight, out_weight, text_half)
    text_halves = {0: [text_half]}
    for slot in range(2, group, 2):
        bit = low_bit(slot)
        text_halves[slot] = [swap(text_halves[slot - bit][0], "heads", bit)]
        text_halves[slot] = list(after(text_halves[slot], weight_qkv))
    for slot in range(0, group, 2):
        text_halves[slot].append(swap(text_halves[slot][0], "dp", 1))
        text_halves[slot + 1] = [swap(piece, "heads", 1) for piece in text_halves[slot]]
    slot_rows = stack_rows // group
    text_pieces, text_starts = [], []
    for slot, pieces in text_halves.items():
        for which, piece in enumerate(pieces):
            text_pieces.append(piece)
            text_starts.append(
                slot_owner[slot] * slot_rows + ((own_data + which) % 2) * (slot_rows // 2)
            )
    unpacked = (
        in_proj.shape,
        pw_in.shape,
        pw_out.shape,
        dw_kernel.shape,
        text_bias.shape,
        gain.shape,
        text_hidden.shape,
        frame_bias.shape,
        (3, width),
        (1, units),
    )
    mods_shape = (8 * group * data, model_width)
    unpacked = run_kernel(
        partial(text_unpack, len(text_pieces), group),
        1,
        [(SMEM, jnp.stack(text_starts).astype(jnp.int32)), (SMEM, own_index)]
        + [(ANY, member) for member in text_pieces],
        [(whole(shape), shape, F32) for shape in unpacked]
        + [(whole(mods_shape), mods_shape, BF16)],
        [
            pltpu.VMEM((stack_rows, model_width), BF16),
            semaphores(len(text_pieces), 1),
            pltpu.VMEM((small_rows(group), model_width), F32),
        ],
    )
    seen = unpacked[10].reshape(group * data, 8, model_width)
    grad_mod_all = seen[:, :6].reshape(group * data, 6 * model_width)
    grad_mod_all = lax.dynamic_slice_in_dim(grad_mod_all, own * columns, columns, axis=1)
    grad_mod_weight = inner_rows(seen[:, 6], grad_mod_all)
    grad_mod_bias = jnp.sum(grad_mod_all.astype(F32), axis=0)
    return (
        output,
        grad_text,
        grad_time,
        unpacked[3],
        unpacked[4],
        unpacked[5][0],
        unpacked[6],
        unpacked[1],
        unpacked[2],
        unpacked[0],
        unpacked[7],
        grad_mod_weight,
        grad_mod_bias,
        weight_qkv,
        unpacked[8],
        weight_out,
        weight_up,
        unpacked[9][0],
        weight_down,
    )


def solution(mesh):
    in_specs = (
        P(("dp", "heads"), None),
        P(("dp", "heads"), None),
        P(("dp", "heads"), None),
        P("dp", None),
        P("dp"),
        P(("dp", "heads"), None),
        P(),
        P(),
        P(),
        P(),
        P(),
        P(),
        P(),
        P(),
        P(None, "heads"),
        P("heads"),
        P(None, None, "heads"),
        P(None, "heads"),
        P("heads", None),
        P(None, "heads"),
        P("heads"),
        P("heads", None),
        P(("dp", "heads"), None),
    )
    out_specs = (
        P(("dp", "heads"), None),
        P(("dp", "heads"), None),
        P("dp", None),
        P(),
        P(),
        P(),
        P(),
        P(),
        P(),
        P(),
        P(),
        P(None, "heads"),
        P("heads"),
        P(None, None, "heads"),
        P(None, "heads"),
        P("heads", None),
        P(None, "heads"),
        P("heads"),
        P("heads", None),
    )
    return jax.shard_map(
        on_device, mesh=mesh, in_specs=in_specs, out_specs=out_specs, check_vma=False
    )
```

```python
from functools import partial

import jax
import jax.numpy as jnp
from jax import lax
from jax.experimental import pallas as pl
from jax.experimental.pallas import tpu as pltpu
from jax.sharding import PartitionSpec as P

HD = 64


def inner_rows(left, right):
    return lax.dot_general(
        left, right, (((0,), (0,)), ((), ())), preferred_element_type=jnp.float32
    )


def inner_cols(left, right):
    return lax.dot_general(
        left, right, (((1,), (1,)), ((), ())), preferred_element_type=jnp.float32
    )


F32 = jnp.float32
BF16 = jnp.bfloat16
CHUNK = 64
SPAN = 256
VMEM = 60 * 1024 * 1024


def mm(left, right):
    return jnp.dot(left, right, preferred_element_type=F32)


def fold(values):
    return jnp.sum(values.reshape(values.shape[0] // 8, 8, values.shape[1]), axis=0)


def norm_parts(values):
    mean = jnp.mean(values, axis=-1, keepdims=True)
    centred = values - mean
    root = lax.rsqrt(jnp.mean(centred * centred, axis=-1, keepdims=True) + 1e-06)
    return centred * root, root


def norm_pull(grad, scale, xhat, root):
    entry = grad * (1.0 + scale)
    mean = jnp.mean(entry, axis=-1, keepdims=True)
    along = jnp.mean(entry * xhat, axis=-1, keepdims=True)
    return root * (entry - mean - xhat * along)


def swap_pairs(block):
    width = block.shape[1]
    lane = lax.broadcasted_iota(jnp.int32, block.shape, 1)
    if width % 128 == 0:
        after = pltpu.roll(block, width - 1, 1)
        before = pltpu.roll(block, 1, 1)
    else:
        after = jnp.concatenate([block[:, 1:], block[:, :1]], axis=1)
        before = jnp.concatenate([block[:, width - 1 :], block[:, : width - 1]], axis=1)
    return jnp.where(lane % 2 == 0, after, before)


def head_lanes(block, head):
    if block.shape[1] == HD:
        return block
    lane = lax.broadcasted_iota(jnp.int32, block.shape, 1)
    return jnp.where((lane >= head * HD) & (lane < (head + 1) * HD), block, jnp.zeros_like(block))


def slot_copies(pieces, target, sems, at, axis, half):
    if len(pieces) == 1:
        return [pltpu.make_async_copy(pieces[0], target.at[at], sems.at[at, 0])]
    copies = []
    for which, piece in enumerate(pieces):
        size = piece.shape[axis]
        start = pl.multiple_of((half if which == 0 else 1 - half) * size, size)
        index = (at,) + (slice(None),) * axis + (pl.ds(start, size),)
        copies.append(pltpu.make_async_copy(piece, target.at[index], sems.at[at, which]))
    return copies


def start_all(step, copies):
    @pl.when(step == 0)
    def _():
        for members in copies:
            for copy in members:
                copy.start()


def wait_own(step, copies):
    for at, members in enumerate(copies):

        @pl.when(step == at)
        def _(members=members):
            for copy in members:
                copy.wait()


def send_own(step, results):
    for at, members in enumerate(results):

        @pl.when(step == at)
        def _(members=members):
            for copy in members:
                copy.start()


def wait_all(step, results):
    @pl.when(step == len(results) - 1)
    def _():
        for members in results:
            for copy in members:
                copy.wait()


def attention_forward(pieces, first, last, *refs):
    parts = len(pieces)
    refs = list(refs)

    def take(count=1):
        taken = [refs.pop(0) for _ in range(count)]
        return taken[0] if count == 1 else taken

    count_ref, half_ref, state_ref, mod_ref, bias_ref, frame_ref, cosine_ref, sine_ref = take(8)
    weights = [[take() for _ in range(number)] for number in pieces]
    outs = [[take() for _ in range(number)] for number in pieces]
    if not first:
        normed_ref, before_ref = take(2)
    query_ref, key_ref, value_ref, attended_ref, log_ref = take(5)
    if first:
        normed_ref = take()
    if last:
        branch_ref, one_ref, ffn_ref = take(3)
    else:
        total_ref = take()
    weight_ref, out_ref, weight_sem, out_sem = take(4)
    if last:
        total_ref = take()
    step = pl.program_id(0)
    rows = state_ref.shape[0]
    width = weight_ref.shape[3]
    block = cosine_ref.shape[1]
    count = count_ref[0]
    half = half_ref[0]
    copies = [
        slot_copies(weights[at], weight_ref, weight_sem, at, 1, half)
        + slot_copies(outs[at], out_ref, out_sem, at, 0, half)
        for at in range(parts)
    ]
    start_all(step, copies)

    @pl.when(step == 0)
    def _():
        if first:

            def chunk(at, carry):
                here = pl.ds(at * CHUNK, CHUNK)
                xhat, _ = norm_parts(state_ref[here, :])
                normed_ref[here, :] = (xhat * (1.0 + mod_ref[1:2, :]) + mod_ref[0:1, :]).astype(
                    BF16
                )
                return carry

            lax.fori_loop(0, rows // CHUNK, chunk, 0)
            total_ref[...] = jnp.zeros_like(total_ref)
        else:
            total_ref[...] = before_ref[...]

    wait_own(step, copies)
    normed = normed_ref[...]
    cosine = cosine_ref[...]
    sine = sine_ref[...]
    logs = jnp.zeros((rows, 128), F32)
    lane = lax.broadcasted_iota(jnp.int32, (rows, 128), 1)
    query_lin = mm(normed, weight_ref[step, 0]) + bias_ref[0, 0:1, :]
    key_lin = mm(normed, weight_ref[step, 1]) + bias_ref[0, 1:2, :]
    value_ref[0] = (mm(normed, weight_ref[step, 2]) + bias_ref[0, 2:3, :]).astype(BF16)
    for at in range(width // block):
        cut = slice(at * block, (at + 1) * block)
        piece = query_lin[:, cut]
        turned = piece * cosine + swap_pairs(piece) * sine
        query_ref[0, :, cut] = (turned * HD**-0.5).astype(BF16)
        piece = key_lin[:, cut]
        key_ref[0, :, cut] = (piece * cosine + swap_pairs(piece) * sine).astype(BF16)
    live = lax.broadcasted_iota(jnp.int32, (1, rows), 1) < count
    for at in range(width // block):
        cut = slice(at * block, (at + 1) * block)
        keys = key_ref[0, :, cut]
        values = value_ref[0, :, cut]
        results = [None] * (rows // SPAN)
        pieces = [[] for _ in range(rows // SPAN)]
        for head in range(block // HD):
            own_values = head_lanes(values, head)
            for part in range(rows // SPAN):
                queries = head_lanes(query_ref[0, part * SPAN : (part + 1) * SPAN, cut], head)
                scores = jnp.where(live, inner_cols(queries, keys), -1e30)
                top = jnp.max(scores, axis=1, keepdims=True)
                expo = jnp.exp(scores - top)
                total = jnp.sum(expo, axis=1, keepdims=True)
                weights = (expo * (1.0 / total)).astype(BF16)
                result = mm(weights, own_values)
                results[part] = result if head == 0 else results[part] + result
                pieces[part].append(top + jnp.log(total))
        for head in range(block // HD):
            column = jnp.concatenate([pieces[part][head] for part in range(rows // SPAN)], axis=0)
            logs = jnp.where(lane == at * (block // HD) + head, column, logs)
        for part in range(rows // SPAN):
            place = part * SPAN + lax.broadcasted_iota(jnp.int32, (SPAN, block), 0)
            attended_ref[0, part * SPAN : (part + 1) * SPAN, cut] = jnp.where(
                place < count, results[part], 0.0
            ).astype(BF16)
    log_ref[0] = jnp.transpose(logs)[0:8, :]
    total_ref[...] += mm(attended_ref[0], out_ref[step])

    if last:

        @pl.when(step == parts - 1)
        def _():
            def chunk(at, carry):
                here = pl.ds(at * CHUNK, CHUNK)
                branch = total_ref[here, :] + frame_ref[1:2, :]
                branch_ref[here, :] = branch
                state_one = state_ref[here, :] + mod_ref[2:3, :] * branch
                one_ref[here, :] = state_one
                xhat, _ = norm_parts(state_one)
                ffn_ref[here, :] = (xhat * (1.0 + mod_ref[4:5, :]) + mod_ref[3:4, :]).astype(BF16)
                return carry

            lax.fori_loop(0, rows // CHUNK, chunk, 0)


def lay(target_ref, at, start, value):
    model, width = value.shape
    for block in range(model // width):
        target_ref[at, start : start + width, block * width : (block + 1) * width] = value[
            block * width : (block + 1) * width, :
        ]


def feed_forward(pieces, first, last, *refs):
    parts = len(pieces)
    refs = list(refs)

    def take(count=1):
        taken = [refs.pop(0) for _ in range(count)]
        return taken[0] if count == 1 else taken

    half_ref, cotangent_ref, one_ref, branch_ref, source_ref, mod_ref, bias_ref, frame_ref = take(8)
    ups = [[take() for _ in range(number)] for number in pieces]
    downs = [[take() for _ in range(number)] for number in pieces]
    if not first:
        grad_ref, total_in_ref, back_in_ref = take(3)
    grad_bias_ref, sums_ref = take(2)
    grads = [take() for _ in range(parts)]
    if first:
        grad_ref = take()
    if last:
        output_ref, grad_one_ref, grad_attn_ref = take(3)
    else:
        total_ref, back_ref = take(2)
    up_ref, down_ref, up_sem, down_sem = take(4)
    grads_ref, grads_sem = take(2)
    turned_ref, hidden_ref, pre_ref = take(3)
    if last:
        total_ref, back_ref = take(2)
    step = pl.program_id(0)
    rows, wide = one_ref.shape
    inner = 0.7978845608028654
    cubic = 0.044715
    half = half_ref[0]
    copies = [
        slot_copies(ups[at], up_ref, up_sem, at, 0, half)
        + slot_copies(downs[at], down_ref, down_sem, at, 0, half)
        for at in range(parts)
    ]
    results = [
        (pltpu.make_async_copy(grads_ref.at[at], grads[at], grads_sem.at[at]),)
        for at in range(parts)
    ]
    start_all(step, copies)

    @pl.when(step == 0)
    def _():
        if first:

            def chunk(at, carry):
                here = pl.ds(at * CHUNK, CHUNK)
                grad = cotangent_ref[here, :].astype(F32) * mod_ref[5:6, :]
                grad_ref[here, :] = grad.astype(BF16)
                return carry + fold(grad)

            lanes = lax.fori_loop(0, rows // CHUNK, chunk, jnp.zeros((8, wide), F32))
            sums_ref[0:1, :] = jnp.sum(lanes, axis=0, keepdims=True)
            total_ref[...] = jnp.zeros_like(total_ref)
            back_ref[...] = jnp.zeros_like(back_ref)
        else:
            total_ref[...] = total_in_ref[...]
            back_ref[...] = back_in_ref[...]
        turned_ref[...] = jnp.transpose(source_ref[...])

    wait_own(step, copies)
    up = up_ref[step]
    down = down_ref[step]
    lanes = jnp.zeros((8, up.shape[1]), F32)
    for part in range(rows // SPAN):
        here = slice(part * SPAN, (part + 1) * SPAN)
        pre = mm(source_ref[here, :], up) + bias_ref[0]
        grad_hidden = inner_cols(grad_ref[here, :], down)
        square = pre * pre
        bend = jnp.tanh(pre * (inner + inner * cubic * square))
        half = 0.5 * (1.0 + bend)
        hidden = (pre * half).astype(BF16)
        slope = half + 0.5 * pre * (1.0 - bend * bend) * (inner + 3.0 * inner * cubic * square)
        grad_pre = grad_hidden * slope
        lanes = lanes + fold(grad_pre)
        grad_pre = grad_pre.astype(BF16)
        hidden_ref[here, :] = hidden
        pre_ref[here, :] = grad_pre
        total_ref[here, :] += mm(hidden, down)
        back_ref[here, :] += inner_cols(grad_pre, up)
    grad_bias_ref[0] = jnp.sum(lanes, axis=0, keepdims=True)
    width = up_ref.shape[2]
    grads_ref[step, width:, :] = inner_rows(hidden_ref[...], grad_ref[...]).astype(BF16)
    lay(grads_ref, step, 0, mm(turned_ref[...], pre_ref[...]).astype(BF16))
    send_own(step, results)

    if last:

        @pl.when(step == parts - 1)
        def _():
            def chunk(at, carry):
                gate_ffn, scale_ffn, shift_ffn, bias_attn, gate_attn = carry
                here = pl.ds(at * CHUNK, CHUNK)
                branch = total_ref[here, :] + frame_ref[2:3, :]
                state_one = one_ref[here, :]
                output_ref[here, :] = (state_one + mod_ref[5:6, :] * branch).astype(BF16)
                cotangent = cotangent_ref[here, :].astype(F32)
                xhat, root = norm_parts(state_one)
                back = back_ref[here, :]
                grad_one = cotangent + norm_pull(back, mod_ref[4:5, :], xhat, root)
                grad_one_ref[here, :] = grad_one
                grad_attn = grad_one * mod_ref[2:3, :]
                grad_attn_ref[here, :] = grad_attn.astype(BF16)
                return (
                    gate_ffn + fold(cotangent * branch),
                    scale_ffn + fold(back * xhat),
                    shift_ffn + fold(back),
                    bias_attn + fold(grad_attn),
                    gate_attn + fold(grad_one * branch_ref[here, :]),
                )

            start = tuple(jnp.zeros((8, wide), F32) for _ in range(5))
            lanes = lax.fori_loop(0, rows // CHUNK, chunk, start)
            for at, member in enumerate(lanes):
                sums_ref[at + 1 : at + 2, :] = jnp.sum(member, axis=0, keepdims=True)

    wait_all(step, results)


def attention_backward(pieces, first, last, *refs):
    parts = len(pieces)
    refs = list(refs)

    def take(count=1):
        taken = [refs.pop(0) for _ in range(count)]
        return taken[0] if count == 1 else taken

    count_ref, half_ref, grad_attn_ref, normed_ref, mod_ref, cosine_ref, sine_ref = take(7)
    query_ref, key_ref, value_ref, attended_ref, log_ref = take(5)
    weights = [[take() for _ in range(number)] for number in pieces]
    outs = [[take() for _ in range(number)] for number in pieces]
    if not first:
        before_ref = take()
    if last:
        state_ref, grad_one_ref = take(2)
    grad_bias_ref = take()
    grads = [take() for _ in range(parts)]
    if last:
        grad_zero_ref, sums_ref = take(2)
    else:
        back_ref = take()
    weight_ref, out_ref, weight_sem, out_sem = take(4)
    grads_ref, grads_sem = take(2)
    turned_ref, item_ref = take(2)
    if last:
        back_ref = take()
    step = pl.program_id(0)
    rows, wide = normed_ref.shape
    width = weight_ref.shape[3]
    block = cosine_ref.shape[1]
    count = count_ref[0]
    half = half_ref[0]
    copies = [
        slot_copies(weights[at], weight_ref, weight_sem, at, 1, half)
        + slot_copies(outs[at], out_ref, out_sem, at, 0, half)
        for at in range(parts)
    ]
    results = [
        (pltpu.make_async_copy(grads_ref.at[at], grads[at], grads_sem.at[at]),)
        for at in range(parts)
    ]
    start_all(step, copies)

    @pl.when(step == 0)
    def _():
        turned_ref[...] = jnp.transpose(normed_ref[...])
        back_ref[...] = jnp.zeros_like(back_ref) if first else before_ref[...]

    wait_own(step, copies)
    grad_attn = grad_attn_ref[...]
    place = lax.broadcasted_iota(jnp.int32, (rows, width), 0)
    item_ref[...] = jnp.where(place < count, inner_cols(grad_attn, out_ref[step]), 0.0).astype(BF16)
    grads_ref[step, 3 * width :, :] = inner_rows(attended_ref[0], grad_attn).astype(BF16)
    cosine = cosine_ref[...]
    sine = sine_ref[...]
    live = lax.broadcasted_iota(jnp.int32, (rows, 1), 0) < count
    linear = [[], [], []]
    for at in range(width // block):
        cut = slice(at * block, (at + 1) * block)
        keys = key_ref[0, :, cut]
        values = value_ref[0, :, cut]
        keys_turned = jnp.transpose(keys)
        grad_keys = jnp.zeros((rows, block), F32)
        grad_values = jnp.zeros((rows, block), F32)
        grad_queries = [[] for _ in range(rows // SPAN)]
        for head in range(block // HD):
            index = at * (block // HD) + head
            for part in range(rows // SPAN):
                here = slice(part * SPAN, (part + 1) * SPAN)
                queries = head_lanes(query_ref[0, here, cut], head)
                items = head_lanes(item_ref[here, cut], head)
                scores = jnp.where(live, inner_cols(keys, queries), -1e30)
                weights = jnp.exp(scores - log_ref[0, index : index + 1, here])
                grad_weights = inner_cols(values, items)
                along = jnp.sum(grad_weights * weights, axis=0, keepdims=True)
                grad_scores = (weights * (grad_weights - along)).astype(BF16)
                grad_values = grad_values + mm(weights.astype(BF16), items)
                grad_keys = grad_keys + mm(grad_scores, queries)
                grad_queries[part].append(
                    mm(keys_turned[head * HD : (head + 1) * HD, :], grad_scores)
                )
        grad_query = jnp.concatenate(
            [jnp.concatenate(grad_queries[part], axis=0) for part in range(rows // SPAN)], axis=1
        )
        grad_query = jnp.transpose(grad_query) * HD**-0.5
        for which, member in enumerate((grad_query, grad_keys)):
            linear[which].append(member * cosine - swap_pairs(member) * sine)
        linear[2].append(grad_values)
    for which in range(3):
        member = jnp.concatenate(linear[which], axis=1) if width > block else linear[which][0]
        grad_bias_ref[0, which : which + 1, :] = jnp.sum(member, axis=0, keepdims=True)
        member = member.astype(BF16)
        lay(grads_ref, step, which * width, mm(turned_ref[...], member).astype(BF16))
        back_ref[...] += inner_cols(member, weight_ref[step, which])

    send_own(step, results)

    if last:

        @pl.when(step == parts - 1)
        def _():
            def chunk(at, carry):
                scale_attn, shift_attn, bias_in = carry
                here = pl.ds(at * CHUNK, CHUNK)
                xhat, root = norm_parts(state_ref[here, :])
                back = back_ref[here, :]
                grad_zero = grad_one_ref[here, :] + norm_pull(back, mod_ref[1:2, :], xhat, root)
                grad_zero_ref[here, :] = grad_zero.astype(BF16)
                return (
                    scale_attn + fold(back * xhat),
                    shift_attn + fold(back),
                    bias_in + fold(grad_zero),
                )

            start = tuple(jnp.zeros((8, wide), F32) for _ in range(3))
            lanes = lax.fori_loop(0, rows // CHUNK, chunk, start)
            for at, member in enumerate(lanes):
                sums_ref[at : at + 1, :] = jnp.sum(member, axis=0, keepdims=True)

    wait_all(step, results)


def total_of(refs):
    total = refs[0][...].astype(F32)
    for ref in refs[1:]:
        total = total + ref[...].astype(F32)
    return total.astype(BF16)


def sum_kernel(count, *refs):
    refs[count][...] = total_of(refs[:count])


def split_kernel(count, parts, *refs):
    own = refs[0][0]
    sums = [total_of(refs[1 + at * count : 1 + (at + 1) * count]) for at in range(parts)]
    for mask, ref in enumerate(refs[1 + parts * count :]):
        value = sums[mask]
        for at in range(1, parts):
            value = jnp.where(own == at, sums[at ^ mask], value)
        ref[...] = value


def merge_kernel(count, starts_ref, *refs):
    bring(starts_ref, refs[:count], refs[count], refs[count + 1])


def bring(starts_ref, pieces, stack_ref, sems):
    size = pieces[0].shape[0]
    copies = []
    for at, piece in enumerate(pieces):
        start = pl.multiple_of(starts_ref[at], 16)
        copies.append(
            pltpu.make_async_copy(piece, stack_ref.at[pl.ds(start, size), :], sems.at[at])
        )
    for copy in copies:
        copy.start()
    for copy in copies:
        copy.wait()


def unlay(target, stack_ref, start, width):
    for block in range(target.shape[0] // width):
        target[block * width : (block + 1) * width, :] = stack_ref[
            start : start + width, block * width : (block + 1) * width
        ].astype(F32)


def ffn_unpack(count, starts_ref, *refs):
    pieces = refs[:count]
    up_ref, down_ref, stack_ref, sems = refs[count:]
    bring(starts_ref, pieces, stack_ref, sems)
    width = up_ref.shape[1]
    unlay(up_ref, stack_ref, 0, width)
    down_ref[...] = stack_ref[width:, :].astype(F32)


def attn_unpack(count, starts_ref, *refs):
    pieces = refs[:count]
    weight_ref, out_ref, stack_ref, sems = refs[count:]
    bring(starts_ref, pieces, stack_ref, sems)
    width = weight_ref.shape[2]
    for which in range(3):
        unlay(weight_ref.at[which], stack_ref, which * width, width)
    out_ref[...] = stack_ref[3 * width :, :].astype(F32)


def gelu_parts(pre):
    share = 0.5 * (1.0 + lax.erf(pre * 0.7071067811865476))
    slope = share + pre * (0.3989422804014327 * jnp.exp(-0.5 * pre * pre))
    return pre * share, slope


def fill_padded(padded_ref, text_ref):
    rows, wide = text_ref.shape
    edge = jnp.zeros((8, wide), F32)
    padded_ref[0:8, :] = edge
    padded_ref[rows + 8 : rows + 16, :] = edge
    for at in range(rows // CHUNK):
        here = slice(at * CHUNK, (at + 1) * CHUNK)
        padded_ref[at * CHUNK + 8 : (at + 1) * CHUNK + 8, :] = text_ref[here, :].astype(F32)


def text_forward(
    text_ref,
    mel_ref,
    kernel_ref,
    bias_ref,
    gain_ref,
    hidden_bias_ref,
    in_ref,
    out_ref,
    project_ref,
    frame_ref,
    normed_ref,
    pre_ref,
    energy_ref,
    mixed_ref,
    refined_ref,
    state_ref,
    padded_ref,
    hidden_ref,
):
    rows, wide = text_ref.shape
    taps = kernel_ref.shape[0]
    fill_padded(padded_ref, text_ref)

    def front(at, carry):
        start = pl.multiple_of(at * CHUNK, CHUNK)
        near = padded_ref[pl.ds(start, CHUNK + 16), :]
        conv = bias_ref[0:1, :]
        for tap in range(taps):
            shift = 8 + tap - taps // 2
            conv = conv + near[shift : shift + CHUNK, :] * kernel_ref[tap : tap + 1, :]
        xhat, _ = norm_parts(conv)
        normed_ref[pl.ds(start, CHUNK), :] = (xhat * gain_ref[...] + bias_ref[1:2, :]).astype(BF16)
        return carry

    lax.fori_loop(0, rows // CHUNK, front, 0)
    pre_ref[...] = mm(normed_ref[...], in_ref[...]) + hidden_bias_ref[0:1, :]

    def gelu(at, carry):
        here = pl.ds(at * CHUNK, CHUNK)
        hidden, _ = gelu_parts(pre_ref[here, :])
        hidden_ref[here, :] = hidden
        return carry + fold(hidden * hidden)

    squares = lax.fori_loop(0, rows // CHUNK, gelu, jnp.zeros((8, pre_ref.shape[1]), F32))
    energy = jnp.sqrt(jnp.sum(squares, axis=0, keepdims=True))
    energy_ref[0:1, :] = energy
    ratio = energy / (jnp.mean(energy, axis=1, keepdims=True) + 1e-06)

    def mix(at, carry):
        here = pl.ds(at * CHUNK, CHUNK)
        hidden = hidden_ref[here, :]
        mixed = hidden_bias_ref[1:2, :] * (hidden * ratio) + hidden_bias_ref[2:3, :] + hidden
        mixed_ref[here, :] = mixed.astype(BF16)
        return carry

    lax.fori_loop(0, rows // CHUNK, mix, 0)
    refined_ref[...] = (
        text_ref[...].astype(F32) + mm(mixed_ref[...], out_ref[...]) + bias_ref[2:3, :]
    ).astype(BF16)
    state_ref[...] = (
        mm(mel_ref[...], project_ref[0 : mel_ref.shape[1], :])
        + mm(refined_ref[...], project_ref[mel_ref.shape[1] :, :])
        + frame_ref[0:1, :]
    )


def full_line(members, wide):
    have = sum(member.shape[1] for member in members)
    return jnp.concatenate(list(members) + [jnp.zeros((1, wide - have), F32)], axis=1)


def small_rows(group):
    count = 12 + 2 * group
    return count + -count % 16


def text_backward(group, *refs):
    refs = list(refs)

    def take(count=1):
        taken = [refs.pop(0) for _ in range(count)]
        return taken[0] if count == 1 else taken

    own_ref, grad_zero_ref, text_ref, mel_ref, refined_ref, mixed_ref, normed_ref = take(7)
    pre_ref, energy_ref, kernel_ref, bias_ref, gain_ref, hidden_bias_ref = take(6)
    in_ref, out_ref, project_ref, attn_sums_ref, ffn_sums_ref = take(5)
    high_bias_ref, low_bias_ref, up_bias_ref, active_ref = take(4)
    grad_text_ref, mods_ref = take(2)
    slots = [take() for _ in range(group)]
    stack_ref, sems, padded_ref, outer_ref, refined_grad_ref, low_ref, mixed_grad_ref = take(7)
    pre_low_ref, normed_grad_ref, lines_ref = take(3)
    small = small_rows(group)
    own = own_ref[0]
    rows, wide = text_ref.shape
    model = grad_zero_ref.shape[1]
    taps = kernel_ref.shape[0]
    mel_at = 3 * wide
    small_at = mel_at + mel_ref.shape[1] + (-(mel_at + mel_ref.shape[1])) % 16

    lines = [attn_sums_ref[1:2, :], attn_sums_ref[0:1, :]]
    lines += [ffn_sums_ref[row : row + 1, :] for row in (5, 3, 2, 1)]
    mods_at = small_at + small
    stack_ref[mods_at:, :] = jnp.zeros((stack_ref.shape[0] - mods_at, model), BF16)
    for at, member in enumerate(lines):
        mods_ref[at : at + 1, :] = member.astype(BF16)
    lines += [active_ref[...].astype(F32), jnp.zeros((1, model), F32)]
    lines = jnp.concatenate(lines, axis=0)
    empty = jnp.zeros_like(lines)
    odd = own_ref[1] % 2 == 1
    lines = jnp.where(
        odd, jnp.concatenate([empty, lines], axis=0), jnp.concatenate([lines, empty], axis=0)
    )
    place = pl.multiple_of(mods_at + own_ref[1] // 2 * 16, 16)
    stack_ref[pl.ds(place, 16), :] = lines.astype(BF16)

    grad_zero = grad_zero_ref[...]
    grad_refined = inner_cols(grad_zero, project_ref[mel_ref.shape[1] :, :])
    refined_grad_ref[...] = grad_refined
    low_ref[...] = grad_refined.astype(BF16)
    sum_out = jnp.sum(fold(grad_refined), axis=0, keepdims=True)
    mixed_grad_ref[...] = inner_cols(low_ref[...], out_ref[...])
    stack_ref[0:wide, :] = inner_rows(refined_ref[...], grad_zero).astype(BF16)
    spare = jnp.zeros((small_at - mel_at - mel_ref.shape[1], model), F32)
    grad_mel = inner_rows(mel_ref[...], grad_zero)
    stack_ref[mel_at:small_at, :] = jnp.concatenate([grad_mel, spare], axis=0).astype(BF16)
    grad_out = inner_rows(mixed_ref[...], low_ref[...]).astype(BF16)
    stack_ref[2 * wide : 3 * wide, 0:wide] = grad_out[0:wide, :]
    stack_ref[2 * wide : 3 * wide, wide:] = grad_out[wide:, :]

    energy = energy_ref[0:1, :]
    mean = jnp.mean(energy, axis=1, keepdims=True) + 1e-06
    ratio = energy / mean

    def first_pass(at, carry):
        along, plain = carry
        here = pl.ds(at * CHUNK, CHUNK)
        hidden, _ = gelu_parts(pre_ref[here, :])
        grad = mixed_grad_ref[here, :]
        return along + fold(grad * hidden), plain + fold(grad)

    zero = jnp.zeros((8, model), F32)
    along, plain = lax.fori_loop(0, rows // CHUNK, first_pass, (zero, zero))
    along = jnp.sum(along, axis=0, keepdims=True)
    sum_beta = jnp.sum(plain, axis=0, keepdims=True)
    gamma = hidden_bias_ref[1:2, :]
    grad_ratio = gamma * along
    grad_mean = jnp.sum(grad_ratio * energy, axis=1, keepdims=True) / (mean * mean)
    grad_energy = grad_ratio / mean - grad_mean / model
    spread = grad_energy / energy
    factor = 1.0 + gamma * ratio

    def second_pass(at, carry):
        here = pl.ds(at * CHUNK, CHUNK)
        hidden, slope = gelu_parts(pre_ref[here, :])
        grad = (mixed_grad_ref[here, :] * factor + hidden * spread) * slope
        pre_low_ref[here, :] = grad.astype(BF16)
        return carry + fold(grad)

    sum_in = jnp.sum(lax.fori_loop(0, rows // CHUNK, second_pass, zero), axis=0, keepdims=True)
    normed_grad_ref[...] = inner_cols(pre_low_ref[...], in_ref[...])
    stack_ref[wide : 2 * wide, :] = inner_rows(normed_ref[...], pre_low_ref[...]).astype(BF16)

    fill_padded(padded_ref, text_ref)
    edge = jnp.zeros((8, wide), F32)
    outer_ref[0:8, :] = edge
    outer_ref[rows + 8 : rows + 16, :] = edge
    narrow = jnp.zeros((8, wide), F32)
    step = CHUNK // 2

    def conv_back(at, carry):
        sum_gain, sum_norm, sum_conv, sum_taps = carry
        start = pl.multiple_of(at * step, step)
        near = padded_ref[pl.ds(start, step + 16), :]
        conv = bias_ref[0:1, :]
        for tap in range(taps):
            shift = 8 + tap - taps // 2
            conv = conv + near[shift : shift + step, :] * kernel_ref[tap : tap + 1, :]
        xhat, root = norm_parts(conv)
        grad = normed_grad_ref[pl.ds(start, step), :]
        entry = grad * gain_ref[...]
        entry_mean = jnp.mean(entry, axis=-1, keepdims=True)
        entry_along = jnp.mean(entry * xhat, axis=-1, keepdims=True)
        grad_conv = root * (entry - entry_mean - xhat * entry_along)
        outer_ref[pl.ds(start + 8, step), :] = grad_conv
        sum_taps = tuple(
            member
            + fold(grad_conv * near[8 + tap - taps // 2 : 8 + tap - taps // 2 + step, :])
            for tap, member in enumerate(sum_taps)
        )
        return (
            sum_gain + fold(grad * xhat),
            sum_norm + fold(grad),
            sum_conv + fold(grad_conv),
            sum_taps,
        )

    sum_gain, sum_norm, sum_conv, sum_taps = lax.fori_loop(
        0, rows // step, conv_back, (narrow, narrow, narrow, (narrow,) * taps)
    )

    def text_grad(at, carry):
        start = pl.multiple_of(at * CHUNK, CHUNK)
        near = outer_ref[pl.ds(start, CHUNK + 16), :]
        total = refined_grad_ref[pl.ds(start, CHUNK), :]
        for tap in range(taps):
            shift = 8 + taps // 2 - tap
            total = total + near[shift : shift + CHUNK, :] * kernel_ref[tap : tap + 1, :]
        grad_text_ref[pl.ds(start, CHUNK), :] = total
        return carry

    lax.fori_loop(0, rows // CHUNK, text_grad, 0)

    def line(member):
        return jnp.sum(member, axis=0, keepdims=True)

    halves = [line(member) for member in sum_taps] + [line(sum_gain)]
    halves += [line(sum_conv), line(sum_norm), sum_out, jnp.zeros((1, wide), F32)]
    lines = [
        jnp.concatenate(halves[at : at + 2], axis=1) for at in range(0, len(halves), 2)
    ]
    lines += [sum_in, ratio * along, sum_beta]
    lines += [attn_sums_ref[2:3, :], ffn_sums_ref[4:5, :], ffn_sums_ref[0:1, :]]
    lines_ref[...] = jnp.zeros_like(lines_ref)
    for at, member in enumerate(lines):
        lines_ref[at : at + 1, :] = member
    parts = group // 2
    row = lax.broadcasted_iota(jnp.int32, lines_ref.shape, 0)
    total = lines_ref[...]
    for slot in range(group):
        source_ref = low_bias_ref if slot < parts else high_bias_ref
        owner = jnp.bitwise_xor(own, slot)
        members = [source_ref[slot % parts, which : which + 1, :] for which in range(3)]
        total = jnp.where(row == 12 + owner, full_line(members, model), total)
        total = jnp.where(row == 12 + group + owner, full_line([up_bias_ref[slot]], model), total)
    lines_ref[...] = total
    stack_ref[small_at : small_at + small, :] = lines_ref[...].astype(BF16)

    size = stack_ref.shape[0] // group
    copies = []
    for slot in range(group):
        start = pl.multiple_of(jnp.bitwise_xor(own, slot) * size, size)
        copies.append(
            pltpu.make_async_copy(stack_ref.at[pl.ds(start, size), :], slots[slot], sems.at[slot])
        )
    for copy in copies:
        copy.start()
    for copy in copies:
        copy.wait()


def text_unpack(count, group, utterances, starts_ref, own_ref, *refs):
    pieces = refs[:count]
    project_ref, in_ref, out_ref, taps_ref, bias_ref, gain_ref = refs[count : count + 6]
    hidden_ref, frame_ref, qkv_bias_ref, up_bias_ref = refs[count + 6 : count + 10]
    mod_ref, mod_bias_ref, stack_ref, sems, lines_ref = refs[count + 10 :]
    bring(starts_ref, pieces, stack_ref, sems)
    own = own_ref[0]
    wide = in_ref.shape[0]
    taps = taps_ref.shape[0]
    mels = project_ref.shape[0] - wide
    mel_at = 3 * wide
    small_at = mel_at + mels + (-(mel_at + mels)) % 16
    project_ref[0:mels, :] = stack_ref[mel_at : mel_at + mels, :].astype(F32)
    project_ref[mels:, :] = stack_ref[0:wide, :].astype(F32)
    in_ref[...] = stack_ref[wide : 2 * wide, :].astype(F32)
    out_ref[0:wide, :] = stack_ref[2 * wide : 3 * wide, 0:wide].astype(F32)
    out_ref[wide:, :] = stack_ref[2 * wide : 3 * wide, wide:].astype(F32)
    lines_ref[...] = stack_ref[small_at : small_at + small_rows(group), :].astype(F32)
    mods_at = small_at + small_rows(group)
    mods = stack_ref[mods_at : mods_at + 8 * utterances, :].astype(F32)
    mods = mods.reshape(utterances, 8, mods.shape[1])
    place = lax.broadcasted_iota(jnp.int32, mods.shape, 1)

    def block_rows(at):
        return jnp.sum(jnp.where(place == at, mods, 0.0), axis=1)

    active = block_rows(6).astype(BF16)
    unit = mod_ref.shape[1] // 3
    share = mods.shape[2] // unit
    for at in range(3):
        index = own * 3 + at
        line = block_rows(index // share)
        piece = line[:, 0:unit]
        for other in range(1, share):
            piece = jnp.where(
                index % share == other, line[:, other * unit : (other + 1) * unit], piece
            )
        cut = slice(at * unit, (at + 1) * unit)
        mod_bias_ref[:, cut] = jnp.sum(piece, axis=0, keepdims=True)
        mod_ref[:, cut] = inner_rows(active, piece.astype(BF16))

    def half(at):
        return lines_ref[at // 2 : at // 2 + 1, (at % 2) * wide : (at % 2 + 1) * wide]

    for tap in range(taps):
        taps_ref[tap : tap + 1, :] = half(tap)
    gain_ref[...] = half(taps)
    for at in range(3):
        bias_ref[at : at + 1, :] = half(taps + 1 + at)
    first = (taps + 5) // 2
    hidden_ref[...] = lines_ref[first : first + 3, :]
    frame_ref[...] = lines_ref[first + 3 : first + 6, :]
    row = lax.broadcasted_iota(jnp.int32, lines_ref.shape, 0)

    def pick(at):
        return jnp.sum(jnp.where(row == at, lines_ref[...], 0.0), axis=0, keepdims=True)

    line = pick(12 + own)
    width = qkv_bias_ref.shape[1]
    for which in range(3):
        qkv_bias_ref[which : which + 1, :] = line[:, which * width : (which + 1) * width]
    up_bias_ref[...] = pick(12 + group + own)[:, 0 : up_bias_ref.shape[1]]


ANY = pl.BlockSpec(memory_space=pl.ANY)
SMEM = pl.BlockSpec(memory_space=pltpu.SMEM)


def whole(shape):
    return pl.BlockSpec(shape, lambda g: (0,) * len(shape))


def held(shape, parts=None):
    if parts is None:
        return pl.BlockSpec((1,) + shape, lambda g: (g,) + (0,) * len(shape))
    return pl.BlockSpec((1,) + shape, lambda g: (parts - 1 - g,) + (0,) * len(shape))


def run_kernel(kernel, parts, inputs, outputs, scratch):
    return pl.pallas_call(
        kernel,
        grid=(parts,),
        in_specs=[spec for spec, _ in inputs],
        out_specs=[spec for spec, _, _ in outputs],
        out_shape=[jax.ShapeDtypeStruct(shape, kind) for _, shape, kind in outputs],
        scratch_shapes=scratch,
        compiler_params=pltpu.CompilerParams(vmem_limit_bytes=VMEM),
        cost_estimate=pl.CostEstimate(flops=1024, bytes_accessed=1024, transcendentals=0),
    )(*[array for _, array in inputs])


def after(arrays, *others):
    arrays = tuple(arrays)
    return lax.optimization_barrier(arrays + others)[: len(arrays)]


def swap(array, axis, bit):
    return lax.ppermute(array, axis, [(at, at ^ bit) for at in range(lax.axis_size(axis))])


def low_bit(slot):
    return slot & -slot


def tile_rows(rows):
    return next(size for size in (256, 224, 128, 112, 96, 80, 64, 48, 32, 16) if rows % size == 0)


def add_arrays(arrays):
    rows, wide = arrays[0].shape
    tile = tile_rows(rows)
    spec = pl.BlockSpec((tile, wide), lambda g: (g, 0))
    return run_kernel(
        partial(sum_kernel, len(arrays)),
        rows // tile,
        [(spec, array) for array in arrays],
        [(spec, (rows, wide), BF16)],
        [],
    )[0]


def add_and_split(arrays, own, parts):
    rows, wide = arrays[0].shape
    size = rows // parts
    tile = tile_rows(size)
    steps = size // tile

    def block_at(part):
        return pl.BlockSpec((tile, wide), lambda g: (g + part * steps, 0))

    return run_kernel(
        partial(split_kernel, len(arrays), parts),
        steps,
        [(SMEM, own.astype(jnp.int32).reshape(1))]
        + [(block_at(part), array) for part in range(parts) for array in arrays],
        [(block_at(0), (size, wide), BF16)] * parts,
        [],
    )


def merge(pieces, starts, rows):
    return run_kernel(
        partial(merge_kernel, len(pieces)),
        1,
        [(SMEM, jnp.stack(starts).astype(jnp.int32))] + [(ANY, piece) for piece in pieces],
        [(whole((rows, pieces[0].shape[1])), (rows, pieces[0].shape[1]), BF16)],
        [pltpu.SemaphoreType.DMA((len(pieces),))],
    )[0]


class Fetch:
    def __init__(self, array, axis):
        size = array.shape[axis] // 2
        start = lax.axis_index("dp") % 2 * size
        self.half = lax.dynamic_slice_in_dim(array, start, size, axis=axis)
        self.group = lax.axis_size("heads")
        self.slots = {0: [array]}
        self.sent = {}

    def core(self, slot, *others):
        pieces = after(self.slots[slot], *others)
        self.slots[slot + 1] = [swap(piece, "heads", 1) for piece in pieces]

    def send(self, *others):
        (self.half,) = after([self.half], *others)
        for slot in range(2, self.group, 2):
            bit = low_bit(slot)
            if slot == bit:
                self.sent[slot] = swap(self.half, "heads", bit)

    def share(self, *others):
        for slot in range(2, self.group, 2):
            bit = low_bit(slot)
            if slot == bit:
                (came,) = after([self.sent[slot]], *others)
            else:
                came = swap(self.slots[slot - bit][0], "heads", bit)
            self.slots[slot] = [came, swap(came, "dp", 1)]

    def cores(self, first, last, *others):
        for slot in range(first, last, 2):
            self.core(slot, *others)

    def listed(self):
        return [self.slots[slot] for slot in range(self.group)]


def flat(slots):
    return [piece for pieces in slots for piece in pieces]


class GroupSum:
    def __init__(self):
        self.arrived = {}

    def put(self, slot, array, *others):
        arrays = [array] + self.arrived.pop(slot, [])
        if slot == 0:
            return arrays
        total = add_arrays(after(arrays, *others)) if len(arrays) > 1 else array
        bit = low_bit(slot)
        self.arrived.setdefault(slot - bit, []).append(swap(total, "heads", bit))
        return total


class DataSum:
    def __init__(self, arrays, bits, merged=False):
        self.merged = merged
        self.arrays = list(arrays)
        self.bits = list(bits)
        self.halved = []
        self.rows = arrays[0].shape[0]
        self.pieces = None

    def step(self, *others):
        arrays = after(self.arrays, *others)
        if not self.bits:
            total = add_arrays(arrays)
            self.gather(total)
            return total
        bit = self.bits.pop(0)
        keep, send = add_and_split(arrays, lax.axis_index("dp") // bit % 2, 2)
        self.halved.append(bit)
        self.arrays = [keep, swap(send, "dp", bit)]
        return keep

    def gather(self, total):
        self.pieces = {0: total}
        for bit in self.halved[: 0 if self.merged else None : -1]:
            for mask, piece in list(self.pieces.items()):
                self.pieces[mask | bit] = swap(piece, "dp", bit)

    def half(self, *others):
        starts = [start % (self.rows // 2) for start in self.starts()]
        return merge(after(self.pieces.values(), *others), starts, self.rows // 2)

    def starts(self):
        own = lax.axis_index("dp")
        return [
            sum(
                (own ^ mask) // bit % 2 * (self.rows >> (at + 1))
                for at, bit in enumerate(self.halved)
            )
            for mask in self.pieces
        ]


def axis_bits(axis):
    size = lax.axis_size(axis)
    return [1 << at for at in range(size.bit_length() - 1)]


def on_device(
    noisy_mel,
    cond_mel,
    text_embed,
    time_embed,
    lengths,
    spans,
    dw_kernel,
    text_bias,
    text_gain,
    text_hidden,
    pw_in,
    pw_out,
    in_proj,
    frame_bias,
    mod_weight,
    mod_bias,
    qkv_weight,
    qkv_bias,
    out_weight,
    ff_in,
    ff_in_bias,
    ff_out,
    cotangent,
):
    group = lax.axis_size("heads")
    own = lax.axis_index("heads")
    own_data = lax.axis_index("dp")
    rows = text_embed.shape[0]
    model_width = in_proj.shape[1]
    width = qkv_weight.shape[2]
    units = ff_in.shape[1]
    block = min(128, width)
    parts = group // 2
    full = (rows, model_width)

    fetches = [Fetch(qkv_weight, 1), Fetch(out_weight, 0), Fetch(ff_in, 0), Fetch(ff_out, 0)]
    for fetch in fetches[:2]:
        fetch.send()
        fetch.core(0)

    position = jnp.arange(rows, dtype=jnp.int32)
    inside = (position >= spans[0, 0]) & (position < spans[0, 1])
    keep = jnp.where(inside, 0.0, 1.0).astype(F32)[:, None]
    count = lax.dynamic_slice_in_dim(lengths, own, 1)
    lane = jnp.arange(block, dtype=jnp.int32)
    pair = ((lane % HD) // 2).astype(F32)
    angle = position.astype(F32)[:, None] * (10000.0 ** (-2.0 * pair / HD))[None, :]
    cosine = jnp.cos(angle)
    sine = jnp.sin(angle) * jnp.where(lane % 2 == 0, -1.0, 1.0)[None, :]

    cond_low = (cond_mel.astype(F32) * keep).astype(BF16)
    mel = jnp.concatenate([noisy_mel, cond_low], axis=1)
    mels = mel.shape[1]
    text_width = text_embed.shape[1]
    gain = text_gain[None, :]

    def block_of(array):
        return (whole(array.shape), array)

    normed_text, pre_act, energy, mixed_text, refined, state_zero = run_kernel(
        text_forward,
        1,
        [
            block_of(member)
            for member in (
                text_embed,
                mel,
                dw_kernel,
                text_bias,
                gain,
                text_hidden,
                pw_in,
                pw_out,
                in_proj,
                frame_bias,
            )
        ],
        [
            (whole(shape), shape, kind)
            for shape, kind in (
                ((rows, text_width), BF16),
                ((rows, pw_in.shape[1]), F32),
                ((8, pw_in.shape[1]), F32),
                ((rows, pw_in.shape[1]), BF16),
                ((rows, text_width), BF16),
                (full, F32),
            )
        ],
        [pltpu.VMEM((rows + 16, text_width), F32), pltpu.VMEM((rows, pw_in.shape[1]), F32)],
    )

    def semaphores(number, pieces=2):
        shape = (number, pieces) if pieces > 1 else (number,)
        return pltpu.SemaphoreType.DMA(shape)

    def attn_buffers(number, pieces=2):
        return [
            pltpu.VMEM((number, 3, model_width, width), BF16),
            pltpu.VMEM((number, width, model_width), BF16),
            semaphores(number, pieces),
            semaphores(number, pieces),
        ]

    def ffn_buffers(number, pieces=2):
        return [
            pltpu.VMEM((number, model_width, units), BF16),
            pltpu.VMEM((number, units, model_width), BF16),
            semaphores(number, pieces),
            semaphores(number, pieces),
        ]

    half_index = (own_data % 2).astype(jnp.int32).reshape(1)

    def pieces_of(slots):
        return tuple(len(pieces) for pieces in slots)

    (time_late,) = after([time_embed], state_zero)
    time_rows = time_late.astype(F32)
    activated, silu_back = jax.vjp(jax.nn.silu, time_rows)
    activated_low = activated.astype(BF16)
    modulation = (mm(activated_low, mod_weight) + mod_bias).astype(BF16)
    biases = jnp.concatenate([qkv_bias.reshape(-1), ff_in_bias])
    riders = jnp.broadcast_to(biases[None, :], (group, biases.size))
    sent = jnp.concatenate([modulation, riders], axis=1)
    came = lax.all_to_all(sent, "heads", split_axis=0, concat_axis=1, tiled=True)
    came = came.reshape(group, sent.shape[1]).astype(F32)
    mod_rows = came[:, : modulation.shape[1]].reshape(6, model_width)
    slot_owner = jnp.bitwise_xor(jnp.arange(group, dtype=jnp.int32), own)
    biases_all = jnp.take(came[:, modulation.shape[1] :], slot_owner, axis=0)
    qkv_bias_all = biases_all[:, : 3 * width].reshape(group, 3, width)
    up_bias_all = biases_all[:, 3 * width :].reshape(group, 1, units)

    for fetch in fetches[2:]:
        fetch.send(came)
    for fetch in fetches[:2]:
        fetch.share()
        fetch.cores(2, parts)
    (mod_rows,) = after([mod_rows], *[fetch.sent[2] for fetch in fetches[:2]])
    kept = []
    for turn in range(2):
        first, last = turn == 0, turn == 1
        if last:
            for fetch in fetches[:2]:
                fetch.cores(parts, group, normed)
            for fetch in fetches[2:]:
                fetch.share(normed)
                fetch.core(0, normed)
            own_index = jnp.stack([own, own_data * group + own]).astype(jnp.int32)
            own_active = lax.dynamic_index_in_dim(activated_low, own, 0)
            before, own_index, own_active = lax.optimization_barrier(
                (before, own_index, own_active)
            )
            (before,) = after([before], *[fetch.slots[2][0] for fetch in fetches[2:]])
        chosen = range(turn * parts, (turn + 1) * parts)
        qkv_here = [fetches[0].slots[slot] for slot in chosen]
        out_here = [fetches[1].slots[slot] for slot in chosen]
        inputs = [
            (SMEM, count),
            (SMEM, half_index),
            (whole(full), state_zero),
            (whole((6, model_width)), mod_rows),
            (held((3, width)), qkv_bias_all[chosen[0] : chosen[-1] + 1]),
            (whole((3, model_width)), frame_bias),
            (whole((rows, block)), cosine),
            (whole((rows, block)), sine),
        ]
        inputs += [(ANY, member) for member in flat(qkv_here) + flat(out_here)]
        if not first:
            inputs += [(whole(full), normed), (whole(full), before)]
        outputs = [(held((rows, width)), (parts, rows, width), BF16)] * 4
        outputs += [(held((8, rows)), (parts, 8, rows), F32)]
        if first:
            outputs += [(whole(full), full, BF16)]
        outputs += [(whole(full), full, F32)]
        if last:
            outputs += [(whole(full), full, F32), (whole(full), full, BF16)]
        results = run_kernel(
            partial(attention_forward, pieces_of(qkv_here), first, last),
            parts,
            inputs,
            outputs,
            attn_buffers(parts) + ([pltpu.VMEM(full, F32)] if last else []),
        )
        kept.append(results[:5])
        if first:
            normed, before = results[5:]
        else:
            branch, state_one, ffn_in = results[5:]

    qkv_all, out_all = fetches[0].listed(), fetches[1].listed()
    fetches[2].cores(2, group, ffn_in)
    fetches[3].cores(2, group, ffn_in)
    up_all, down_all = fetches[2].listed()[::-1], fetches[3].listed()[::-1]
    inputs = [
        (SMEM, half_index),
        (whole(full), cotangent),
        (whole(full), state_one),
        (whole(full), branch),
        (whole(full), ffn_in),
        (whole((6, model_width)), mod_rows),
        (held((1, units), group), up_bias_all),
        (whole((3, model_width)), frame_bias),
    ]
    inputs += [(ANY, member) for member in flat(up_all) + flat(down_all)]
    merged = (2 * units, model_width)
    outputs = [(held((1, units), group), (group, 1, units), F32)]
    outputs += [(whole((8, model_width)), (8, model_width), F32)]
    outputs += [(ANY, merged, BF16)] * group
    outputs += [(whole(full), full, BF16)] * 2 + [(whole(full), full, F32)]
    outputs += [(whole(full), full, BF16)]
    results = run_kernel(
        partial(feed_forward, pieces_of(up_all), True, True),
        group,
        inputs,
        outputs,
        [
            pltpu.VMEM((group, model_width, units), BF16),
            pltpu.VMEM((group, units, model_width), BF16),
            semaphores(group),
            semaphores(group),
            pltpu.VMEM((group,) + merged, BF16),
            semaphores(group, 1),
            pltpu.VMEM((model_width, rows), BF16),
            pltpu.VMEM((rows, units), BF16),
            pltpu.VMEM((rows, units), BF16),
        ]
        + [pltpu.VMEM(full, F32)] * 2,
    )
    grad_up_bias, ffn_sums = results[:2]
    output, grad_one, grad_attn = results[3 + group :]
    ffn_grads = results[2 : 2 + group][::-1]

    attn_grads = []
    merged = (4 * width, model_width)
    qkv_bias_parts = []
    for turn in range(2):
        first, last = turn == 0, turn == 1
        chosen = [group - 1 - turn * parts - at for at in range(parts)]
        inputs = [
            (SMEM, count),
            (SMEM, half_index),
            (whole(full), grad_attn),
            (whole(full), normed),
            (whole((6, model_width)), mod_rows),
            (whole((rows, block)), cosine),
            (whole((rows, block)), sine),
        ]
        inputs += [(held((rows, width), parts), member) for member in kept[1 - turn][:4]]
        inputs += [(held((8, rows), parts), kept[1 - turn][4])]
        inputs += [(ANY, member) for member in flat([qkv_all[slot] for slot in chosen])]
        inputs += [(ANY, member) for member in flat([out_all[slot] for slot in chosen])]
        if not first:
            inputs += [(whole(full), back)]
        if last:
            inputs += [(whole(full), state_zero), (whole(full), grad_one)]
        outputs = [(held((3, width), parts), (parts, 3, width), F32)]
        outputs += [(ANY, merged, BF16)] * parts
        if last:
            outputs += [(whole(full), full, BF16), (whole((8, model_width)), (8, model_width), F32)]
        else:
            outputs += [(whole(full), full, F32)]
        results = run_kernel(
            partial(attention_backward, pieces_of([qkv_all[slot] for slot in chosen]), first, last),
            parts,
            inputs,
            outputs,
            attn_buffers(parts)
            + [pltpu.VMEM((parts,) + merged, BF16), semaphores(parts, 1)]
            + [pltpu.VMEM((model_width, rows), BF16), pltpu.VMEM((rows, width), BF16)]
            + ([pltpu.VMEM(full, F32)] if last else []),
        )
        qkv_bias_parts.append(results[0])
        attn_grads = list(results[1 : 1 + parts])[::-1] + attn_grads
        if first:
            back = results[1 + parts]
            ffn_sum = GroupSum()
            token = back
            for slot in range(group - 1, 0, -1):
                total = ffn_sum.put(slot, ffn_grads[slot], token)
                if slot % 2 == 0:
                    token = total
            (back,) = after([back], token)
        else:
            grad_zero, attn_sums = results[1 + parts :]
    token = grad_zero
    attn_sum = GroupSum()
    for slot in range(group - 1, 0, -1):
        total = attn_sum.put(slot, attn_grads[slot], token)
        if slot % 2 == 0:
            token = total
    (grad_zero,) = after([grad_zero], token)

    data = lax.axis_size("dp")
    stack_rows = 3 * text_width + mels
    stack_rows += -stack_rows % 16 + small_rows(group) + 8 * group * data
    stack_rows += -stack_rows % (16 * group * data)
    results = run_kernel(
        partial(text_backward, group),
        1,
        [(SMEM, own_index)]
        + [
            block_of(member)
            for member in (
                grad_zero,
                text_embed,
                mel,
                refined,
                mixed_text,
                normed_text,
                pre_act,
                energy,
                dw_kernel,
                text_bias,
                gain,
                text_hidden,
                pw_in,
                pw_out,
                in_proj,
                attn_sums,
                ffn_sums,
                qkv_bias_parts[0],
                qkv_bias_parts[1],
                grad_up_bias,
                own_active,
            )
        ],
        [
            (whole((rows, text_width)), (rows, text_width), F32),
            (whole((6, model_width)), (6, model_width), BF16),
        ]
        + [(ANY, (stack_rows // group, model_width), BF16)] * group,
        [
            pltpu.VMEM((stack_rows, model_width), BF16),
            semaphores(group, 1),
            pltpu.VMEM((rows + 16, text_width), F32),
            pltpu.VMEM((rows + 16, text_width), F32),
            pltpu.VMEM((rows, text_width), F32),
            pltpu.VMEM((rows, text_width), BF16),
            pltpu.VMEM((rows, pw_in.shape[1]), F32),
            pltpu.VMEM((rows, pw_in.shape[1]), BF16),
            pltpu.VMEM((rows, text_width), F32),
            pltpu.VMEM((small_rows(group), model_width), F32),
        ],
    )
    grad_text, grad_mod = results[:2]
    def unpack(kernel, data, first, second, *others):
        pieces = after(data.pieces.values(), *others)
        return run_kernel(
            partial(kernel, len(pieces)),
            1,
            [(SMEM, jnp.stack(data.starts()).astype(jnp.int32))]
            + [(ANY, member) for member in pieces],
            [(whole(first.shape), first.shape, F32), (whole(second.shape), second.shape, F32)],
            [pltpu.VMEM((data.rows, model_width), BF16), semaphores(len(pieces), 1)],
        )

    bits = axis_bits("dp")
    ffn_data = DataSum(ffn_sum.put(0, ffn_grads[0]), bits)
    token = ffn_data.step(grad_mod)
    text_sum = GroupSum()
    for slot in range(group - 1, 0, -1):
        total = text_sum.put(slot, results[2 + slot], token)
        if slot % 2 == 0:
            token = total
    attn_data = DataSum(attn_sum.put(0, attn_grads[0]), bits)
    text_data = DataSum(text_sum.put(0, results[2]), bits, merged=True)
    steps = [(at, ffn_data) for at in range(1, len(bits) + 1)]
    for at in range(len(bits) + 1):
        steps.append((at + 1.9 if at else 1.5, attn_data))
        steps.append((at + 2.25, text_data))
    steps.sort(key=lambda step: step[0])
    columns = mod_weight.shape[1]
    grad_time = None
    for at, member in steps:
        if at > len(bits) and member is attn_data and grad_time is None:
            (grad_mod,) = after([grad_mod], token)
            grad_mod = grad_mod.reshape(1, group * columns)
            grad_cols = lax.all_to_all(grad_mod, "heads", split_axis=1, concat_axis=0, tiled=True)
            (grad_time,) = silu_back(inner_cols(grad_cols, mod_weight))
            token = member.step(token, grad_time)
        elif at == steps[-1][0]:
            (grad_time,) = after([grad_time], token)
            grad_time = jnp.broadcast_to(grad_time.astype(BF16), (group,) + grad_time.shape)
            grad_time = lax.all_to_all(grad_time, "heads", split_axis=0, concat_axis=0)
            grad_time = jnp.sum(grad_time.astype(F32), axis=0)
            token = member.step(token, grad_time)
        else:
            token = member.step(token)

    weight_up, weight_down = unpack(ffn_unpack, ffn_data, ff_in, ff_out, attn_data.pieces[0])
    text_half = text_data.half(weight_up, *list(attn_data.pieces.values())[1:-2])
    weight_qkv, weight_out = unpack(attn_unpack, attn_data, qkv_weight, out_weight, text_half)
    text_halves = {0: [text_half]}
    for slot in range(2, group, 2):
        bit = low_bit(slot)
        text_halves[slot] = [swap(text_halves[slot - bit][0], "heads", bit)]
        text_halves[slot] = list(after(text_halves[slot], weight_qkv))
    for slot in range(0, group, 2):
        text_halves[slot].append(swap(text_halves[slot][0], "dp", 1))
        text_halves[slot + 1] = [swap(piece, "heads", 1) for piece in text_halves[slot]]
    slot_rows = stack_rows // group
    text_pieces, text_starts = [], []
    for slot, pieces in text_halves.items():
        for which, piece in enumerate(pieces):
            text_pieces.append(piece)
            text_starts.append(
                slot_owner[slot] * slot_rows + ((own_data + which) % 2) * (slot_rows // 2)
            )
    unpacked = (
        in_proj.shape,
        pw_in.shape,
        pw_out.shape,
        dw_kernel.shape,
        text_bias.shape,
        gain.shape,
        text_hidden.shape,
        frame_bias.shape,
        (3, width),
        (1, units),
    )
    mods_shape = mod_weight.shape
    unpacked = run_kernel(
        partial(text_unpack, len(text_pieces), group, group * data),
        1,
        [(SMEM, jnp.stack(text_starts).astype(jnp.int32)), (SMEM, own_index)]
        + [(ANY, member) for member in text_pieces],
        [(whole(shape), shape, F32) for shape in unpacked]
        + [(whole(shape), shape, F32) for shape in (mods_shape, (1, columns))],
        [
            pltpu.VMEM((stack_rows, model_width), BF16),
            semaphores(len(text_pieces), 1),
            pltpu.VMEM((small_rows(group), model_width), F32),
        ],
    )
    return (
        output,
        grad_text,
        grad_time,
        unpacked[3],
        unpacked[4],
        unpacked[5][0],
        unpacked[6],
        unpacked[1],
        unpacked[2],
        unpacked[0],
        unpacked[7],
        unpacked[10],
        unpacked[11][0],
        weight_qkv,
        unpacked[8],
        weight_out,
        weight_up,
        unpacked[9][0],
        weight_down,
    )


def solution(mesh):
    in_specs = (
        P(("dp", "heads"), None),
        P(("dp", "heads"), None),
        P(("dp", "heads"), None),
        P("dp", None),
        P("dp"),
        P(("dp", "heads"), None),
        P(),
        P(),
        P(),
        P(),
        P(),
        P(),
        P(),
        P(),
        P(None, "heads"),
        P("heads"),
        P(None, None, "heads"),
        P(None, "heads"),
        P("heads", None),
        P(None, "heads"),
        P("heads"),
        P("heads", None),
        P(("dp", "heads"), None),
    )
    out_specs = (
        P(("dp", "heads"), None),
        P(("dp", "heads"), None),
        P("dp", None),
        P(),
        P(),
        P(),
        P(),
        P(),
        P(),
        P(),
        P(),
        P(None, "heads"),
        P("heads"),
        P(None, None, "heads"),
        P(None, "heads"),
        P("heads", None),
        P(None, "heads"),
        P("heads"),
        P("heads", None),
    )
    return jax.shard_map(
        on_device, mesh=mesh, in_specs=in_specs, out_specs=out_specs, check_vma=False
    )
```

```python
from functools import partial

import jax
import jax.numpy as jnp
from jax import lax
from jax.experimental import pallas as pl
from jax.experimental.pallas import tpu as pltpu
from jax.sharding import PartitionSpec as P

HD = 64


def inner_rows(left, right):
    return lax.dot_general(
        left, right, (((0,), (0,)), ((), ())), preferred_element_type=jnp.float32
    )


def inner_cols(left, right):
    return lax.dot_general(
        left, right, (((1,), (1,)), ((), ())), preferred_element_type=jnp.float32
    )


F32 = jnp.float32
BF16 = jnp.bfloat16
CHUNK = 64
SPAN = 256
VMEM = 60 * 1024 * 1024


def mm(left, right):
    return jnp.dot(left, right, preferred_element_type=F32)


def fold(values):
    return jnp.sum(values.reshape(values.shape[0] // 8, 8, values.shape[1]), axis=0)


def norm_parts(values):
    mean = jnp.mean(values, axis=-1, keepdims=True)
    centred = values - mean
    root = lax.rsqrt(jnp.mean(centred * centred, axis=-1, keepdims=True) + 1e-06)
    return centred * root, root


def norm_pull(grad, scale, xhat, root):
    entry = grad * (1.0 + scale)
    mean = jnp.mean(entry, axis=-1, keepdims=True)
    along = jnp.mean(entry * xhat, axis=-1, keepdims=True)
    return root * (entry - mean - xhat * along)


def swap_pairs(block):
    width = block.shape[1]
    lane = lax.broadcasted_iota(jnp.int32, block.shape, 1)
    if width % 128 == 0:
        after = pltpu.roll(block, width - 1, 1)
        before = pltpu.roll(block, 1, 1)
    else:
        after = jnp.concatenate([block[:, 1:], block[:, :1]], axis=1)
        before = jnp.concatenate([block[:, width - 1 :], block[:, : width - 1]], axis=1)
    return jnp.where(lane % 2 == 0, after, before)


def head_lanes(block, head):
    if block.shape[1] == HD:
        return block
    lane = lax.broadcasted_iota(jnp.int32, block.shape, 1)
    return jnp.where((lane >= head * HD) & (lane < (head + 1) * HD), block, jnp.zeros_like(block))


def slot_copies(pieces, target, sems, at, axis, half):
    if len(pieces) == 1:
        return [pltpu.make_async_copy(pieces[0], target.at[at], sems.at[at, 0])]
    copies = []
    for which, piece in enumerate(pieces):
        size = piece.shape[axis]
        start = pl.multiple_of((half if which == 0 else 1 - half) * size, size)
        index = (at,) + (slice(None),) * axis + (pl.ds(start, size),)
        copies.append(pltpu.make_async_copy(piece, target.at[index], sems.at[at, which]))
    return copies


def start_all(step, copies):
    @pl.when(step == 0)
    def _():
        for members in copies:
            for copy in members:
                copy.start()


def wait_own(step, copies):
    for at, members in enumerate(copies):

        @pl.when(step == at)
        def _(members=members):
            for copy in members:
                copy.wait()


def send_own(step, results):
    for at, members in enumerate(results):

        @pl.when(step == at)
        def _(members=members):
            for copy in members:
                copy.start()


def wait_all(step, results):
    @pl.when(step == len(results) - 1)
    def _():
        for members in results:
            for copy in members:
                copy.wait()


def attention_forward(pieces, first, last, *refs):
    parts = len(pieces)
    refs = list(refs)

    def take(count=1):
        taken = [refs.pop(0) for _ in range(count)]
        return taken[0] if count == 1 else taken

    count_ref, half_ref, state_ref, mod_ref, bias_ref, frame_ref, cosine_ref, sine_ref = take(8)
    weights = [[take() for _ in range(number)] for number in pieces]
    outs = [[take() for _ in range(number)] for number in pieces]
    if not first:
        normed_ref, before_ref = take(2)
    query_ref, key_ref, value_ref, attended_ref, log_ref = take(5)
    if first:
        normed_ref = take()
    if last:
        branch_ref, one_ref, ffn_ref = take(3)
    else:
        total_ref = take()
    weight_ref, out_ref, weight_sem, out_sem = take(4)
    if last:
        total_ref = take()
    step = pl.program_id(0)
    rows = state_ref.shape[0]
    width = weight_ref.shape[3]
    block = cosine_ref.shape[1]
    count = count_ref[0]
    half = half_ref[0]
    copies = [
        slot_copies(weights[at], weight_ref, weight_sem, at, 1, half)
        + slot_copies(outs[at], out_ref, out_sem, at, 0, half)
        for at in range(parts)
    ]
    start_all(step, copies)

    @pl.when(step == 0)
    def _():
        if first:

            def chunk(at, carry):
                here = pl.ds(at * CHUNK, CHUNK)
                xhat, _ = norm_parts(state_ref[here, :])
                normed_ref[here, :] = (xhat * (1.0 + mod_ref[1:2, :]) + mod_ref[0:1, :]).astype(
                    BF16
                )
                return carry

            lax.fori_loop(0, rows // CHUNK, chunk, 0)
            total_ref[...] = jnp.zeros_like(total_ref)
        else:
            total_ref[...] = before_ref[...]

    wait_own(step, copies)
    normed = normed_ref[...]
    cosine = cosine_ref[...]
    sine = sine_ref[...]
    logs = jnp.zeros((rows, 128), F32)
    lane = lax.broadcasted_iota(jnp.int32, (rows, 128), 1)
    query_lin = mm(normed, weight_ref[step, 0]) + bias_ref[0, 0:1, :]
    key_lin = mm(normed, weight_ref[step, 1]) + bias_ref[0, 1:2, :]
    value_ref[0] = (mm(normed, weight_ref[step, 2]) + bias_ref[0, 2:3, :]).astype(BF16)
    for at in range(width // block):
        cut = slice(at * block, (at + 1) * block)
        piece = query_lin[:, cut]
        turned = piece * cosine + swap_pairs(piece) * sine
        query_ref[0, :, cut] = (turned * HD**-0.5).astype(BF16)
        piece = key_lin[:, cut]
        key_ref[0, :, cut] = (piece * cosine + swap_pairs(piece) * sine).astype(BF16)
    live = lax.broadcasted_iota(jnp.int32, (1, rows), 1) < count
    for at in range(width // block):
        cut = slice(at * block, (at + 1) * block)
        keys = key_ref[0, :, cut]
        values = value_ref[0, :, cut]
        results = [None] * (rows // SPAN)
        pieces = [[] for _ in range(rows // SPAN)]
        for head in range(block // HD):
            own_values = head_lanes(values, head)
            for part in range(rows // SPAN):
                queries = head_lanes(query_ref[0, part * SPAN : (part + 1) * SPAN, cut], head)
                scores = jnp.where(live, inner_cols(queries, keys), -1e30)
                top = jnp.max(scores, axis=1, keepdims=True)
                expo = jnp.exp(scores - top)
                total = jnp.sum(expo, axis=1, keepdims=True)
                weights = (expo * (1.0 / total)).astype(BF16)
                result = mm(weights, own_values)
                results[part] = result if head == 0 else results[part] + result
                pieces[part].append(top + jnp.log(total))
        for head in range(block // HD):
            column = jnp.concatenate([pieces[part][head] for part in range(rows // SPAN)], axis=0)
            logs = jnp.where(lane == at * (block // HD) + head, column, logs)
        for part in range(rows // SPAN):
            place = part * SPAN + lax.broadcasted_iota(jnp.int32, (SPAN, block), 0)
            attended_ref[0, part * SPAN : (part + 1) * SPAN, cut] = jnp.where(
                place < count, results[part], 0.0
            ).astype(BF16)
    log_ref[0] = jnp.transpose(logs)[0:8, :]
    total_ref[...] += mm(attended_ref[0], out_ref[step])

    if last:

        @pl.when(step == parts - 1)
        def _():
            def chunk(at, carry):
                here = pl.ds(at * CHUNK, CHUNK)
                branch = total_ref[here, :] + frame_ref[1:2, :]
                branch_ref[here, :] = branch
                state_one = state_ref[here, :] + mod_ref[2:3, :] * branch
                one_ref[here, :] = state_one
                xhat, _ = norm_parts(state_one)
                ffn_ref[here, :] = (xhat * (1.0 + mod_ref[4:5, :]) + mod_ref[3:4, :]).astype(BF16)
                return carry

            lax.fori_loop(0, rows // CHUNK, chunk, 0)


def lay(target_ref, at, start, value):
    model, width = value.shape
    for block in range(model // width):
        target_ref[at, start : start + width, block * width : (block + 1) * width] = value[
            block * width : (block + 1) * width, :
        ]


def feed_forward(pieces, first, last, *refs):
    parts = len(pieces)
    refs = list(refs)

    def take(count=1):
        taken = [refs.pop(0) for _ in range(count)]
        return taken[0] if count == 1 else taken

    half_ref, cotangent_ref, one_ref, branch_ref, source_ref, mod_ref, bias_ref, frame_ref = take(8)
    ups = [[take() for _ in range(number)] for number in pieces]
    downs = [[take() for _ in range(number)] for number in pieces]
    if not first:
        grad_ref, total_in_ref, back_in_ref = take(3)
    grad_bias_ref, sums_ref = take(2)
    grads = [take() for _ in range(parts)]
    if first:
        grad_ref = take()
    if last:
        output_ref, grad_one_ref, grad_attn_ref = take(3)
    else:
        total_ref, back_ref = take(2)
    up_ref, down_ref, up_sem, down_sem = take(4)
    grads_ref, grads_sem = take(2)
    turned_ref, hidden_ref, pre_ref = take(3)
    if last:
        total_ref, back_ref = take(2)
    step = pl.program_id(0)
    rows, wide = one_ref.shape
    inner = 0.7978845608028654
    cubic = 0.044715
    half = half_ref[0]
    copies = [
        slot_copies(ups[at], up_ref, up_sem, at, 0, half)
        + slot_copies(downs[at], down_ref, down_sem, at, 0, half)
        for at in range(parts)
    ]
    results = [
        (pltpu.make_async_copy(grads_ref.at[at], grads[at], grads_sem.at[at]),)
        for at in range(parts)
    ]
    start_all(step, copies)

    @pl.when(step == 0)
    def _():
        if first:

            def chunk(at, carry):
                here = pl.ds(at * CHUNK, CHUNK)
                grad = cotangent_ref[here, :].astype(F32) * mod_ref[5:6, :]
                grad_ref[here, :] = grad.astype(BF16)
                return carry + fold(grad)

            lanes = lax.fori_loop(0, rows // CHUNK, chunk, jnp.zeros((8, wide), F32))
            sums_ref[0:1, :] = jnp.sum(lanes, axis=0, keepdims=True)
            total_ref[...] = jnp.zeros_like(total_ref)
            back_ref[...] = jnp.zeros_like(back_ref)
        else:
            total_ref[...] = total_in_ref[...]
            back_ref[...] = back_in_ref[...]
        turned_ref[...] = jnp.transpose(source_ref[...])

    wait_own(step, copies)
    up = up_ref[step]
    down = down_ref[step]
    lanes = jnp.zeros((8, up.shape[1]), F32)
    for part in range(rows // SPAN):
        here = slice(part * SPAN, (part + 1) * SPAN)
        pre = mm(source_ref[here, :], up) + bias_ref[0]
        grad_hidden = inner_cols(grad_ref[here, :], down)
        square = pre * pre
        bend = jnp.tanh(pre * (inner + inner * cubic * square))
        half = 0.5 * (1.0 + bend)
        hidden = (pre * half).astype(BF16)
        slope = half + 0.5 * pre * (1.0 - bend * bend) * (inner + 3.0 * inner * cubic * square)
        grad_pre = grad_hidden * slope
        lanes = lanes + fold(grad_pre)
        grad_pre = grad_pre.astype(BF16)
        hidden_ref[here, :] = hidden
        pre_ref[here, :] = grad_pre
        total_ref[here, :] += mm(hidden, down)
        back_ref[here, :] += inner_cols(grad_pre, up)
    grad_bias_ref[0] = jnp.sum(lanes, axis=0, keepdims=True)
    width = up_ref.shape[2]
    grads_ref[step, width:, :] = inner_rows(hidden_ref[...], grad_ref[...]).astype(BF16)
    lay(grads_ref, step, 0, mm(turned_ref[...], pre_ref[...]).astype(BF16))
    send_own(step, results)

    if last:

        @pl.when(step == parts - 1)
        def _():
            def chunk(at, carry):
                gate_ffn, scale_ffn, shift_ffn, bias_attn, gate_attn = carry
                here = pl.ds(at * CHUNK, CHUNK)
                branch = total_ref[here, :] + frame_ref[2:3, :]
                state_one = one_ref[here, :]
                output_ref[here, :] = (state_one + mod_ref[5:6, :] * branch).astype(BF16)
                cotangent = cotangent_ref[here, :].astype(F32)
                xhat, root = norm_parts(state_one)
                back = back_ref[here, :]
                grad_one = cotangent + norm_pull(back, mod_ref[4:5, :], xhat, root)
                grad_one_ref[here, :] = grad_one
                grad_attn = grad_one * mod_ref[2:3, :]
                grad_attn_ref[here, :] = grad_attn.astype(BF16)
                return (
                    gate_ffn + fold(cotangent * branch),
                    scale_ffn + fold(back * xhat),
                    shift_ffn + fold(back),
                    bias_attn + fold(grad_attn),
                    gate_attn + fold(grad_one * branch_ref[here, :]),
                )

            start = tuple(jnp.zeros((8, wide), F32) for _ in range(5))
            lanes = lax.fori_loop(0, rows // CHUNK, chunk, start)
            for at, member in enumerate(lanes):
                sums_ref[at + 1 : at + 2, :] = jnp.sum(member, axis=0, keepdims=True)

    wait_all(step, results)


def attention_backward(pieces, first, last, *refs):
    parts = len(pieces)
    refs = list(refs)

    def take(count=1):
        taken = [refs.pop(0) for _ in range(count)]
        return taken[0] if count == 1 else taken

    count_ref, half_ref, grad_attn_ref, normed_ref, mod_ref, cosine_ref, sine_ref = take(7)
    query_ref, key_ref, value_ref, attended_ref, log_ref = take(5)
    weights = [[take() for _ in range(number)] for number in pieces]
    outs = [[take() for _ in range(number)] for number in pieces]
    if not first:
        before_ref = take()
    if last:
        state_ref, grad_one_ref = take(2)
    grad_bias_ref = take()
    grads = [take() for _ in range(parts)]
    if last:
        grad_zero_ref, sums_ref = take(2)
    else:
        back_ref = take()
    weight_ref, out_ref, weight_sem, out_sem = take(4)
    grads_ref, grads_sem = take(2)
    turned_ref, item_ref = take(2)
    if last:
        back_ref = take()
    step = pl.program_id(0)
    rows, wide = normed_ref.shape
    width = weight_ref.shape[3]
    block = cosine_ref.shape[1]
    count = count_ref[0]
    half = half_ref[0]
    copies = [
        slot_copies(weights[at], weight_ref, weight_sem, at, 1, half)
        + slot_copies(outs[at], out_ref, out_sem, at, 0, half)
        for at in range(parts)
    ]
    results = [
        (pltpu.make_async_copy(grads_ref.at[at], grads[at], grads_sem.at[at]),)
        for at in range(parts)
    ]
    start_all(step, copies)

    @pl.when(step == 0)
    def _():
        turned_ref[...] = jnp.transpose(normed_ref[...])
        back_ref[...] = jnp.zeros_like(back_ref) if first else before_ref[...]

    wait_own(step, copies)
    grad_attn = grad_attn_ref[...]
    place = lax.broadcasted_iota(jnp.int32, (rows, width), 0)
    item_ref[...] = jnp.where(place < count, inner_cols(grad_attn, out_ref[step]), 0.0).astype(BF16)
    grads_ref[step, 3 * width :, :] = inner_rows(attended_ref[0], grad_attn).astype(BF16)
    cosine = cosine_ref[...]
    sine = sine_ref[...]
    live = lax.broadcasted_iota(jnp.int32, (rows, 1), 0) < count
    linear = [[], [], []]
    for at in range(width // block):
        cut = slice(at * block, (at + 1) * block)
        keys = key_ref[0, :, cut]
        values = value_ref[0, :, cut]
        keys_turned = jnp.transpose(keys)
        grad_keys = jnp.zeros((rows, block), F32)
        grad_values = jnp.zeros((rows, block), F32)
        grad_queries = [[] for _ in range(rows // SPAN)]
        for head in range(block // HD):
            index = at * (block // HD) + head
            for part in range(rows // SPAN):
                here = slice(part * SPAN, (part + 1) * SPAN)
                queries = head_lanes(query_ref[0, here, cut], head)
                items = head_lanes(item_ref[here, cut], head)
                scores = jnp.where(live, inner_cols(keys, queries), -1e30)
                weights = jnp.exp(scores - log_ref[0, index : index + 1, here])
                grad_weights = inner_cols(values, items)
                along = jnp.sum(grad_weights * weights, axis=0, keepdims=True)
                grad_scores = (weights * (grad_weights - along)).astype(BF16)
                grad_values = grad_values + mm(weights.astype(BF16), items)
                grad_keys = grad_keys + mm(grad_scores, queries)
                grad_queries[part].append(
                    mm(keys_turned[head * HD : (head + 1) * HD, :], grad_scores)
                )
        grad_query = jnp.concatenate(
            [jnp.concatenate(grad_queries[part], axis=0) for part in range(rows // SPAN)], axis=1
        )
        grad_query = jnp.transpose(grad_query) * HD**-0.5
        for which, member in enumerate((grad_query, grad_keys)):
            linear[which].append(member * cosine - swap_pairs(member) * sine)
        linear[2].append(grad_values)
    for which in range(3):
        member = jnp.concatenate(linear[which], axis=1) if width > block else linear[which][0]
        grad_bias_ref[0, which : which + 1, :] = jnp.sum(member, axis=0, keepdims=True)
        member = member.astype(BF16)
        lay(grads_ref, step, which * width, mm(turned_ref[...], member).astype(BF16))
        back_ref[...] += inner_cols(member, weight_ref[step, which])

    send_own(step, results)

    if last:

        @pl.when(step == parts - 1)
        def _():
            def chunk(at, carry):
                scale_attn, shift_attn, bias_in = carry
                here = pl.ds(at * CHUNK, CHUNK)
                xhat, root = norm_parts(state_ref[here, :])
                back = back_ref[here, :]
                grad_zero = grad_one_ref[here, :] + norm_pull(back, mod_ref[1:2, :], xhat, root)
                grad_zero_ref[here, :] = grad_zero.astype(BF16)
                return (
                    scale_attn + fold(back * xhat),
                    shift_attn + fold(back),
                    bias_in + fold(grad_zero),
                )

            start = tuple(jnp.zeros((8, wide), F32) for _ in range(3))
            lanes = lax.fori_loop(0, rows // CHUNK, chunk, start)
            for at, member in enumerate(lanes):
                sums_ref[at : at + 1, :] = jnp.sum(member, axis=0, keepdims=True)

    wait_all(step, results)


def total_of(refs):
    total = refs[0][...].astype(F32)
    for ref in refs[1:]:
        total = total + ref[...].astype(F32)
    return total.astype(BF16)


def sum_kernel(count, *refs):
    refs[count][...] = total_of(refs[:count])


def split_kernel(count, parts, *refs):
    own = refs[0][0]
    sums = [total_of(refs[1 + at * count : 1 + (at + 1) * count]) for at in range(parts)]
    for mask, ref in enumerate(refs[1 + parts * count :]):
        value = sums[mask]
        for at in range(1, parts):
            value = jnp.where(own == at, sums[at ^ mask], value)
        ref[...] = value


def merge_kernel(count, starts_ref, *refs):
    bring(starts_ref, refs[:count], refs[count], refs[count + 1])


def bring(starts_ref, pieces, stack_ref, sems):
    size = pieces[0].shape[0]
    copies = []
    for at, piece in enumerate(pieces):
        start = pl.multiple_of(starts_ref[at], 16)
        copies.append(
            pltpu.make_async_copy(piece, stack_ref.at[pl.ds(start, size), :], sems.at[at])
        )
    for copy in copies:
        copy.start()
    for copy in copies:
        copy.wait()


def unlay(target, stack_ref, start, width):
    for block in range(target.shape[0] // width):
        target[block * width : (block + 1) * width, :] = stack_ref[
            start : start + width, block * width : (block + 1) * width
        ].astype(F32)


def ffn_unpack(count, starts_ref, *refs):
    pieces = refs[:count]
    up_ref, down_ref, stack_ref, sems = refs[count:]
    bring(starts_ref, pieces, stack_ref, sems)
    width = up_ref.shape[1]
    unlay(up_ref, stack_ref, 0, width)
    down_ref[...] = stack_ref[width:, :].astype(F32)


def attn_unpack(count, starts_ref, *refs):
    pieces = refs[:count]
    weight_ref, out_ref, stack_ref, sems = refs[count:]
    bring(starts_ref, pieces, stack_ref, sems)
    width = weight_ref.shape[2]
    for which in range(3):
        unlay(weight_ref.at[which], stack_ref, which * width, width)
    out_ref[...] = stack_ref[3 * width :, :].astype(F32)


def gelu_parts(pre):
    share = 0.5 * (1.0 + lax.erf(pre * 0.7071067811865476))
    slope = share + pre * (0.3989422804014327 * jnp.exp(-0.5 * pre * pre))
    return pre * share, slope


def fill_padded(padded_ref, text_ref):
    rows, wide = text_ref.shape
    edge = jnp.zeros((8, wide), F32)
    padded_ref[0:8, :] = edge
    padded_ref[rows + 8 : rows + 16, :] = edge
    for at in range(rows // CHUNK):
        here = slice(at * CHUNK, (at + 1) * CHUNK)
        padded_ref[at * CHUNK + 8 : (at + 1) * CHUNK + 8, :] = text_ref[here, :].astype(F32)


def text_forward(
    text_ref,
    mel_ref,
    kernel_ref,
    bias_ref,
    gain_ref,
    hidden_bias_ref,
    in_ref,
    out_ref,
    project_ref,
    frame_ref,
    normed_ref,
    pre_ref,
    energy_ref,
    mixed_ref,
    refined_ref,
    state_ref,
    padded_ref,
    hidden_ref,
):
    rows, wide = text_ref.shape
    taps = kernel_ref.shape[0]
    fill_padded(padded_ref, text_ref)

    def front(at, carry):
        start = pl.multiple_of(at * CHUNK, CHUNK)
        near = padded_ref[pl.ds(start, CHUNK + 16), :]
        conv = bias_ref[0:1, :]
        for tap in range(taps):
            shift = 8 + tap - taps // 2
            conv = conv + near[shift : shift + CHUNK, :] * kernel_ref[tap : tap + 1, :]
        xhat, _ = norm_parts(conv)
        normed_ref[pl.ds(start, CHUNK), :] = (xhat * gain_ref[...] + bias_ref[1:2, :]).astype(BF16)
        return carry

    lax.fori_loop(0, rows // CHUNK, front, 0)
    pre_ref[...] = mm(normed_ref[...], in_ref[...]) + hidden_bias_ref[0:1, :]

    def gelu(at, carry):
        here = pl.ds(at * CHUNK, CHUNK)
        hidden, _ = gelu_parts(pre_ref[here, :])
        hidden_ref[here, :] = hidden
        return carry + fold(hidden * hidden)

    squares = lax.fori_loop(0, rows // CHUNK, gelu, jnp.zeros((8, pre_ref.shape[1]), F32))
    energy = jnp.sqrt(jnp.sum(squares, axis=0, keepdims=True))
    energy_ref[0:1, :] = energy
    ratio = energy / (jnp.mean(energy, axis=1, keepdims=True) + 1e-06)

    def mix(at, carry):
        here = pl.ds(at * CHUNK, CHUNK)
        hidden = hidden_ref[here, :]
        mixed = hidden_bias_ref[1:2, :] * (hidden * ratio) + hidden_bias_ref[2:3, :] + hidden
        mixed_ref[here, :] = mixed.astype(BF16)
        return carry

    lax.fori_loop(0, rows // CHUNK, mix, 0)
    refined_ref[...] = (
        text_ref[...].astype(F32) + mm(mixed_ref[...], out_ref[...]) + bias_ref[2:3, :]
    ).astype(BF16)
    state_ref[...] = (
        mm(mel_ref[...], project_ref[0 : mel_ref.shape[1], :])
        + mm(refined_ref[...], project_ref[mel_ref.shape[1] :, :])
        + frame_ref[0:1, :]
    )


def full_line(members, wide):
    have = sum(member.shape[1] for member in members)
    return jnp.concatenate(list(members) + [jnp.zeros((1, wide - have), F32)], axis=1)


def small_rows(group):
    count = 12 + 2 * group
    return count + -count % 16


def text_backward(group, *refs):
    refs = list(refs)

    def take(count=1):
        taken = [refs.pop(0) for _ in range(count)]
        return taken[0] if count == 1 else taken

    own_ref, grad_zero_ref, text_ref, mel_ref, refined_ref, mixed_ref, normed_ref = take(7)
    pre_ref, energy_ref, kernel_ref, bias_ref, gain_ref, hidden_bias_ref = take(6)
    in_ref, out_ref, project_ref, attn_sums_ref, ffn_sums_ref = take(5)
    high_bias_ref, low_bias_ref, up_bias_ref, active_ref = take(4)
    grad_text_ref, mods_ref = take(2)
    slots = [take() for _ in range(group)]
    stack_ref, sems, padded_ref, outer_ref, refined_grad_ref, low_ref, mixed_grad_ref = take(7)
    pre_low_ref, normed_grad_ref, lines_ref = take(3)
    small = small_rows(group)
    own = own_ref[0]
    rows, wide = text_ref.shape
    model = grad_zero_ref.shape[1]
    taps = kernel_ref.shape[0]
    mel_at = 3 * wide
    small_at = mel_at + mel_ref.shape[1] + (-(mel_at + mel_ref.shape[1])) % 16

    lines = [attn_sums_ref[1:2, :], attn_sums_ref[0:1, :]]
    lines += [ffn_sums_ref[row : row + 1, :] for row in (5, 3, 2, 1)]
    mods_at = small_at + small
    stack_ref[mods_at:, :] = jnp.zeros((stack_ref.shape[0] - mods_at, model), BF16)
    for at, member in enumerate(lines):
        mods_ref[at : at + 1, :] = member.astype(BF16)
    lines += [active_ref[...].astype(F32), jnp.zeros((1, model), F32)]
    lines = jnp.concatenate(lines, axis=0)
    empty = jnp.zeros_like(lines)
    odd = own_ref[1] % 2 == 1
    lines = jnp.where(
        odd, jnp.concatenate([empty, lines], axis=0), jnp.concatenate([lines, empty], axis=0)
    )
    place = pl.multiple_of(mods_at + own_ref[1] // 2 * 16, 16)
    stack_ref[pl.ds(place, 16), :] = lines.astype(BF16)

    grad_zero = grad_zero_ref[...]
    grad_refined = inner_cols(grad_zero, project_ref[mel_ref.shape[1] :, :])
    refined_grad_ref[...] = grad_refined
    low_ref[...] = grad_refined.astype(BF16)
    sum_out = jnp.sum(fold(grad_refined), axis=0, keepdims=True)
    mixed_grad_ref[...] = inner_cols(low_ref[...], out_ref[...])
    stack_ref[0:wide, :] = inner_rows(refined_ref[...], grad_zero).astype(BF16)
    spare = jnp.zeros((small_at - mel_at - mel_ref.shape[1], model), F32)
    grad_mel = inner_rows(mel_ref[...], grad_zero)
    stack_ref[mel_at:small_at, :] = jnp.concatenate([grad_mel, spare], axis=0).astype(BF16)
    grad_out = inner_rows(mixed_ref[...], low_ref[...]).astype(BF16)
    stack_ref[2 * wide : 3 * wide, 0:wide] = grad_out[0:wide, :]
    stack_ref[2 * wide : 3 * wide, wide:] = grad_out[wide:, :]

    energy = energy_ref[0:1, :]
    mean = jnp.mean(energy, axis=1, keepdims=True) + 1e-06
    ratio = energy / mean

    def first_pass(at, carry):
        along, plain = carry
        here = pl.ds(at * CHUNK, CHUNK)
        hidden, _ = gelu_parts(pre_ref[here, :])
        grad = mixed_grad_ref[here, :]
        return along + fold(grad * hidden), plain + fold(grad)

    zero = jnp.zeros((8, model), F32)
    along, plain = lax.fori_loop(0, rows // CHUNK, first_pass, (zero, zero))
    along = jnp.sum(along, axis=0, keepdims=True)
    sum_beta = jnp.sum(plain, axis=0, keepdims=True)
    gamma = hidden_bias_ref[1:2, :]
    grad_ratio = gamma * along
    grad_mean = jnp.sum(grad_ratio * energy, axis=1, keepdims=True) / (mean * mean)
    grad_energy = grad_ratio / mean - grad_mean / model
    spread = grad_energy / energy
    factor = 1.0 + gamma * ratio

    def second_pass(at, carry):
        here = pl.ds(at * CHUNK, CHUNK)
        hidden, slope = gelu_parts(pre_ref[here, :])
        grad = (mixed_grad_ref[here, :] * factor + hidden * spread) * slope
        pre_low_ref[here, :] = grad.astype(BF16)
        return carry + fold(grad)

    sum_in = jnp.sum(lax.fori_loop(0, rows // CHUNK, second_pass, zero), axis=0, keepdims=True)
    normed_grad_ref[...] = inner_cols(pre_low_ref[...], in_ref[...])
    stack_ref[wide : 2 * wide, :] = inner_rows(normed_ref[...], pre_low_ref[...]).astype(BF16)

    fill_padded(padded_ref, text_ref)
    edge = jnp.zeros((8, wide), F32)
    outer_ref[0:8, :] = edge
    outer_ref[rows + 8 : rows + 16, :] = edge
    narrow = jnp.zeros((8, wide), F32)
    step = CHUNK // 2

    def conv_back(at, carry):
        sum_gain, sum_norm, sum_conv, sum_taps = carry
        start = pl.multiple_of(at * step, step)
        near = padded_ref[pl.ds(start, step + 16), :]
        conv = bias_ref[0:1, :]
        for tap in range(taps):
            shift = 8 + tap - taps // 2
            conv = conv + near[shift : shift + step, :] * kernel_ref[tap : tap + 1, :]
        xhat, root = norm_parts(conv)
        grad = normed_grad_ref[pl.ds(start, step), :]
        entry = grad * gain_ref[...]
        entry_mean = jnp.mean(entry, axis=-1, keepdims=True)
        entry_along = jnp.mean(entry * xhat, axis=-1, keepdims=True)
        grad_conv = root * (entry - entry_mean - xhat * entry_along)
        outer_ref[pl.ds(start + 8, step), :] = grad_conv
        sum_taps = tuple(
            member
            + fold(grad_conv * near[8 + tap - taps // 2 : 8 + tap - taps // 2 + step, :])
            for tap, member in enumerate(sum_taps)
        )
        return (
            sum_gain + fold(grad * xhat),
            sum_norm + fold(grad),
            sum_conv + fold(grad_conv),
            sum_taps,
        )

    sum_gain, sum_norm, sum_conv, sum_taps = lax.fori_loop(
        0, rows // step, conv_back, (narrow, narrow, narrow, (narrow,) * taps)
    )

    def text_grad(at, carry):
        start = pl.multiple_of(at * CHUNK, CHUNK)
        near = outer_ref[pl.ds(start, CHUNK + 16), :]
        total = refined_grad_ref[pl.ds(start, CHUNK), :]
        for tap in range(taps):
            shift = 8 + taps // 2 - tap
            total = total + near[shift : shift + CHUNK, :] * kernel_ref[tap : tap + 1, :]
        grad_text_ref[pl.ds(start, CHUNK), :] = total
        return carry

    lax.fori_loop(0, rows // CHUNK, text_grad, 0)

    def line(member):
        return jnp.sum(member, axis=0, keepdims=True)

    halves = [line(member) for member in sum_taps] + [line(sum_gain)]
    halves += [line(sum_conv), line(sum_norm), sum_out, jnp.zeros((1, wide), F32)]
    lines = [
        jnp.concatenate(halves[at : at + 2], axis=1) for at in range(0, len(halves), 2)
    ]
    lines += [sum_in, ratio * along, sum_beta]
    lines += [attn_sums_ref[2:3, :], ffn_sums_ref[4:5, :], ffn_sums_ref[0:1, :]]
    lines_ref[...] = jnp.zeros_like(lines_ref)
    for at, member in enumerate(lines):
        lines_ref[at : at + 1, :] = member
    parts = group // 2
    row = lax.broadcasted_iota(jnp.int32, lines_ref.shape, 0)
    total = lines_ref[...]
    for slot in range(group):
        source_ref = low_bias_ref if slot < parts else high_bias_ref
        owner = jnp.bitwise_xor(own, slot)
        members = [source_ref[slot % parts, which : which + 1, :] for which in range(3)]
        total = jnp.where(row == 12 + owner, full_line(members, model), total)
        total = jnp.where(row == 12 + group + owner, full_line([up_bias_ref[slot]], model), total)
    lines_ref[...] = total
    stack_ref[small_at : small_at + small, :] = lines_ref[...].astype(BF16)

    size = stack_ref.shape[0] // group
    copies = []
    for slot in range(group):
        start = pl.multiple_of(jnp.bitwise_xor(own, slot) * size, size)
        copies.append(
            pltpu.make_async_copy(stack_ref.at[pl.ds(start, size), :], slots[slot], sems.at[slot])
        )
    for copy in copies:
        copy.start()
    for copy in copies:
        copy.wait()


def text_unpack(count, group, utterances, starts_ref, own_ref, *refs):
    pieces = refs[:count]
    project_ref, in_ref, out_ref, taps_ref, bias_ref, gain_ref = refs[count : count + 6]
    hidden_ref, frame_ref, qkv_bias_ref, up_bias_ref = refs[count + 6 : count + 10]
    mod_ref, mod_bias_ref, stack_ref, sems, lines_ref = refs[count + 10 :]
    bring(starts_ref, pieces, stack_ref, sems)
    own = own_ref[0]
    wide = in_ref.shape[0]
    taps = taps_ref.shape[0]
    mels = project_ref.shape[0] - wide
    mel_at = 3 * wide
    small_at = mel_at + mels + (-(mel_at + mels)) % 16
    project_ref[0:mels, :] = stack_ref[mel_at : mel_at + mels, :].astype(F32)
    project_ref[mels:, :] = stack_ref[0:wide, :].astype(F32)
    in_ref[...] = stack_ref[wide : 2 * wide, :].astype(F32)
    out_ref[0:wide, :] = stack_ref[2 * wide : 3 * wide, 0:wide].astype(F32)
    out_ref[wide:, :] = stack_ref[2 * wide : 3 * wide, wide:].astype(F32)
    lines_ref[...] = stack_ref[small_at : small_at + small_rows(group), :].astype(F32)
    mods_at = small_at + small_rows(group)
    mods = stack_ref[mods_at : mods_at + 8 * utterances, :].astype(F32)
    mods = mods.reshape(utterances, 8, mods.shape[1])
    place = lax.broadcasted_iota(jnp.int32, mods.shape, 1)

    def block_rows(at):
        return jnp.sum(jnp.where(place == at, mods, 0.0), axis=1)

    active = block_rows(6).astype(BF16)
    unit = mod_ref.shape[1] // 3
    share = mods.shape[2] // unit
    for at in range(3):
        index = own * 3 + at
        line = block_rows(index // share)
        piece = line[:, 0:unit]
        for other in range(1, share):
            piece = jnp.where(
                index % share == other, line[:, other * unit : (other + 1) * unit], piece
            )
        cut = slice(at * unit, (at + 1) * unit)
        mod_bias_ref[:, cut] = jnp.sum(piece, axis=0, keepdims=True)
        mod_ref[:, cut] = inner_rows(active, piece.astype(BF16))

    def half(at):
        return lines_ref[at // 2 : at // 2 + 1, (at % 2) * wide : (at % 2 + 1) * wide]

    for tap in range(taps):
        taps_ref[tap : tap + 1, :] = half(tap)
    gain_ref[...] = half(taps)
    for at in range(3):
        bias_ref[at : at + 1, :] = half(taps + 1 + at)
    first = (taps + 5) // 2
    hidden_ref[...] = lines_ref[first : first + 3, :]
    frame_ref[...] = lines_ref[first + 3 : first + 6, :]
    row = lax.broadcasted_iota(jnp.int32, lines_ref.shape, 0)

    def pick(at):
        return jnp.sum(jnp.where(row == at, lines_ref[...], 0.0), axis=0, keepdims=True)

    line = pick(12 + own)
    width = qkv_bias_ref.shape[1]
    for which in range(3):
        qkv_bias_ref[which : which + 1, :] = line[:, which * width : (which + 1) * width]
    up_bias_ref[...] = pick(12 + group + own)[:, 0 : up_bias_ref.shape[1]]


ANY = pl.BlockSpec(memory_space=pl.ANY)
SMEM = pl.BlockSpec(memory_space=pltpu.SMEM)


def whole(shape):
    return pl.BlockSpec(shape, lambda g: (0,) * len(shape))


def held(shape, parts=None):
    if parts is None:
        return pl.BlockSpec((1,) + shape, lambda g: (g,) + (0,) * len(shape))
    return pl.BlockSpec((1,) + shape, lambda g: (parts - 1 - g,) + (0,) * len(shape))


def run_kernel(kernel, parts, inputs, outputs, scratch):
    return pl.pallas_call(
        kernel,
        grid=(parts,),
        in_specs=[spec for spec, _ in inputs],
        out_specs=[spec for spec, _, _ in outputs],
        out_shape=[jax.ShapeDtypeStruct(shape, kind) for _, shape, kind in outputs],
        scratch_shapes=scratch,
        compiler_params=pltpu.CompilerParams(vmem_limit_bytes=VMEM),
        cost_estimate=pl.CostEstimate(flops=1024, bytes_accessed=1024, transcendentals=0),
    )(*[array for _, array in inputs])


def after(arrays, *others):
    arrays = tuple(arrays)
    return lax.optimization_barrier(arrays + others)[: len(arrays)]


def swap(array, axis, bit):
    return lax.ppermute(array, axis, [(at, at ^ bit) for at in range(lax.axis_size(axis))])


def low_bit(slot):
    return slot & -slot


def tile_rows(rows):
    return next(size for size in (256, 224, 128, 112, 96, 80, 64, 48, 32, 16) if rows % size == 0)


def add_arrays(arrays):
    rows, wide = arrays[0].shape
    tile = tile_rows(rows)
    spec = pl.BlockSpec((tile, wide), lambda g: (g, 0))
    return run_kernel(
        partial(sum_kernel, len(arrays)),
        rows // tile,
        [(spec, array) for array in arrays],
        [(spec, (rows, wide), BF16)],
        [],
    )[0]


def add_and_split(arrays, own, parts):
    rows, wide = arrays[0].shape
    size = rows // parts
    tile = tile_rows(size)
    steps = size // tile

    def block_at(part):
        return pl.BlockSpec((tile, wide), lambda g: (g + part * steps, 0))

    return run_kernel(
        partial(split_kernel, len(arrays), parts),
        steps,
        [(SMEM, own.astype(jnp.int32).reshape(1))]
        + [(block_at(part), array) for part in range(parts) for array in arrays],
        [(block_at(0), (size, wide), BF16)] * parts,
        [],
    )


def merge(pieces, starts, rows):
    return run_kernel(
        partial(merge_kernel, len(pieces)),
        1,
        [(SMEM, jnp.stack(starts).astype(jnp.int32))] + [(ANY, piece) for piece in pieces],
        [(whole((rows, pieces[0].shape[1])), (rows, pieces[0].shape[1]), BF16)],
        [pltpu.SemaphoreType.DMA((len(pieces),))],
    )[0]


class Fetch:
    def __init__(self, array, axis):
        size = array.shape[axis] // 2
        start = lax.axis_index("dp") % 2 * size
        self.half = lax.dynamic_slice_in_dim(array, start, size, axis=axis)
        self.group = lax.axis_size("heads")
        self.slots = {0: [array]}
        self.sent = {}

    def core(self, slot, *others):
        pieces = after(self.slots[slot], *others)
        self.slots[slot + 1] = [swap(piece, "heads", 1) for piece in pieces]

    def send(self, *others):
        (self.half,) = after([self.half], *others)
        for slot in range(2, self.group, 2):
            bit = low_bit(slot)
            if slot == bit:
                self.sent[slot] = swap(self.half, "heads", bit)

    def share(self, *others):
        for slot in range(2, self.group, 2):
            bit = low_bit(slot)
            if slot == bit:
                (came,) = after([self.sent[slot]], *others)
            else:
                came = swap(self.slots[slot - bit][0], "heads", bit)
            self.slots[slot] = [came, swap(came, "dp", 1)]

    def cores(self, first, last, *others):
        for slot in range(first, last, 2):
            self.core(slot, *others)

    def listed(self):
        return [self.slots[slot] for slot in range(self.group)]


def flat(slots):
    return [piece for pieces in slots for piece in pieces]


class GroupSum:
    def __init__(self):
        self.arrived = {}

    def put(self, slot, array, *others):
        arrays = [array] + self.arrived.pop(slot, [])
        if slot == 0:
            return arrays
        total = add_arrays(after(arrays, *others)) if len(arrays) > 1 else array
        bit = low_bit(slot)
        self.arrived.setdefault(slot - bit, []).append(swap(total, "heads", bit))
        return total


class DataSum:
    def __init__(self, arrays, bits, merged=False):
        self.merged = merged
        self.arrays = list(arrays)
        self.bits = list(bits)
        self.halved = []
        self.rows = arrays[0].shape[0]
        self.pieces = None

    def step(self, *others):
        arrays = after(self.arrays, *others)
        if not self.bits:
            total = add_arrays(arrays)
            self.gather(total)
            return total
        bit = self.bits.pop(0)
        keep, send = add_and_split(arrays, lax.axis_index("dp") // bit % 2, 2)
        self.halved.append(bit)
        self.arrays = [keep, swap(send, "dp", bit)]
        return keep

    def gather(self, total):
        self.pieces = {0: total}
        for bit in self.halved[: 0 if self.merged else None : -1]:
            for mask, piece in list(self.pieces.items()):
                self.pieces[mask | bit] = swap(piece, "dp", bit)

    def half(self, *others):
        starts = [start % (self.rows // 2) for start in self.starts()]
        return merge(after(self.pieces.values(), *others), starts, self.rows // 2)

    def starts(self):
        own = lax.axis_index("dp")
        return [
            sum(
                (own ^ mask) // bit % 2 * (self.rows >> (at + 1))
                for at, bit in enumerate(self.halved)
            )
            for mask in self.pieces
        ]


def axis_bits(axis):
    size = lax.axis_size(axis)
    return [1 << at for at in range(size.bit_length() - 1)]


def on_device(
    noisy_mel,
    cond_mel,
    text_embed,
    time_embed,
    lengths,
    spans,
    dw_kernel,
    text_bias,
    text_gain,
    text_hidden,
    pw_in,
    pw_out,
    in_proj,
    frame_bias,
    mod_weight,
    mod_bias,
    qkv_weight,
    qkv_bias,
    out_weight,
    ff_in,
    ff_in_bias,
    ff_out,
    cotangent,
):
    group = lax.axis_size("heads")
    own = lax.axis_index("heads")
    own_data = lax.axis_index("dp")
    rows = text_embed.shape[0]
    model_width = in_proj.shape[1]
    width = qkv_weight.shape[2]
    units = ff_in.shape[1]
    block = min(128, width)
    parts = group // 2
    full = (rows, model_width)

    fetches = [Fetch(qkv_weight, 1), Fetch(out_weight, 0), Fetch(ff_in, 0), Fetch(ff_out, 0)]
    for fetch in fetches[:2]:
        fetch.send()
        fetch.core(0)

    position = jnp.arange(rows, dtype=jnp.int32)
    inside = (position >= spans[0, 0]) & (position < spans[0, 1])
    keep = jnp.where(inside, 0.0, 1.0).astype(F32)[:, None]
    count = lax.dynamic_slice_in_dim(lengths, own, 1)
    lane = jnp.arange(block, dtype=jnp.int32)
    pair = ((lane % HD) // 2).astype(F32)
    angle = position.astype(F32)[:, None] * (10000.0 ** (-2.0 * pair / HD))[None, :]
    cosine = jnp.cos(angle)
    sine = jnp.sin(angle) * jnp.where(lane % 2 == 0, -1.0, 1.0)[None, :]

    cond_low = (cond_mel.astype(F32) * keep).astype(BF16)
    mel = jnp.concatenate([noisy_mel, cond_low], axis=1)
    mels = mel.shape[1]
    text_width = text_embed.shape[1]
    gain = text_gain[None, :]

    def block_of(array):
        return (whole(array.shape), array)

    normed_text, pre_act, energy, mixed_text, refined, state_zero = run_kernel(
        text_forward,
        1,
        [
            block_of(member)
            for member in (
                text_embed,
                mel,
                dw_kernel,
                text_bias,
                gain,
                text_hidden,
                pw_in,
                pw_out,
                in_proj,
                frame_bias,
            )
        ],
        [
            (whole(shape), shape, kind)
            for shape, kind in (
                ((rows, text_width), BF16),
                ((rows, pw_in.shape[1]), F32),
                ((8, pw_in.shape[1]), F32),
                ((rows, pw_in.shape[1]), BF16),
                ((rows, text_width), BF16),
                (full, F32),
            )
        ],
        [pltpu.VMEM((rows + 16, text_width), F32), pltpu.VMEM((rows, pw_in.shape[1]), F32)],
    )

    def semaphores(number, pieces=2):
        shape = (number, pieces) if pieces > 1 else (number,)
        return pltpu.SemaphoreType.DMA(shape)

    def attn_buffers(number, pieces=2):
        return [
            pltpu.VMEM((number, 3, model_width, width), BF16),
            pltpu.VMEM((number, width, model_width), BF16),
            semaphores(number, pieces),
            semaphores(number, pieces),
        ]

    def ffn_buffers(number, pieces=2):
        return [
            pltpu.VMEM((number, model_width, units), BF16),
            pltpu.VMEM((number, units, model_width), BF16),
            semaphores(number, pieces),
            semaphores(number, pieces),
        ]

    half_index = (own_data % 2).astype(jnp.int32).reshape(1)

    def pieces_of(slots):
        return tuple(len(pieces) for pieces in slots)

    (time_late,) = after([time_embed], state_zero)
    time_rows = time_late.astype(F32)
    activated, silu_back = jax.vjp(jax.nn.silu, time_rows)
    activated_low = activated.astype(BF16)
    modulation = (mm(activated_low, mod_weight) + mod_bias).astype(BF16)
    biases = jnp.concatenate([qkv_bias.reshape(-1), ff_in_bias])
    riders = jnp.broadcast_to(biases[None, :], (group, biases.size))
    sent = jnp.concatenate([modulation, riders], axis=1)
    came = lax.all_to_all(sent, "heads", split_axis=0, concat_axis=1, tiled=True)
    came = came.reshape(group, sent.shape[1]).astype(F32)
    mod_rows = came[:, : modulation.shape[1]].reshape(6, model_width)
    slot_owner = jnp.bitwise_xor(jnp.arange(group, dtype=jnp.int32), own)
    biases_all = jnp.take(came[:, modulation.shape[1] :], slot_owner, axis=0)
    qkv_bias_all = biases_all[:, : 3 * width].reshape(group, 3, width)
    up_bias_all = biases_all[:, 3 * width :].reshape(group, 1, units)

    for fetch in fetches[2:]:
        fetch.send(came)
    for fetch in fetches[:2]:
        fetch.share()
        fetch.cores(2, parts)
    (mod_rows,) = after([mod_rows], *[fetch.sent[2] for fetch in fetches[:2]])
    kept = []
    for turn in range(2):
        first, last = turn == 0, turn == 1
        if last:
            for fetch in fetches[:2]:
                fetch.cores(parts, group, normed)
            for fetch in fetches[2:]:
                fetch.share(normed)
                fetch.core(0, normed)
            own_index = jnp.stack([own, own_data * group + own]).astype(jnp.int32)
            own_active = lax.dynamic_index_in_dim(activated_low, own, 0)
            before, own_index, own_active = lax.optimization_barrier(
                (before, own_index, own_active)
            )
            (before,) = after([before], *[fetch.slots[2][0] for fetch in fetches[2:]])
        chosen = range(turn * parts, (turn + 1) * parts)
        qkv_here = [fetches[0].slots[slot] for slot in chosen]
        out_here = [fetches[1].slots[slot] for slot in chosen]
        inputs = [
            (SMEM, count),
            (SMEM, half_index),
            (whole(full), state_zero),
            (whole((6, model_width)), mod_rows),
            (held((3, width)), qkv_bias_all[chosen[0] : chosen[-1] + 1]),
            (whole((3, model_width)), frame_bias),
            (whole((rows, block)), cosine),
            (whole((rows, block)), sine),
        ]
        inputs += [(ANY, member) for member in flat(qkv_here) + flat(out_here)]
        if not first:
            inputs += [(whole(full), normed), (whole(full), before)]
        outputs = [(held((rows, width)), (parts, rows, width), BF16)] * 4
        outputs += [(held((8, rows)), (parts, 8, rows), F32)]
        if first:
            outputs += [(whole(full), full, BF16)]
        outputs += [(whole(full), full, F32)]
        if last:
            outputs += [(whole(full), full, F32), (whole(full), full, BF16)]
        results = run_kernel(
            partial(attention_forward, pieces_of(qkv_here), first, last),
            parts,
            inputs,
            outputs,
            attn_buffers(parts) + ([pltpu.VMEM(full, F32)] if last else []),
        )
        kept.append(results[:5])
        if first:
            normed, before = results[5:]
        else:
            branch, state_one, ffn_in = results[5:]

    qkv_all, out_all = fetches[0].listed(), fetches[1].listed()
    fetches[2].cores(2, group, ffn_in)
    fetches[3].cores(2, group, ffn_in)
    up_all, down_all = fetches[2].listed()[::-1], fetches[3].listed()[::-1]
    inputs = [
        (SMEM, half_index),
        (whole(full), cotangent),
        (whole(full), state_one),
        (whole(full), branch),
        (whole(full), ffn_in),
        (whole((6, model_width)), mod_rows),
        (held((1, units), group), up_bias_all),
        (whole((3, model_width)), frame_bias),
    ]
    inputs += [(ANY, member) for member in flat(up_all) + flat(down_all)]
    merged = (2 * units, model_width)
    outputs = [(held((1, units), group), (group, 1, units), F32)]
    outputs += [(whole((8, model_width)), (8, model_width), F32)]
    outputs += [(ANY, merged, BF16)] * group
    outputs += [(whole(full), full, BF16)] * 2 + [(whole(full), full, F32)]
    outputs += [(whole(full), full, BF16)]
    results = run_kernel(
        partial(feed_forward, pieces_of(up_all), True, True),
        group,
        inputs,
        outputs,
        [
            pltpu.VMEM((group, model_width, units), BF16),
            pltpu.VMEM((group, units, model_width), BF16),
            semaphores(group),
            semaphores(group),
            pltpu.VMEM((group,) + merged, BF16),
            semaphores(group, 1),
            pltpu.VMEM((model_width, rows), BF16),
            pltpu.VMEM((rows, units), BF16),
            pltpu.VMEM((rows, units), BF16),
        ]
        + [pltpu.VMEM(full, F32)] * 2,
    )
    grad_up_bias, ffn_sums = results[:2]
    output, grad_one, grad_attn = results[3 + group :]
    ffn_grads = results[2 : 2 + group][::-1]

    attn_grads = []
    merged = (4 * width, model_width)
    qkv_bias_parts = []
    for turn in range(2):
        first, last = turn == 0, turn == 1
        chosen = [group - 1 - turn * parts - at for at in range(parts)]
        inputs = [
            (SMEM, count),
            (SMEM, half_index),
            (whole(full), grad_attn),
            (whole(full), normed),
            (whole((6, model_width)), mod_rows),
            (whole((rows, block)), cosine),
            (whole((rows, block)), sine),
        ]
        inputs += [(held((rows, width), parts), member) for member in kept[1 - turn][:4]]
        inputs += [(held((8, rows), parts), kept[1 - turn][4])]
        inputs += [(ANY, member) for member in flat([qkv_all[slot] for slot in chosen])]
        inputs += [(ANY, member) for member in flat([out_all[slot] for slot in chosen])]
        if not first:
            inputs += [(whole(full), back)]
        if last:
            inputs += [(whole(full), state_zero), (whole(full), grad_one)]
        outputs = [(held((3, width), parts), (parts, 3, width), F32)]
        outputs += [(ANY, merged, BF16)] * parts
        if last:
            outputs += [(whole(full), full, BF16), (whole((8, model_width)), (8, model_width), F32)]
        else:
            outputs += [(whole(full), full, F32)]
        results = run_kernel(
            partial(attention_backward, pieces_of([qkv_all[slot] for slot in chosen]), first, last),
            parts,
            inputs,
            outputs,
            attn_buffers(parts)
            + [pltpu.VMEM((parts,) + merged, BF16), semaphores(parts, 1)]
            + [pltpu.VMEM((model_width, rows), BF16), pltpu.VMEM((rows, width), BF16)]
            + ([pltpu.VMEM(full, F32)] if last else []),
        )
        qkv_bias_parts.append(results[0])
        attn_grads = list(results[1 : 1 + parts])[::-1] + attn_grads
        if first:
            back = results[1 + parts]
            ffn_sum = GroupSum()
            token = back
            for slot in range(group - 1, 0, -1):
                total = ffn_sum.put(slot, ffn_grads[slot], token)
                if slot % 2 == 0:
                    token = total
            (back,) = after([back], token)
        else:
            grad_zero, attn_sums = results[1 + parts :]
    token = grad_zero
    attn_sum = GroupSum()
    for slot in range(group - 1, 0, -1):
        total = attn_sum.put(slot, attn_grads[slot], token)
        if slot % 2 == 0:
            token = total
    (grad_zero,) = after([grad_zero], token)

    data = lax.axis_size("dp")
    stack_rows = 3 * text_width + mels
    stack_rows += -stack_rows % 16 + small_rows(group) + 8 * group * data
    stack_rows += -stack_rows % (16 * group * data)
    results = run_kernel(
        partial(text_backward, group),
        1,
        [(SMEM, own_index)]
        + [
            block_of(member)
            for member in (
                grad_zero,
                text_embed,
                mel,
                refined,
                mixed_text,
                normed_text,
                pre_act,
                energy,
                dw_kernel,
                text_bias,
                gain,
                text_hidden,
                pw_in,
                pw_out,
                in_proj,
                attn_sums,
                ffn_sums,
                qkv_bias_parts[0],
                qkv_bias_parts[1],
                grad_up_bias,
                own_active,
            )
        ],
        [
            (whole((rows, text_width)), (rows, text_width), F32),
            (whole((6, model_width)), (6, model_width), BF16),
        ]
        + [(ANY, (stack_rows // group, model_width), BF16)] * group,
        [
            pltpu.VMEM((stack_rows, model_width), BF16),
            semaphores(group, 1),
            pltpu.VMEM((rows + 16, text_width), F32),
            pltpu.VMEM((rows + 16, text_width), F32),
            pltpu.VMEM((rows, text_width), F32),
            pltpu.VMEM((rows, text_width), BF16),
            pltpu.VMEM((rows, pw_in.shape[1]), F32),
            pltpu.VMEM((rows, pw_in.shape[1]), BF16),
            pltpu.VMEM((rows, text_width), F32),
            pltpu.VMEM((small_rows(group), model_width), F32),
        ],
    )
    grad_text, grad_mod = results[:2]
    def unpack(kernel, data, first, second, *others):
        pieces = after(data.pieces.values(), *others)
        return run_kernel(
            partial(kernel, len(pieces)),
            1,
            [(SMEM, jnp.stack(data.starts()).astype(jnp.int32))]
            + [(ANY, member) for member in pieces],
            [(whole(first.shape), first.shape, F32), (whole(second.shape), second.shape, F32)],
            [pltpu.VMEM((data.rows, model_width), BF16), semaphores(len(pieces), 1)],
        )

    bits = axis_bits("dp")
    ffn_data = DataSum(ffn_sum.put(0, ffn_grads[0]), bits)
    token = ffn_data.step(grad_mod)
    text_sum = GroupSum()
    for slot in range(group - 1, 0, -1):
        total = text_sum.put(slot, results[2 + slot], token)
        if slot % 2 == 0:
            token = total
    attn_data = DataSum(attn_sum.put(0, attn_grads[0]), bits)
    text_data = DataSum(text_sum.put(0, results[2]), bits, merged=True)
    steps = [(at, ffn_data) for at in range(1, len(bits) + 1)]
    for at in range(len(bits) + 1):
        steps.append((at + 1.9 if at else 1.5, attn_data))
        steps.append((at + 2.25, text_data))
    steps.sort(key=lambda step: step[0])
    columns = mod_weight.shape[1]
    grad_time = None
    for at, member in steps:
        if at > len(bits) and member is attn_data and grad_time is None:
            (grad_mod,) = after([grad_mod], token)
            grad_mod = grad_mod.reshape(1, group * columns)
            grad_cols = lax.all_to_all(grad_mod, "heads", split_axis=1, concat_axis=0, tiled=True)
            (grad_time,) = silu_back(inner_cols(grad_cols, mod_weight))
            token = member.step(token, grad_time)
        elif at == steps[-1][0]:
            (grad_time,) = after([grad_time], token)
            grad_time = jnp.broadcast_to(grad_time.astype(BF16), (group,) + grad_time.shape)
            grad_time = lax.all_to_all(grad_time, "heads", split_axis=0, concat_axis=0)
            grad_time = jnp.sum(grad_time.astype(F32), axis=0)
            token = member.step(token, grad_time)
        else:
            token = member.step(token)

    weight_up, weight_down = unpack(ffn_unpack, ffn_data, ff_in, ff_out, attn_data.pieces[0])
    text_half = text_data.half(weight_up, *list(attn_data.pieces.values())[1:-2])
    weight_qkv, weight_out = unpack(attn_unpack, attn_data, qkv_weight, out_weight, text_half)
    text_halves = {0: [text_half]}
    for slot in range(2, group, 2):
        bit = low_bit(slot)
        text_halves[slot] = [swap(text_halves[slot - bit][0], "heads", bit)]
    for slot in range(0, group, 2):
        text_halves[slot].append(swap(text_halves[slot][0], "dp", 1))
        pieces = after(text_halves[slot], weight_qkv) if slot else text_halves[slot]
        text_halves[slot + 1] = [swap(piece, "heads", 1) for piece in pieces]
    slot_rows = stack_rows // group
    text_pieces, text_starts = [], []
    for slot, pieces in text_halves.items():
        for which, piece in enumerate(pieces):
            text_pieces.append(piece)
            text_starts.append(
                slot_owner[slot] * slot_rows + ((own_data + which) % 2) * (slot_rows // 2)
            )
    unpacked = (
        in_proj.shape,
        pw_in.shape,
        pw_out.shape,
        dw_kernel.shape,
        text_bias.shape,
        gain.shape,
        text_hidden.shape,
        frame_bias.shape,
        (3, width),
        (1, units),
    )
    mods_shape = mod_weight.shape
    unpacked = run_kernel(
        partial(text_unpack, len(text_pieces), group, group * data),
        1,
        [(SMEM, jnp.stack(text_starts).astype(jnp.int32)), (SMEM, own_index)]
        + [(ANY, member) for member in text_pieces],
        [(whole(shape), shape, F32) for shape in unpacked]
        + [(whole(shape), shape, F32) for shape in (mods_shape, (1, columns))],
        [
            pltpu.VMEM((stack_rows, model_width), BF16),
            semaphores(len(text_pieces), 1),
            pltpu.VMEM((small_rows(group), model_width), F32),
        ],
    )
    return (
        output,
        grad_text,
        grad_time,
        unpacked[3],
        unpacked[4],
        unpacked[5][0],
        unpacked[6],
        unpacked[1],
        unpacked[2],
        unpacked[0],
        unpacked[7],
        unpacked[10],
        unpacked[11][0],
        weight_qkv,
        unpacked[8],
        weight_out,
        weight_up,
        unpacked[9][0],
        weight_down,
    )


def solution(mesh):
    in_specs = (
        P(("dp", "heads"), None),
        P(("dp", "heads"), None),
        P(("dp", "heads"), None),
        P("dp", None),
        P("dp"),
        P(("dp", "heads"), None),
        P(),
        P(),
        P(),
        P(),
        P(),
        P(),
        P(),
        P(),
        P(None, "heads"),
        P("heads"),
        P(None, None, "heads"),
        P(None, "heads"),
        P("heads", None),
        P(None, "heads"),
        P("heads"),
        P("heads", None),
        P(("dp", "heads"), None),
    )
    out_specs = (
        P(("dp", "heads"), None),
        P(("dp", "heads"), None),
        P("dp", None),
        P(),
        P(),
        P(),
        P(),
        P(),
        P(),
        P(),
        P(),
        P(None, "heads"),
        P("heads"),
        P(None, None, "heads"),
        P(None, "heads"),
        P("heads", None),
        P(None, "heads"),
        P("heads"),
        P("heads", None),
    )
    return jax.shard_map(
        on_device, mesh=mesh, in_specs=in_specs, out_specs=out_specs, check_vma=False
    )
```
